32 devices in a mesh: fleet: 2 (over x), leaf: 16 (over z, y, core).
Axes of the slice: x: 2, y: 2, z: 4, core: 2. Of those that a mesh axis runs over, the one named last changes fastest.
Arguments:
- points: float32 [16, 196608], P(None, ('fleet', 'leaf')), parts along dimension 1, may hold values from -6 to 6
- charges: float32 [16, 196608], P(None, ('fleet', 'leaf')), parts along dimension 1, may hold values from -6 to 6
- inv_scale: float32 [32], P('fleet'), parts along dimension 0, may hold values from 0.25 to 0.75
- order: int32 [196608], P(('fleet', 'leaf')), parts along dimension 0, may hold values from 0 to 98303, as said below
- near_list: int32 [192, 3], P(('fleet', 'leaf')), parts along dimension 0, may hold values from 0 to 95, as said below
- near_count: int32 [192], P(('fleet', 'leaf')), parts along dimension 0, may hold values from 2 to 3, as said below
- far_list: int32 [192, 6], P(('fleet', 'leaf')), parts along dimension 0, may hold values from 0 to 95, as said below
- skel_idx: int32 [192, 128], P(('fleet', 'leaf')), parts along dimension 0, may hold values from 0 to 1023, as said below
- interp: bfloat16 [128, 196608], P(None, ('fleet', 'leaf')), parts along dimension 1, may hold values from -0.1875 to 0.1875
- group_map: bfloat16 [24576, 128], P(('fleet', 'leaf')), parts along dimension 0, may hold values from -0.375 to 0.375
- parent_map: bfloat16 [512, 128], P('fleet'), parts along dimension 0, may hold values from -0.4375 to 0.4375
Outputs:
- potential: float32 [16, 196608], P(None, ('fleet', 'leaf')), parts along dimension 1
The draws below stay inside these ranges and needn't reach their ends.
There are 2 independent parts, one for each index of `fleet`. The reference program is written for one: setup_inputs(seed, part) draws one part's arguments, and reference() takes and returns one part's arrays. A program takes and returns all parts, laid end to end along the dimension named above; each array names one. Nothing has to cross between parts.
Inputs may be any that keep to these rules, and one draw needn't show every extreme that they name: order maps the 6144 slots of each group to the points of that same group, each once. `near_list`: each entry names a leaf of the leaf's own group or of the group just before or after it; the used slots of a list are distinct. `near_count`: the first leaf of every group uses all 3 slots. `far_list`: distinct leaves of the leaf's own group or of the group just before or after it. `skel_idx`: the slots of one leaf are distinct.
All inputs are finite; a program needn't handle non-finite values.
Results may differ from the reference program's by a relative error of at most 0.0044.
Values sent between devices are 32-bit elements; how exact they have to be, the bound alone decides.
No kernel may reach another device: no remote copies, remote signals or barrier semaphores. Data moves between devices by JAX's collectives and lax.ppermute only.
A program may use at most 64 MiB of HBM per device.

```python
import math
import jax
import jax.numpy as jnp
from jax import lax

F = 16
R = 16
LEAF_PTS = 1024
RANK = 128
NEAR = 3
FARN = 6
LEAF_DEV = 6
NLEAF = 96
NPTS = 98304


def window_pick(key, count):
    span = 3 * LEAF_DEV
    keys = jax.random.split(key, NLEAF)
    scores = jax.vmap(lambda k: jax.random.permutation(k, span))(keys).astype(jnp.int32)
    leaves = jnp.arange(NLEAF, dtype=jnp.int32)
    start = (leaves // LEAF_DEV - 1) * LEAF_DEV
    ids = start[:, None] + jnp.arange(span, dtype=jnp.int32)[None, :]
    valid = (ids >= 0) & (ids < NLEAF)
    scores = jnp.where(valid, scores, -1 - jnp.arange(span, dtype=jnp.int32)[None, :])
    _, picked = lax.top_k(scores, count)
    return jnp.take_along_axis(ids, picked.astype(jnp.int32), axis=1).astype(jnp.int32)


def draw_order(key, part):
    key = jax.random.fold_in(key, 14)
    groups = NLEAF // LEAF_DEV
    block = LEAF_DEV * LEAF_PTS
    keys = jax.random.split(key, groups)
    perms = jax.vmap(lambda k: jax.random.permutation(k, block))(keys).astype(jnp.int32)
    offsets = (jnp.arange(groups, dtype=jnp.int32) * block)[:, None]
    return (perms + offsets).reshape(NPTS).astype(jnp.int32)


def draw_near_list(key, part):
    key = jax.random.fold_in(key, 11)
    return window_pick(key, NEAR)


def draw_far_list(key, part):
    key = jax.random.fold_in(key, 12)
    return window_pick(key, FARN)


def draw_near_count(key, part):
    key = jax.random.fold_in(key, 13)
    counts = jax.random.randint(key, (NLEAF,), 2, NEAR + 1).astype(jnp.int32)
    first = jnp.arange(NLEAF, dtype=jnp.int32) % LEAF_DEV == 0
    return jnp.where(first, NEAR, counts).astype(jnp.int32)


def draw_skel_idx(key, part):
    key = jax.random.fold_in(key, 15)
    keys = jax.random.split(key, NLEAF)
    perms = jax.vmap(lambda k: jax.random.permutation(k, LEAF_PTS))(keys).astype(jnp.int32)
    return perms[:, :RANK].astype(jnp.int32)


def block_levels(own_key, extent, cuts, least, top_value):
    factor_of = 1.0
    for dim, blocks in cuts:
        steps = jax.random.uniform(jax.random.fold_in(jax.random.fold_in(own_key, 6), dim), (blocks,), jnp.float32, least / len(cuts), top_value / len(cuts))
        factor_of = factor_of * jnp.repeat(jnp.exp(steps), extent[dim] // blocks).reshape((-1,) + (1,) * (len(extent) - 1 - dim))
    return factor_of


def gaussian(key, extent, scale, reach, cuts=(), kind=jnp.bfloat16):
    drawn = jax.random.normal(key, extent, jnp.float32) * scale
    if len(cuts) > 0:
        drawn = block_levels(key, extent, cuts, -0.22, 0.18) * drawn
    return jnp.clip(drawn, min=-reach, max=reach).astype(kind)


def setup_inputs(seed: int = 0, part: int = 0) -> dict:
    key_of = jax.random.split(jax.random.key(seed), 12)
    part_splits = jax.random.split(jax.random.fold_in(key_of[11], part), 12)
    points = gaussian(part_splits[0], (F, NPTS), 1.0, 6.0, ((1, 16),), jnp.float32)
    charges = gaussian(part_splits[1], (R, NPTS), 1.0, 6.0, ((1, 16),), jnp.float32)
    inv_scale = jnp.clip(jnp.exp(jax.random.uniform(part_splits[2], (F,), jnp.float32, math.log(0.25), math.log(0.75))), 0.25, 0.75)
    order = draw_order(jax.random.fold_in(jax.random.fold_in(key_of[11], part), 71), part)
    near_list = draw_near_list(jax.random.fold_in(jax.random.fold_in(key_of[11], part), 71), part)
    near_count = draw_near_count(jax.random.fold_in(jax.random.fold_in(key_of[11], part), 71), part)
    far_list = draw_far_list(jax.random.fold_in(jax.random.fold_in(key_of[11], part), 71), part)
    skel_idx = draw_skel_idx(jax.random.fold_in(jax.random.fold_in(key_of[11], part), 71), part)
    interp = gaussian(part_splits[8], (RANK, NPTS), LEAF_PTS ** -0.5, 0.1875, ((1, 16),))
    group_map = gaussian(part_splits[9], (NLEAF * RANK, RANK), (2 * RANK) ** -0.5, 0.375, ((0, 16),))
    parent_map = gaussian(part_splits[10], (2 * RANK, RANK), (7 * RANK // 5) ** -0.5, 0.4375)
    return dict(points=points, charges=charges, inv_scale=inv_scale, order=order, near_list=near_list, near_count=near_count, far_list=far_list, skel_idx=skel_idx, interp=interp, group_map=group_map, parent_map=parent_map)


def gauss(left, right):
    hi = lax.Precision.HIGHEST
    norm_left = jnp.sum(left * left, 0)
    norm_right = jnp.sum(right * right, 0)
    cross = lax.dot_general(left, right, (((0,), (0,)), ((), ())), precision=hi, preferred_element_type=jnp.float32)
    return jnp.exp(-0.5 * (norm_left[:, None] + norm_right[None, :] - 2.0 * cross))


def rounded(value):
    return lax.optimization_barrier(value.astype(jnp.bfloat16)).astype(jnp.float32)


def reference(points, charges, inv_scale, order, near_list, near_count, far_list, skel_idx, interp, group_map, parent_map):
    hi = lax.Precision.HIGHEST
    scaled = points * inv_scale[:, None]
    zleaf = scaled[:, order].reshape(F, NLEAF, LEAF_PTS)
    bleaf = charges[:, order].astype(jnp.bfloat16).reshape(R, NLEAF, LEAF_PTS)

    def near_leaf(leaf):
        total = jnp.zeros((R, LEAF_PTS), jnp.float32)
        for slot in range(NEAR):
            other = near_list[leaf, slot]
            tile = gauss(zleaf[:, other], zleaf[:, leaf]).astype(jnp.bfloat16)
            term = jnp.dot(bleaf[:, other], tile, preferred_element_type=jnp.float32)
            total = total + jnp.where(slot < near_count[leaf], term, 0.0)
        return total

    near = lax.map(near_leaf, jnp.arange(NLEAF))
    skel = jnp.take_along_axis(zleaf, skel_idx[None], axis=2)
    bases = interp.reshape(RANK, NLEAF, LEAF_PTS).astype(jnp.float32)
    charge = jnp.einsum('rlp,klp->lrk', bleaf.astype(jnp.float32), bases, precision=hi)
    cbound = rounded(charge)

    def far_leaf(leaf):
        total = jnp.zeros((R, RANK), jnp.float32)
        for slot in range(FARN):
            other = far_list[leaf, slot]
            tile = rounded(gauss(skel[:, other], skel[:, leaf]))
            total = total + jnp.dot(cbound[other], tile, precision=hi, preferred_element_type=jnp.float32)
        return total

    field = lax.map(far_leaf, jnp.arange(NLEAF))
    groups = NLEAF // LEAF_DEV
    node_z = skel.reshape(F, groups, LEAF_DEV * RANK)[:, :, ::LEAF_DEV]
    group_in = cbound.reshape(groups, LEAF_DEV, R, RANK).transpose(0, 2, 1, 3).reshape(groups, R, LEAF_DEV * RANK)
    gmatrix = group_map.astype(jnp.float32).reshape(groups, LEAF_DEV * RANK, RANK)
    node_q = jnp.einsum('grk,gkj->grj', group_in, gmatrix, precision=hi)
    emap = parent_map.astype(jnp.float32)
    levels = groups.bit_length() - 1
    inters = []
    for level in range(levels):
        count = node_q.shape[0]
        sibling = jnp.arange(count) ^ 1
        kernels = rounded(jax.vmap(gauss, in_axes=(1, 1))(node_z[:, sibling], node_z))
        inters.append(jnp.einsum('nrk,nki->nri', rounded(node_q[sibling]), kernels, precision=hi))
        node_z = node_z.reshape(F, count // 2, 2, RANK)[:, :, :, ::2].reshape(F, count // 2, RANK)
        joined = node_q.reshape(count // 2, 2, R, RANK).transpose(0, 2, 1, 3).reshape(count // 2, R, 2 * RANK)
        node_q = jnp.einsum('nrk,kj->nrj', rounded(joined), emap, precision=hi)
    downward = jnp.zeros((1, R, RANK), jnp.float32)
    for level in reversed(range(levels)):
        spread = jnp.einsum('nrj,kj->nrk', rounded(downward), emap, precision=hi)
        count = 2 * spread.shape[0]
        spread = spread.reshape(count // 2, R, 2, RANK).transpose(0, 2, 1, 3).reshape(count, R, RANK)
        downward = inters[level] + spread
    group_out = jnp.einsum('grj,gkj->grk', rounded(downward), gmatrix, precision=hi)
    leaf_out = group_out.reshape(groups, R, LEAF_DEV, RANK).transpose(0, 2, 1, 3).reshape(NLEAF, R, RANK)
    ufield = (field + leaf_out).astype(jnp.bfloat16)
    far = jnp.einsum('lrk,klp->lrp', ufield.astype(jnp.float32), bases, precision=hi)
    yleaf = (near + far).transpose(1, 0, 2).reshape(R, NPTS)
    return jnp.zeros((R, NPTS), jnp.float32).at[:, order].set(yleaf)
```

```python
import functools
import math

import jax
import jax.numpy as jnp
from jax import lax
from jax.experimental import pallas as pl
from jax.experimental.pallas import tpu as pltpu
from jax.sharding import PartitionSpec as P

BF = jnp.bfloat16
F32 = jnp.float32
LANES = 128
BLOCK = 256
CHUNK = 1024
ROWS = 512
VMEM = pl.BlockSpec(memory_space=pltpu.VMEM)
SMEM = pl.BlockSpec(memory_space=pltpu.SMEM)


def params():
    return pltpu.CompilerParams(vmem_limit_bytes=48 * 2**20)


def halves(z):
    hi = z.astype(BF)
    return hi, (z - hi.astype(F32)).astype(BF)


def stacked_rows(z):
    hi, mid = halves(z)
    norm = -0.5 * jnp.sum(z * z, 0, keepdims=True)
    n1 = norm.astype(BF).astype(F32)
    n2 = (norm - n1).astype(BF).astype(F32)
    n3 = norm - n1 - n2
    shape = (16, z.shape[1])
    row = lax.broadcasted_iota(jnp.int32, shape, 0)

    def extra(first):
        out = jnp.where((row >= 3 - first) & (row < 6 - first), 1.0, 0.0)
        for i, piece in enumerate((n1, n2, n3)):
            out = jnp.where(row == first + i, jnp.broadcast_to(piece, shape), out)
        return out.astype(BF)

    source = jnp.concatenate([hi, mid, hi, mid, extra(3)], 0)
    target = jnp.concatenate([hi, hi, mid, mid, extra(0)], 0)
    return source, target


def tile_of(source, target):
    e = lax.dot_general(source, target, (((0,), (0,)), ((), ())), preferred_element_type=F32)
    return jnp.exp2(e).astype(BF)


def dot_t(a, b):
    return lax.dot_general(a, b, (((1,), (1,)), ((), ())), preferred_element_type=F32)


def dot(a, b):
    return jnp.dot(a, b, preferred_element_type=F32)


def one_hot(low, size):
    rows = lax.broadcasted_iota(jnp.int32, (size, low.shape[1]), 0)
    return (rows == low).astype(F32).astype(BF)


def pick_lanes(blocks, index):
    rows = blocks[0].shape[0]
    parts = []
    for top in range(0, rows, 8):
        idx = jnp.broadcast_to(index, (8, LANES))
        high, low = idx >> 7, idx & (LANES - 1)
        out = jnp.zeros((8, LANES), F32)
        for k, block in enumerate(blocks):
            got = jnp.take_along_axis(block[top : top + 8], low, axis=1, mode="promise_in_bounds")
            out = jnp.where(high == k, got, out)
        parts.append(out)
    return jnp.concatenate(parts, 0)


def sort_kernel(scale_ref, points_ref, charges_ref, order_ref, out_ref, zs_ref, bs_ref):
    feats, total = points_ref.shape
    rhs = charges_ref.shape[0]
    base = lax.axis_index("leaf") * total
    blocks = total // BLOCK
    row = lax.broadcasted_iota(jnp.int32, (feats, LANES), 0)
    scale = jnp.zeros((feats, LANES), F32)
    for r in range(feats):
        scale = jnp.where(row == r, scale_ref[r], scale)
    scale = scale[:, :1] * math.sqrt(math.log2(math.e))
    for k in range(blocks):
        span = slice(k * BLOCK, (k + 1) * BLOCK)
        hi, mid = halves(points_ref[:, span] * scale)
        zs_ref[k * feats : (k + 1) * feats, :BLOCK] = hi
        zs_ref[k * feats : (k + 1) * feats, BLOCK:] = mid
        bs_ref[k * rhs : (k + 1) * rhs, :] = charges_ref[:, span].astype(BF)
    shift = BLOCK.bit_length() - 1

    def step(j, carry):
        start = pl.multiple_of(j * CHUNK, CHUNK)
        index = order_ref[:, pl.ds(start, CHUNK)] - base
        hot = one_hot(index & (BLOCK - 1), BLOCK)
        yz = dot(zs_ref[...], jnp.concatenate([hot, hot], 0))
        yb = dot(bs_ref[...], hot)
        high = jnp.broadcast_to(index >> shift, (feats, CHUNK))
        az = jnp.zeros((feats, CHUNK), F32)
        ab = jnp.zeros((rhs, CHUNK), F32)
        for k in range(blocks):
            mask = high == k
            az = jnp.where(mask, yz[k * feats : (k + 1) * feats], az)
            ab = jnp.where(mask, yb[k * rhs : (k + 1) * rhs], ab)
        out_ref[:feats, pl.ds(start, CHUNK)] = az
        out_ref[feats:, pl.ds(start, CHUNK)] = ab
        return carry

    lax.fori_loop(0, total // CHUNK, step, 0)


def sort_points(inv_scale, points, charges, order):
    feats, total = points.shape
    rhs = charges.shape[0]
    blocks = total // BLOCK
    return pl.pallas_call(
        sort_kernel,
        out_shape=jax.ShapeDtypeStruct((feats + rhs, total), F32),
        in_specs=[SMEM, VMEM, VMEM, VMEM],
        out_specs=VMEM,
        scratch_shapes=[
            pltpu.VMEM((blocks * feats, 2 * BLOCK), BF),
            pltpu.VMEM((blocks * rhs, BLOCK), BF),
        ],
        compiler_params=params(),
        name="sort_points",
    )(inv_scale, points, charges, order)


def skeleton_kernel(pack_ref, skel_ref, interp_ref, map_ref, skel_out, node_out, *, feats):
    leaves, rank = skel_ref.shape
    width = pack_ref.shape[1] // leaves
    rhs = pack_ref.shape[0] - feats
    group_q = jnp.zeros((rhs, rank), F32)
    for leaf in range(leaves):
        blocks = [
            pack_ref[:feats, leaf * width + k : leaf * width + k + LANES]
            for k in range(0, width, LANES)
        ]
        skel_out[:feats, leaf * rank : (leaf + 1) * rank] = pick_lanes(
            blocks, skel_ref[leaf : leaf + 1, :]
        )
        span = slice(leaf * width, (leaf + 1) * width)
        charge = dot_t(pack_ref[feats:, span].astype(BF), interp_ref[:, span]).astype(BF)
        skel_out[feats:, leaf * rank : (leaf + 1) * rank] = charge.astype(F32)
        group_q += dot(charge, map_ref[leaf * rank : (leaf + 1) * rank, :])
    blocks = [skel_out[:feats, k : k + LANES] for k in range(0, leaves * rank, LANES)]
    node_out[:feats, :] = pick_lanes(
        blocks, lax.broadcasted_iota(jnp.int32, (1, rank), 1) * leaves
    )
    node_out[feats:, :] = group_q


def skeletons(pack, skel_idx, interp, group_map, feats):
    leaves, rank = skel_idx.shape
    return pl.pallas_call(
        functools.partial(skeleton_kernel, feats=feats),
        out_shape=(
            jax.ShapeDtypeStruct((pack.shape[0], leaves * rank), F32),
            jax.ShapeDtypeStruct((pack.shape[0], rank), F32),
        ),
        in_specs=[VMEM] * 4,
        out_specs=(VMEM, VMEM),
        compiler_params=params(),
        name="skeletons",
    )(pack, skel_idx, interp, group_map)


def region_of(leaf_id, leaves):
    device = lax.axis_index("leaf")
    rel = leaf_id - (device - 1) * leaves
    side = (rel >= leaves).astype(jnp.int32) + (rel >= 2 * leaves).astype(jnp.int32)
    odd = device & 1
    region = jnp.where(side == 1, 0, jnp.where(side == 2 * (1 - odd), 1, 2))
    return region, rel - side * leaves


def near_kernel(list_ref, count_ref, own_ref, src_ref, *refs, feats, region, first):
    if first:
        out_ref, source_ref, target_ref, charge_ref = refs
    else:
        acc_ref, out_ref, source_ref, target_ref, charge_ref = refs
    leaves, slots = list_ref.shape
    width = own_ref.shape[1] // leaves
    for leaf in range(leaves):
        span = slice(leaf * width, (leaf + 1) * width)
        source, target = stacked_rows(own_ref[:feats, span])
        target_ref[leaf] = target
        if region > 0:
            source, _ = stacked_rows(src_ref[:feats, span])
        source_ref[leaf] = source
        charge_ref[leaf] = src_ref[feats:, span].astype(BF)
        out_ref[:, span] = jnp.zeros_like(out_ref[:, span]) if first else acc_ref[:, span]

    def per_leaf(leaf, carry):
        start = pl.multiple_of(leaf * width, width)

        def per_slot(slot, carry):
            found, place = region_of(list_ref[leaf, slot], leaves)

            @pl.when(found == region)
            def _():
                acc = out_ref[:, pl.ds(start, width)]
                for row in range(0, width, ROWS):
                    tile = tile_of(source_ref[place, :, row : row + ROWS], target_ref[leaf])
                    acc = acc + dot(charge_ref[place, :, row : row + ROWS], tile)
                out_ref[:, pl.ds(start, width)] = acc

            return carry

        return lax.fori_loop(0, count_ref[leaf], per_slot, carry)

    lax.fori_loop(0, leaves, per_leaf, 0)


def near_part(near_list, near_count, own, source, acc, feats, region):
    leaves = near_list.shape[0]
    rhs = own.shape[0] - feats
    total = own.shape[1]
    width = total // leaves
    stack = 4 * feats + 16
    first = acc is None
    extra = () if first else (acc,)
    return pl.pallas_call(
        functools.partial(near_kernel, feats=feats, region=region, first=first),
        out_shape=jax.ShapeDtypeStruct((rhs, total), F32),
        in_specs=[SMEM, SMEM] + [VMEM] * (2 + len(extra)),
        out_specs=VMEM,
        scratch_shapes=[
            pltpu.VMEM((leaves, stack, width), BF),
            pltpu.VMEM((leaves, stack, width), BF),
            pltpu.VMEM((leaves, rhs, width), BF),
        ],
        compiler_params=params(),
        name=f"near_{region}",
    )(near_list, near_count, own, source, *extra)


def climb(nodes, base, levels, parent_map, feats):
    device = lax.axis_index("leaf")
    rank = nodes[0].shape[1]
    lane = lax.broadcasted_iota(jnp.int32, (1, rank), 1)
    inters = []
    for level in range(levels):
        own, other = nodes[0], nodes[1]
        source, _ = stacked_rows(other[:feats])
        _, target = stacked_rows(own[:feats])
        inters.append(dot(other[feats:].astype(BF), tile_of(source, target)))
        odd = (device >> (base + level)) & 1
        parents = []
        for k in range(0, len(nodes), 2):
            left = jnp.where(odd == 1, nodes[k + 1], nodes[k])
            right = jnp.where(odd == 1, nodes[k], nodes[k + 1])
            z = pick_lanes([left[:feats], right[:feats]], lane * 2)
            q = dot(left[feats:].astype(BF), parent_map[:rank, :])
            q += dot(right[feats:].astype(BF), parent_map[rank:, :])
            parents.append(jnp.concatenate([z, q], 0))
        nodes = parents
    return inters, nodes[0]


def climb_kernel(*refs, base, levels, feats):
    count = 2**levels
    nodes = [ref[...] for ref in refs[:count]]
    inters, node = climb(nodes, base, levels, refs[count][...], feats)
    for ref, value in zip(refs[count + 1 :], inters + [node]):
        ref[...] = value


def climb_stage(nodes, base, levels, parent_map, feats):
    rows, rank = nodes[0].shape
    small = jax.ShapeDtypeStruct((rows - feats, rank), F32)
    outs = pl.pallas_call(
        functools.partial(climb_kernel, base=base, levels=levels, feats=feats),
        out_shape=(small,) * levels + (jax.ShapeDtypeStruct((rows, rank), F32),),
        in_specs=[VMEM] * (len(nodes) + 1),
        out_specs=(VMEM,) * (levels + 1),
        compiler_params=params(),
        name=f"climb_{base}",
    )(*nodes, parent_map)
    return list(outs[:-1]), outs[-1]


def finish_kernel(*refs, feats, base, levels, done):
    far_ref, near_ref, own_ref, sib_ref, beyond_ref, interp_ref, map_ref, parent_ref, order_ref = refs[:9]
    refs = refs[9:]
    count = 2**levels
    nodes = [ref[...] for ref in refs[:count]]
    inters = [ref[...] for ref in refs[count : count + done]]
    out_ref, skel_ref, charge_ref, acc_ref = refs[count + done :]
    leaves, slots = far_ref.shape
    rank = own_ref.shape[1] // leaves
    rhs, total = near_ref.shape
    width = total // leaves
    device = lax.axis_index("leaf")
    parent_map = parent_ref[...]

    fresh, _ = climb(nodes, base, levels, parent_map, feats)
    inters = inters + fresh
    down = inters[-1]
    for level in range(len(inters) - 2, -1, -1):
        spread = dot_t(down.astype(BF), parent_map)
        odd = (device >> level) & 1
        down = inters[level] + jnp.where(odd == 1, spread[:, rank:], spread[:, :rank])
    leaf_out = dot_t(down.astype(BF), map_ref[...])

    targets = []
    for region, ref in enumerate((own_ref, sib_ref, beyond_ref)):
        source, target = stacked_rows(ref[:feats, :])
        charge = ref[feats:, :].astype(BF)
        for leaf in range(leaves):
            span = slice(leaf * rank, (leaf + 1) * rank)
            skel_ref[region * leaves + leaf] = source[:, span]
            charge_ref[region * leaves + leaf] = charge[:, span]
            if region == 0:
                targets.append(target[:, span])
    pieces = []
    for leaf in range(leaves):
        field = leaf_out[:, leaf * rank : (leaf + 1) * rank]
        where = []
        for slot in range(slots):
            region, place = region_of(far_ref[leaf, slot], leaves)
            where.append(region * leaves + place)
        sources = jnp.concatenate([skel_ref[w] for w in where], 1)
        charges = jnp.concatenate([charge_ref[w] for w in where], 1)
        field += dot(charges, tile_of(sources, targets[leaf]))
        span = slice(leaf * width, (leaf + 1) * width)
        pieces.append(near_ref[:, span] + dot(field.astype(BF), interp_ref[:, span]))

    blocks = total // BLOCK
    shift = BLOCK.bit_length() - 1
    for leaf in range(leaves):
        index = order_ref[:, leaf * width : (leaf + 1) * width] - device * total
        hot = one_hot(index & (BLOCK - 1), BLOCK)
        high = jnp.broadcast_to(index >> shift, (rhs, width))
        hi, mid = halves(pieces[leaf])
        hi, mid = hi.astype(F32), mid.astype(F32)
        rows = []
        for k in range(blocks):
            mask = high == k
            rows.append(jnp.where(mask, hi, 0.0).astype(BF))
            rows.append(jnp.where(mask, mid, 0.0).astype(BF))
        part = dot_t(jnp.concatenate(rows, 0), hot)
        acc_ref[...] = part if leaf == 0 else acc_ref[...] + part
    for k in range(blocks):
        top = 2 * rhs * k
        out_ref[:, k * BLOCK : (k + 1) * BLOCK] = (
            acc_ref[top : top + rhs, :] + acc_ref[top + rhs : top + 2 * rhs, :]
        )


def finish(far_list, near, skels, interp, group_map, parent_map, order, nodes, inters, base, levels, feats):
    rhs, total = near.shape
    leaves = far_list.shape[0]
    rank = interp.shape[0]
    return pl.pallas_call(
        functools.partial(
            finish_kernel, feats=feats, base=base, levels=levels, done=len(inters)
        ),
        out_shape=jax.ShapeDtypeStruct((rhs, total), F32),
        in_specs=[SMEM] + [VMEM] * (8 + len(nodes) + len(inters)),
        out_specs=VMEM,
        scratch_shapes=[
            pltpu.VMEM((3 * leaves, 4 * feats + 16, rank), BF),
            pltpu.VMEM((3 * leaves, rhs, rank), BF),
            pltpu.VMEM((total // BLOCK * 2 * rhs, BLOCK), F32),
        ],
        compiler_params=params(),
        name="finish",
    )(far_list, near, *skels, interp, group_map, parent_map, order, *nodes, *inters)


def body(
    points,
    charges,
    inv_scale,
    order,
    near_list,
    near_count,
    far_list,
    skel_idx,
    interp,
    group_map,
    parent_map,
):
    feats = points.shape[0]
    devices = lax.axis_size("leaf")
    order = order.reshape(1, -1)
    chip = [(i, i ^ 1) for i in range(devices)]
    beyond = []
    for i in range(1, devices - 1, 2):
        beyond += [(i, i + 1), (i + 1, i)]

    def send(value, pairs):
        return lax.ppermute(value, "leaf", pairs)

    def relatives(node, base, levels):
        out = [node]
        for k in range(1, 2**levels):
            out.append(send(node, [(i, i ^ (k << base)) for i in range(devices)]))
        return out

    pack = sort_points(inv_scale, points, charges, order)
    pack_beyond = send(pack, beyond)
    pack_chip = send(pack, chip)
    skel, node = skeletons(pack, skel_idx, interp, group_map, feats)
    skel_beyond = send(skel, beyond)
    skel_chip = send(skel, chip)

    levels = devices.bit_length() - 1
    stages = [(base, min(2, levels - base)) for base in range(0, levels, 2)]
    inters = []
    for base, count in stages[:-1]:
        fresh, node = climb_stage(relatives(node, base, count), base, count, parent_map, feats)
        inters += fresh
    base, count = stages[-1]
    nodes = relatives(node, base, count)

    near = near_part(near_list, near_count, pack, pack, None, feats, 0)
    near = near_part(near_list, near_count, pack, pack_chip, near, feats, 1)
    near = near_part(near_list, near_count, pack, pack_beyond, near, feats, 2)
    return finish(
        far_list,
        near,
        (skel, skel_chip, skel_beyond),
        interp,
        group_map,
        parent_map,
        order,
        nodes,
        inters,
        base,
        count,
        feats,
    )


def solution(mesh):
    placed = (
        P(None, ("fleet", "leaf")),
        P(None, ("fleet", "leaf")),
        P("fleet"),
        P(("fleet", "leaf")),
        P(("fleet", "leaf"), None),
        P(("fleet", "leaf")),
        P(("fleet", "leaf"), None),
        P(("fleet", "leaf"), None),
        P(None, ("fleet", "leaf")),
        P(("fleet", "leaf"), None),
        P("fleet", None),
    )
    return jax.shard_map(
        body, mesh=mesh, in_specs=placed, out_specs=P(None, ("fleet", "leaf")), check_vma=False
    )
```

```python
import functools
import math

import jax
import jax.numpy as jnp
from jax import lax
from jax.experimental import pallas as pl
from jax.experimental.pallas import tpu as pltpu
from jax.sharding import PartitionSpec as P

BF = jnp.bfloat16
F32 = jnp.float32
LANES = 128
BLOCK = 256
ROWS = 512
VMEM = pl.BlockSpec(memory_space=pltpu.VMEM)
SMEM = pl.BlockSpec(memory_space=pltpu.SMEM)


def params():
    return pltpu.CompilerParams(vmem_limit_bytes=48 * 2**20)


def halves(z):
    hi = z.astype(BF)
    return hi, (z - hi.astype(F32)).astype(BF)


def stacked_rows(z):
    hi, mid = halves(z)
    norm = -0.5 * jnp.sum(z * z, 0, keepdims=True)
    n1 = norm.astype(BF).astype(F32)
    n2 = (norm - n1).astype(BF).astype(F32)
    n3 = norm - n1 - n2
    shape = (16, z.shape[1])
    row = lax.broadcasted_iota(jnp.int32, shape, 0)

    def extra(first):
        out = jnp.where((row >= 3 - first) & (row < 6 - first), 1.0, 0.0)
        for i, piece in enumerate((n1, n2, n3)):
            out = jnp.where(row == first + i, jnp.broadcast_to(piece, shape), out)
        return out.astype(BF)

    source = jnp.concatenate([hi, mid, hi, mid, extra(3)], 0)
    target = jnp.concatenate([hi, hi, mid, mid, extra(0)], 0)
    return source, target


def tile_of(source, target):
    e = lax.dot_general(source, target, (((0,), (0,)), ((), ())), preferred_element_type=F32)
    return jnp.exp2(e).astype(BF)


def dot_t(a, b):
    return lax.dot_general(a, b, (((1,), (1,)), ((), ())), preferred_element_type=F32)


def dot(a, b):
    return jnp.dot(a, b, preferred_element_type=F32)


def one_hot(low, size):
    rows = lax.broadcasted_iota(jnp.int32, (size, low.shape[1]), 0)
    return (rows == low).astype(F32).astype(BF)


def pick_lanes(blocks, index):
    rows = blocks[0].shape[0]
    parts = []
    for top in range(0, rows, 8):
        idx = jnp.broadcast_to(index, (8, LANES))
        high, low = idx >> 7, idx & (LANES - 1)
        out = jnp.zeros((8, LANES), F32)
        for k, block in enumerate(blocks):
            got = jnp.take_along_axis(block[top : top + 8], low, axis=1, mode="promise_in_bounds")
            out = jnp.where(high == k, got, out)
        parts.append(out)
    return jnp.concatenate(parts, 0)


def prepare_kernel(
    scale_hbm, points_hbm, charges_hbm, order_hbm, skel_hbm, map_hbm, interp_hbm,
    pack_ref, near_ref, rest_ref, node_ref, source_ref, target_ref,
    scale_ref, points_ref, charges_ref, order_ref, skel_ref, map_ref, interp_ref,
    zs_ref, bs_ref, sems,
):
    pairs = (
        (scale_hbm, scale_ref),
        (order_hbm, order_ref),
        (points_hbm, points_ref),
        (charges_hbm, charges_ref),
        (skel_hbm, skel_ref),
        (map_hbm, map_ref),
        (interp_hbm, interp_ref),
    )
    copies = [pltpu.make_async_copy(src, dst, sems.at[i]) for i, (src, dst) in enumerate(pairs)]
    for copy in copies:
        copy.start()
    feats, total = points_ref.shape
    rhs = charges_ref.shape[0]
    leaves, rank = skel_ref.shape
    width = total // leaves
    early = near_ref.shape[1] // width
    base = lax.axis_index("leaf") * total
    blocks = total // BLOCK
    shift = BLOCK.bit_length() - 1
    for copy in copies[:4]:
        copy.wait()
    row = lax.broadcasted_iota(jnp.int32, (feats, LANES), 0)
    scale = jnp.zeros((feats, LANES), F32)
    for r in range(feats):
        scale = jnp.where(row == r, scale_ref[r], scale)
    scale = scale[:, :1] * math.sqrt(math.log2(math.e))
    for k in range(blocks):
        span = slice(k * BLOCK, (k + 1) * BLOCK)
        hi, mid = halves(points_ref[:, span] * scale)
        zs_ref[k * feats : (k + 1) * feats, :BLOCK] = hi
        zs_ref[k * feats : (k + 1) * feats, BLOCK:] = mid
        bs_ref[k * rhs : (k + 1) * rhs, :] = charges_ref[:, span].astype(BF)

    def step(j, carry):
        start = pl.multiple_of(j * width, width)
        index = order_ref[:, pl.ds(start, width)] - base
        hot = one_hot(index & (BLOCK - 1), BLOCK)
        yz = dot(zs_ref[...], jnp.concatenate([hot, hot], 0))
        yb = dot(bs_ref[...], hot)
        high = jnp.broadcast_to(index >> shift, (feats, width))
        az = jnp.zeros((feats, width), F32)
        ab = jnp.zeros((rhs, width), F32)
        for k in range(blocks):
            mask = high == k
            az = jnp.where(mask, yz[k * feats : (k + 1) * feats], az)
            ab = jnp.where(mask, yb[k * rhs : (k + 1) * rhs], ab)
        pack_ref[:feats, pl.ds(start, width)] = az
        pack_ref[feats:, pl.ds(start, width)] = ab
        source, target = stacked_rows(az)
        source_ref[:, pl.ds(start, width)] = source
        target_ref[:, pl.ds(start, width)] = target
        return carry

    lax.fori_loop(0, leaves, step, 0)
    for copy in copies[4:]:
        copy.wait()
    group_q = jnp.zeros((rhs, rank), F32)
    for leaf in range(leaves):
        span = slice(leaf * width, (leaf + 1) * width)
        out = slice(total + leaf * rank, total + (leaf + 1) * rank)
        columns = [
            pack_ref[:feats, leaf * width + k : leaf * width + k + LANES]
            for k in range(0, width, LANES)
        ]
        pack_ref[:feats, out] = pick_lanes(columns, skel_ref[leaf : leaf + 1, :])
        charge = dot_t(pack_ref[feats:, span].astype(BF), interp_ref[:, span]).astype(BF)
        pack_ref[feats:, out] = charge.astype(F32)
        group_q += dot(charge, map_ref[leaf * rank : (leaf + 1) * rank, :])
    columns = [pack_ref[:feats, total + k : total + k + LANES] for k in range(0, leaves * rank, LANES)]
    node_ref[:feats, :] = pick_lanes(
        columns, lax.broadcasted_iota(jnp.int32, (1, rank), 1) * leaves
    )
    node_ref[feats:, :] = group_q
    near_ref[...] = pack_ref[:, : early * width]
    rest_ref[...] = pack_ref[:, early * width :]


def prepare(inv_scale, points, charges, order, skel_idx, interp, group_map, early):
    feats, total = points.shape
    rhs = charges.shape[0]
    leaves, rank = skel_idx.shape
    blocks = total // BLOCK
    rows = feats + rhs
    stack = 4 * feats + 16
    cut = total // leaves * early
    both = total + leaves * rank
    hbm = pl.BlockSpec(memory_space=pltpu.HBM)
    return pl.pallas_call(
        prepare_kernel,
        out_shape=(
            jax.ShapeDtypeStruct((rows, both), F32),
            jax.ShapeDtypeStruct((rows, cut), F32),
            jax.ShapeDtypeStruct((rows, both - cut), F32),
            jax.ShapeDtypeStruct((rows, rank), F32),
            jax.ShapeDtypeStruct((stack, total), BF),
            jax.ShapeDtypeStruct((stack, total), BF),
        ),
        in_specs=[hbm] * 7,
        out_specs=(VMEM,) * 6,
        scratch_shapes=[
            pltpu.SMEM(inv_scale.shape, F32),
            pltpu.VMEM(points.shape, F32),
            pltpu.VMEM(charges.shape, F32),
            pltpu.VMEM(order.shape, jnp.int32),
            pltpu.VMEM(skel_idx.shape, jnp.int32),
            pltpu.VMEM(group_map.shape, BF),
            pltpu.VMEM(interp.shape, BF),
            pltpu.VMEM((blocks * feats, 2 * BLOCK), BF),
            pltpu.VMEM((blocks * rhs, BLOCK), BF),
            pltpu.SemaphoreType.DMA((7,)),
        ],
        compiler_params=params(),
        name="prepare",
    )(inv_scale, points, charges, order, skel_idx, group_map, interp)


def region_of(leaf_id, leaves):
    device = lax.axis_index("leaf")
    rel = leaf_id - (device - 1) * leaves
    side = (rel >= leaves).astype(jnp.int32) + (rel >= 2 * leaves).astype(jnp.int32)
    odd = device & 1
    region = jnp.where(side == 1, 0, jnp.where(side == 2 * (1 - odd), 1, 2))
    return region, rel - side * leaves


def near_kernel(list_ref, count_ref, target_ref, src_ref, *refs, feats, region, places):
    if region == 0:
        stack_ref, out_ref = refs
        out_ref[...] = jnp.zeros_like(out_ref)
    else:
        acc_ref, out_ref, stack_ref = refs
        out_ref[...] = acc_ref[...]
    slots, leaves = list_ref.shape
    width = target_ref.shape[1] // leaves
    low, high = places

    def per_leaf(leaf, carry):
        start = pl.multiple_of(leaf * width, width)

        def per_slot(slot, carry):
            found, place = region_of(list_ref[slot, leaf], leaves)

            @pl.when((found == region) & (place >= low) & (place < high))
            def _():
                at = pl.multiple_of((place - low) * width, width)
                if region == 0:
                    source = stack_ref[:, pl.ds(at, width)]
                else:
                    source, _ = stacked_rows(src_ref[:feats, pl.ds(at, width)])
                    stack_ref[...] = source
                    source = stack_ref[...]
                charge = src_ref[feats:, pl.ds(at, width)].astype(BF)
                target = target_ref[:, pl.ds(start, width)]
                acc = out_ref[:, pl.ds(start, width)]
                for row in range(0, width, ROWS):
                    tile = tile_of(source[:, row : row + ROWS], target)
                    acc = acc + dot(charge[:, row : row + ROWS], tile)
                out_ref[:, pl.ds(start, width)] = acc

            return carry

        return lax.fori_loop(0, count_ref[leaf], per_slot, carry)

    lax.fori_loop(0, leaves, per_leaf, 0)


def near_part(near_list, near_count, targets, source, extra, feats, region, places):
    slots, leaves = near_list.shape
    rhs = source.shape[0] - feats
    total = targets.shape[1]
    width = total // leaves
    stack = targets.shape[0]
    tiles = 2 * (places[1] - places[0])
    return pl.pallas_call(
        functools.partial(near_kernel, feats=feats, region=region, places=places),
        out_shape=jax.ShapeDtypeStruct((rhs, total), F32),
        in_specs=[SMEM, SMEM] + [VMEM] * 3,
        out_specs=VMEM,
        scratch_shapes=[] if region == 0 else [pltpu.VMEM((stack, width), BF)],
        compiler_params=params(),
        cost_estimate=pl.CostEstimate(
            flops=tiles * width * width * 1024,
            bytes_accessed=tiles * 48 * width * 4,
            transcendentals=tiles * width * width,
        ),
        name=f"near_{region}_{places[0]}",
    )(near_list, near_count, targets, source, extra)


def tree_kernel(nodes_ref, parent_ref, map_ref, out_ref, *, feats):
    count, _, rank = nodes_ref.shape
    levels = count.bit_length() - 1
    device = lax.axis_index("leaf")
    lane = lax.broadcasted_iota(jnp.int32, (1, rank), 1)
    zs = [nodes_ref[device ^ k, :feats, :] for k in range(count)]
    qs = [nodes_ref[device ^ k, feats:, :] for k in range(count)]
    inters = []
    for level in range(levels):
        source, _ = stacked_rows(zs[1])
        _, target = stacked_rows(zs[0])
        inters.append(dot(qs[1].astype(BF), tile_of(source, target)))
        if level == levels - 1:
            break
        odd = (device >> level) & 1
        half = len(zs) // 2
        parents = []
        for k in range(half):
            left = jnp.where(odd == 1, zs[2 * k + 1], zs[2 * k])
            right = jnp.where(odd == 1, zs[2 * k], zs[2 * k + 1])
            parents.append(pick_lanes([left, right], lane * 2))
        zs = parents
        even_q = jnp.concatenate(qs[0::2], 0)
        odd_q = jnp.concatenate(qs[1::2], 0)
        left = jnp.where(odd == 1, odd_q, even_q).astype(BF)
        right = jnp.where(odd == 1, even_q, odd_q).astype(BF)
        q = dot(left, parent_ref[:rank, :]) + dot(right, parent_ref[rank:, :])
        rhs = q.shape[0] // half
        qs = [q[k * rhs : (k + 1) * rhs] for k in range(half)]
    down = inters[-1]
    for level in range(levels - 2, -1, -1):
        spread = dot_t(down.astype(BF), parent_ref[...])
        odd = (device >> level) & 1
        down = inters[level] + jnp.where(odd == 1, spread[:, rank:], spread[:, :rank])
    out_ref[...] = dot_t(down.astype(BF), map_ref[...])


def tree(nodes, parent_map, group_map, feats):
    rhs = nodes.shape[1] - feats
    return pl.pallas_call(
        functools.partial(tree_kernel, feats=feats),
        out_shape=jax.ShapeDtypeStruct((rhs, group_map.shape[0]), F32),
        in_specs=[VMEM] * 3,
        out_specs=VMEM,
        compiler_params=params(),
        name="tree",
    )(nodes, parent_map, group_map)


def finish_kernel(
    far_ref, near_ref, leaf_ref, own_ref, chip_ref, beyond_ref, interp_ref, order_ref,
    out_ref, skel_ref, charge_ref, acc_ref, *, feats,
):
    leaves, slots = far_ref.shape
    rank = leaf_ref.shape[1] // leaves
    rhs, total = near_ref.shape
    width = total // leaves
    device = lax.axis_index("leaf")
    targets = []
    for region, ref in enumerate((own_ref, chip_ref, beyond_ref)):
        first = ref.shape[1] - leaves * rank
        source, target = stacked_rows(ref[:feats, first:])
        charge = ref[feats:, first:].astype(BF)
        for leaf in range(leaves):
            span = slice(leaf * rank, (leaf + 1) * rank)
            skel_ref[region * leaves + leaf] = source[:, span]
            charge_ref[region * leaves + leaf] = charge[:, span]
            if region == 0:
                targets.append(target[:, span])
    pieces = []
    for leaf in range(leaves):
        field = leaf_ref[:, leaf * rank : (leaf + 1) * rank]
        where = []
        for slot in range(slots):
            region, place = region_of(far_ref[leaf, slot], leaves)
            where.append(region * leaves + place)
        sources = jnp.concatenate([skel_ref[w] for w in where], 1)
        charges = jnp.concatenate([charge_ref[w] for w in where], 1)
        field += dot(charges, tile_of(sources, targets[leaf]))
        span = slice(leaf * width, (leaf + 1) * width)
        pieces.append(near_ref[:, span] + dot(field.astype(BF), interp_ref[:, span]))

    blocks = total // BLOCK
    shift = BLOCK.bit_length() - 1
    for leaf in range(leaves):
        index = order_ref[:, leaf * width : (leaf + 1) * width] - device * total
        hot = one_hot(index & (BLOCK - 1), BLOCK)
        high = jnp.broadcast_to(index >> shift, (rhs, width))
        hi, mid = halves(pieces[leaf])
        hi, mid = hi.astype(F32), mid.astype(F32)
        rows = []
        for k in range(blocks):
            mask = high == k
            rows.append(jnp.where(mask, hi, 0.0).astype(BF))
            rows.append(jnp.where(mask, mid, 0.0).astype(BF))
        part = dot_t(jnp.concatenate(rows, 0), hot)
        acc_ref[...] = part if leaf == 0 else acc_ref[...] + part
    for k in range(blocks):
        top = 2 * rhs * k
        out_ref[:, k * BLOCK : (k + 1) * BLOCK] = (
            acc_ref[top : top + rhs, :] + acc_ref[top + rhs : top + 2 * rhs, :]
        )


def finish(far_list, near, leaf_out, packs, interp, order, feats):
    rhs, total = near.shape
    leaves = far_list.shape[0]
    rank = interp.shape[0]
    return pl.pallas_call(
        functools.partial(finish_kernel, feats=feats),
        out_shape=jax.ShapeDtypeStruct((rhs, total), F32),
        in_specs=[SMEM] + [VMEM] * 7,
        out_specs=VMEM,
        scratch_shapes=[
            pltpu.VMEM((3 * leaves, 4 * feats + 16, rank), BF),
            pltpu.VMEM((3 * leaves, rhs, rank), BF),
            pltpu.VMEM((total // BLOCK * 2 * rhs, BLOCK), F32),
        ],
        compiler_params=params(),
        name="finish",
    )(far_list, near, leaf_out, *packs, interp, order)


def body(
    points,
    charges,
    inv_scale,
    order,
    near_list,
    near_count,
    far_list,
    skel_idx,
    interp,
    group_map,
    parent_map,
):
    feats = points.shape[0]
    leaves = near_list.shape[0]
    devices = lax.axis_size("leaf")
    order = order.reshape(1, -1)
    near_list = near_list.T
    chip = [(i, i ^ 1) for i in range(devices)]
    beyond = []
    for i in range(1, devices - 1, 2):
        beyond += [(i, i + 1), (i + 1, i)]
    early = leaves // 2

    pack, first, rest, node, sources, targets = prepare(
        inv_scale, points, charges, order, skel_idx, interp, group_map, early
    )
    pack_chip = lax.ppermute(pack, "leaf", chip)
    first = lax.ppermute(first, "leaf", beyond)
    rest = lax.ppermute(rest, "leaf", beyond)
    nodes = lax.all_gather(node, "leaf")

    def near(source, extra, region, places):
        return near_part(near_list, near_count, targets, source, extra, feats, region, places)

    total = near(pack, sources, 0, (0, leaves))
    total = near(pack_chip, total, 1, (0, leaves))
    total = near(first, total, 2, (0, early))
    total = near(rest, total, 2, (early, leaves))
    leaf_out = tree(nodes, parent_map, group_map, feats)
    return finish(far_list, total, leaf_out, (pack, pack_chip, rest), interp, order, feats)


def solution(mesh):
    placed = (
        P(None, ("fleet", "leaf")),
        P(None, ("fleet", "leaf")),
        P("fleet"),
        P(("fleet", "leaf")),
        P(("fleet", "leaf"), None),
        P(("fleet", "leaf")),
        P(("fleet", "leaf"), None),
        P(("fleet", "leaf"), None),
        P(None, ("fleet", "leaf")),
        P(("fleet", "leaf"), None),
        P("fleet", None),
    )
    return jax.shard_map(
        body, mesh=mesh, in_specs=placed, out_specs=P(None, ("fleet", "leaf")), check_vma=False
    )
```

```python
import functools
import math

import jax
import jax.numpy as jnp
from jax import lax
from jax.experimental import pallas as pl
from jax.experimental.pallas import tpu as pltpu
from jax.sharding import PartitionSpec as P

BF = jnp.bfloat16
F32 = jnp.float32
LANES = 128
BLOCK = 256
ROWS = 512
VMEM = pl.BlockSpec(memory_space=pltpu.VMEM)
SMEM = pl.BlockSpec(memory_space=pltpu.SMEM)


def params():
    return pltpu.CompilerParams(vmem_limit_bytes=48 * 2**20)


def halves(z):
    hi = z.astype(BF)
    return hi, (z - hi.astype(F32)).astype(BF)


def stacked_rows(z):
    hi, mid = halves(z)
    norm = -0.5 * jnp.sum(z * z, 0, keepdims=True)
    n1 = norm.astype(BF).astype(F32)
    n2 = (norm - n1).astype(BF).astype(F32)
    n3 = norm - n1 - n2
    shape = (16, z.shape[1])
    row = lax.broadcasted_iota(jnp.int32, shape, 0)

    def extra(first):
        out = jnp.where((row >= 3 - first) & (row < 6 - first), 1.0, 0.0)
        for i, piece in enumerate((n1, n2, n3)):
            out = jnp.where(row == first + i, jnp.broadcast_to(piece, shape), out)
        return out.astype(BF)

    source = jnp.concatenate([hi, mid, hi, mid, extra(3)], 0)
    target = jnp.concatenate([hi, hi, mid, mid, extra(0)], 0)
    return source, target


def tile_of(source, target):
    e = lax.dot_general(source, target, (((0,), (0,)), ((), ())), preferred_element_type=F32)
    return jnp.exp2(e).astype(BF)


def dot_t(a, b):
    return lax.dot_general(a, b, (((1,), (1,)), ((), ())), preferred_element_type=F32)


def dot(a, b):
    return jnp.dot(a, b, preferred_element_type=F32)


def one_hot(low, size):
    rows = lax.broadcasted_iota(jnp.int32, (size, low.shape[1]), 0)
    return (rows == low).astype(F32).astype(BF)


def pick_lanes(blocks, index):
    rows = blocks[0].shape[0]
    parts = []
    for top in range(0, rows, 8):
        idx = jnp.broadcast_to(index, (8, LANES))
        high, low = idx >> 7, idx & (LANES - 1)
        out = jnp.zeros((8, LANES), F32)
        for k, block in enumerate(blocks):
            got = jnp.take_along_axis(block[top : top + 8], low, axis=1, mode="promise_in_bounds")
            out = jnp.where(high == k, got, out)
        parts.append(out)
    return jnp.concatenate(parts, 0)


def index_kernel(order_ref, out_ref):
    out_ref[...] = order_ref[...] - lax.axis_index("leaf") * order_ref.shape[1]


def local_index(order):
    return pl.pallas_call(
        index_kernel,
        out_shape=jax.ShapeDtypeStruct(order.shape, jnp.int32),
        in_specs=[VMEM],
        out_specs=VMEM,
        compiler_params=params(),
        cost_estimate=pl.CostEstimate(flops=10**9, bytes_accessed=10**6, transcendentals=0),
        name="local_index",
    )(order)


def prepare_kernel(
    scale_ref, points_ref, charges_ref, order_ref, skel_ref, map_ref, interp_ref,
    pack_ref, source_ref, target_ref, zs_ref, bs_ref,
):
    feats, total = points_ref.shape
    rhs = charges_ref.shape[0]
    leaves, rank = skel_ref.shape
    width = total // leaves
    blocks = total // BLOCK
    shift = BLOCK.bit_length() - 1
    row = lax.broadcasted_iota(jnp.int32, (feats, LANES), 0)
    scale = jnp.zeros((feats, LANES), F32)
    for r in range(feats):
        scale = jnp.where(row == r, scale_ref[r], scale)
    scale = scale[:, :1] * math.sqrt(math.log2(math.e))
    for k in range(blocks):
        span = slice(k * BLOCK, (k + 1) * BLOCK)
        hi, mid = halves(points_ref[:, span] * scale)
        zs_ref[k * feats : (k + 1) * feats, :BLOCK] = hi
        zs_ref[k * feats : (k + 1) * feats, BLOCK:] = mid
        bs_ref[k * rhs : (k + 1) * rhs, :] = charges_ref[:, span].astype(BF)

    def step(j, carry):
        start = pl.multiple_of(j * width, width)
        index = order_ref[:, pl.ds(start, width)]
        hot = one_hot(index & (BLOCK - 1), BLOCK)
        yz = dot(zs_ref[...], jnp.concatenate([hot, hot], 0))
        yb = dot(bs_ref[...], hot)
        high = jnp.broadcast_to(index >> shift, (feats, width))
        az = jnp.zeros((feats, width), F32)
        ab = jnp.zeros((rhs, width), F32)
        for k in range(blocks):
            mask = high == k
            az = jnp.where(mask, yz[k * feats : (k + 1) * feats], az)
            ab = jnp.where(mask, yb[k * rhs : (k + 1) * rhs], ab)
        pack_ref[:feats, pl.ds(start, width)] = az
        pack_ref[feats:, pl.ds(start, width)] = ab
        source, target = stacked_rows(az)
        source_ref[:, pl.ds(start, width)] = source
        target_ref[:, pl.ds(start, width)] = target
        return carry

    lax.fori_loop(0, leaves, step, 0)
    group_q = jnp.zeros((rhs, rank), F32)
    for leaf in range(leaves):
        span = slice(leaf * width, (leaf + 1) * width)
        out = slice(total + leaf * rank, total + (leaf + 1) * rank)
        columns = [
            pack_ref[:feats, leaf * width + k : leaf * width + k + LANES]
            for k in range(0, width, LANES)
        ]
        pack_ref[:feats, out] = pick_lanes(columns, skel_ref[leaf : leaf + 1, :])
        charge = dot_t(pack_ref[feats:, span].astype(BF), interp_ref[:, span]).astype(BF)
        pack_ref[feats:, out] = charge.astype(F32)
        group_q += dot(charge, map_ref[leaf * rank : (leaf + 1) * rank, :])
    columns = [pack_ref[:feats, total + k : total + k + LANES] for k in range(0, leaves * rank, LANES)]
    node = slice(total + leaves * rank, total + (leaves + 1) * rank)
    pack_ref[:feats, node] = pick_lanes(
        columns, lax.broadcasted_iota(jnp.int32, (1, rank), 1) * leaves
    )
    pack_ref[feats:, node] = group_q


def prepare(inv_scale, points, charges, order, skel_idx, interp, group_map):
    feats, total = points.shape
    rhs = charges.shape[0]
    leaves, rank = skel_idx.shape
    blocks = total // BLOCK
    stack = 4 * feats + 16
    return pl.pallas_call(
        prepare_kernel,
        out_shape=(
            jax.ShapeDtypeStruct((feats + rhs, total + (leaves + 1) * rank), F32),
            jax.ShapeDtypeStruct((stack, total), BF),
            jax.ShapeDtypeStruct((stack, total), BF),
        ),
        in_specs=[SMEM] + [VMEM] * 6,
        out_specs=(VMEM,) * 3,
        scratch_shapes=[
            pltpu.VMEM((blocks * feats, 2 * BLOCK), BF),
            pltpu.VMEM((blocks * rhs, BLOCK), BF),
        ],
        compiler_params=params(),
        name="prepare",
    )(inv_scale, points, charges, order, skel_idx, group_map, interp)


def region_of(leaf_id, leaves):
    device = lax.axis_index("leaf")
    rel = leaf_id - (device - 1) * leaves
    side = (rel >= leaves).astype(jnp.int32) + (rel >= 2 * leaves).astype(jnp.int32)
    odd = device & 1
    region = jnp.where(side == 1, 0, jnp.where(side == 2 * (1 - odd), 1, 2))
    return region, rel - side * leaves


def near_kernel(list_ref, count_ref, target_ref, src_ref, *refs, feats, region, limits, first, after):
    refs = list(refs)
    acc_ref = None if first else refs.pop(0)
    if after:
        refs.pop(0)
    if region == 0:
        stack_ref, out_ref = refs
    else:
        out_ref, stack_ref = refs
    out_ref[...] = jnp.zeros_like(out_ref) if first else acc_ref[...]
    slots, leaves = list_ref.shape
    width = target_ref.shape[1] // leaves
    low, high = limits

    def per_leaf(leaf, seen):
        start = pl.multiple_of(leaf * width, width)

        def per_slot(slot, seen):
            found, place = region_of(list_ref[slot, leaf], leaves)
            match = found == region

            @pl.when(match & (seen >= low) & (seen < high))
            def _():
                at = pl.multiple_of(place * width, width)
                if region == 0:
                    source = stack_ref[:, pl.ds(at, width)]
                else:
                    source, _ = stacked_rows(src_ref[:feats, pl.ds(at, width)])
                    stack_ref[...] = source
                    source = stack_ref[...]
                charge = src_ref[feats:, pl.ds(at, width)].astype(BF)
                target = target_ref[:, pl.ds(start, width)]
                acc = out_ref[:, pl.ds(start, width)]
                for row in range(0, width, ROWS):
                    tile = tile_of(source[:, row : row + ROWS], target)
                    acc = acc + dot(charge[:, row : row + ROWS], tile)
                out_ref[:, pl.ds(start, width)] = acc

            return seen + match.astype(jnp.int32)

        return lax.fori_loop(0, count_ref[leaf], per_slot, seen)

    lax.fori_loop(0, leaves, per_leaf, jnp.int32(0))


def near_part(near_list, near_count, targets, source, acc, after, stack, feats, region, limits, tiles):
    slots, leaves = near_list.shape
    rhs = source.shape[0] - feats
    total = targets.shape[1]
    width = total // leaves
    extra = [value for value in (acc, after, stack) if value is not None]
    return pl.pallas_call(
        functools.partial(
            near_kernel,
            feats=feats,
            region=region,
            limits=limits,
            first=acc is None,
            after=after is not None,
        ),
        out_shape=jax.ShapeDtypeStruct((rhs, total), F32),
        in_specs=[SMEM, SMEM] + [VMEM] * (2 + len(extra)),
        out_specs=VMEM,
        scratch_shapes=[] if region == 0 else [pltpu.VMEM((targets.shape[0], width), BF)],
        compiler_params=params(),
        cost_estimate=pl.CostEstimate(
            flops=tiles * width * width * 1024,
            bytes_accessed=tiles * 48 * width * 4,
            transcendentals=tiles * width * width,
        ),
        name=f"near_{region}_{limits[0]}",
    )(near_list, near_count, targets, source, *extra)


def climb(nodes, base, levels, parent_map, feats, top=False):
    device = lax.axis_index("leaf")
    rank = nodes[0].shape[1]
    lane = lax.broadcasted_iota(jnp.int32, (1, rank), 1)
    inters = []
    for level in range(levels):
        own, other = nodes[0], nodes[1]
        source, _ = stacked_rows(other[:feats])
        _, target = stacked_rows(own[:feats])
        inters.append(dot(other[feats:].astype(BF), tile_of(source, target)))
        if top and level == levels - 1:
            break
        odd = (device >> (base + level)) & 1
        parents = []
        for k in range(0, len(nodes), 2):
            left = jnp.where(odd == 1, nodes[k + 1], nodes[k])
            right = jnp.where(odd == 1, nodes[k], nodes[k + 1])
            z = pick_lanes([left[:feats], right[:feats]], lane * 2)
            q = dot(left[feats:].astype(BF), parent_map[:rank, :])
            q += dot(right[feats:].astype(BF), parent_map[rank:, :])
            parents.append(jnp.concatenate([z, q], 0))
        nodes = parents
    return inters, nodes[0]


def climb_kernel(*refs, base, levels, feats):
    count = 2**levels
    rank = refs[count].shape[1]
    nodes = [ref[:, ref.shape[1] - rank :] for ref in refs[:count]]
    inters, node = climb(nodes, base, levels, refs[count][...], feats)
    for ref, value in zip(refs[count + 1 :], inters + [node]):
        ref[...] = value


def climb_stage(nodes, base, levels, parent_map, feats):
    rows, rank = nodes[0].shape[0], parent_map.shape[1]
    small = jax.ShapeDtypeStruct((rows - feats, rank), F32)
    outs = pl.pallas_call(
        functools.partial(climb_kernel, base=base, levels=levels, feats=feats),
        out_shape=(small,) * levels + (jax.ShapeDtypeStruct((rows, rank), F32),),
        in_specs=[VMEM] * (len(nodes) + 1),
        out_specs=(VMEM,) * (levels + 1),
        compiler_params=params(),
        name=f"climb_{base}",
    )(*nodes, parent_map)
    return list(outs[:-1]), outs[-1]


def finish_kernel(
    far_ref, near_ref, own_ref, chip_ref, beyond_ref, interp_ref, order_ref, map_ref, parent_ref,
    *refs, feats, base, levels, done,
):
    count = 2**levels
    nodes = [ref[...] for ref in refs[:count]]
    inters = [ref[...] for ref in refs[count : count + done]]
    out_ref, skel_ref, charge_ref, acc_ref = refs[count + done :]
    leaves, slots = far_ref.shape
    rank = interp_ref.shape[0]
    rhs, total = near_ref.shape
    width = total // leaves
    device = lax.axis_index("leaf")
    parent_map = parent_ref[...]
    fresh, _ = climb(nodes, base, levels, parent_map, feats, top=True)
    inters = inters + fresh
    down = inters[-1]
    for level in range(len(inters) - 2, -1, -1):
        spread = dot_t(down.astype(BF), parent_map)
        odd = (device >> level) & 1
        down = inters[level] + jnp.where(odd == 1, spread[:, rank:], spread[:, :rank])
    leaf_out = dot_t(down.astype(BF), map_ref[...])

    targets = []
    for region, ref in enumerate((own_ref, chip_ref, beyond_ref)):
        skels = slice(total, total + leaves * rank)
        source, target = stacked_rows(ref[:feats, skels])
        charge = ref[feats:, skels].astype(BF)
        for leaf in range(leaves):
            span = slice(leaf * rank, (leaf + 1) * rank)
            skel_ref[region * leaves + leaf] = source[:, span]
            charge_ref[region * leaves + leaf] = charge[:, span]
            if region == 0:
                targets.append(target[:, span])
    pieces = []
    for leaf in range(leaves):
        field = leaf_out[:, leaf * rank : (leaf + 1) * rank]
        where = []
        for slot in range(slots):
            region, place = region_of(far_ref[leaf, slot], leaves)
            where.append(region * leaves + place)
        sources = jnp.concatenate([skel_ref[w] for w in where], 1)
        charges = jnp.concatenate([charge_ref[w] for w in where], 1)
        field += dot(charges, tile_of(sources, targets[leaf]))
        span = slice(leaf * width, (leaf + 1) * width)
        pieces.append(near_ref[:, span] + dot(field.astype(BF), interp_ref[:, span]))

    blocks = total // BLOCK
    shift = BLOCK.bit_length() - 1
    for leaf in range(leaves):
        index = order_ref[:, leaf * width : (leaf + 1) * width]
        hot = one_hot(index & (BLOCK - 1), BLOCK)
        high = jnp.broadcast_to(index >> shift, (rhs, width))
        hi, mid = halves(pieces[leaf])
        hi, mid = hi.astype(F32), mid.astype(F32)
        rows = []
        for k in range(blocks):
            mask = high == k
            rows.append(jnp.where(mask, hi, 0.0).astype(BF))
            rows.append(jnp.where(mask, mid, 0.0).astype(BF))
        part = dot_t(jnp.concatenate(rows, 0), hot)
        acc_ref[...] = part if leaf == 0 else acc_ref[...] + part
    for k in range(blocks):
        top = 2 * rhs * k
        out_ref[:, k * BLOCK : (k + 1) * BLOCK] = (
            acc_ref[top : top + rhs, :] + acc_ref[top + rhs : top + 2 * rhs, :]
        )


def finish(far_list, near, packs, interp, order, group_map, parent_map, nodes, inters, base, levels, feats):
    rhs, total = near.shape
    leaves = far_list.shape[0]
    rank = interp.shape[0]
    return pl.pallas_call(
        functools.partial(finish_kernel, feats=feats, base=base, levels=levels, done=len(inters)),
        out_shape=jax.ShapeDtypeStruct((rhs, total), F32),
        in_specs=[SMEM] + [VMEM] * (8 + len(nodes) + len(inters)),
        out_specs=VMEM,
        scratch_shapes=[
            pltpu.VMEM((3 * leaves, 4 * feats + 16, rank), BF),
            pltpu.VMEM((3 * leaves, rhs, rank), BF),
            pltpu.VMEM((total // BLOCK * 2 * rhs, BLOCK), F32),
        ],
        compiler_params=params(),
        name="finish",
    )(far_list, near, *packs, interp, order, group_map, parent_map, *nodes, *inters)


def body(
    points,
    charges,
    inv_scale,
    order,
    near_list,
    near_count,
    far_list,
    skel_idx,
    interp,
    group_map,
    parent_map,
):
    feats = points.shape[0]
    leaves = near_list.shape[0]
    devices = lax.axis_size("leaf")
    order = local_index(order.reshape(1, -1))
    near_list = near_list.T
    chip = [(i, i ^ 1) for i in range(devices)]
    beyond = []
    for i in range(1, devices - 1, 2):
        beyond += [(i, i + 1), (i + 1, i)]

    def relatives(node, base, levels):
        out = [node]
        for k in range(1, 2**levels):
            pairs = [(i, i ^ (k << base)) for i in range(devices)]
            out.append(lax.ppermute(node, "leaf", pairs))
        return out

    pack, sources, targets = prepare(
        inv_scale, points, charges, order, skel_idx, interp, group_map
    )

    def near(source, acc, after, region, limits, tiles):
        stack = sources if region == 0 else None
        return near_part(
            near_list, near_count, targets, source, acc, after, stack, feats, region, limits, tiles
        )

    every = near_list.shape[0] * leaves
    pack_chip = lax.ppermute(pack, "leaf", chip)
    pack_beyond = lax.ppermute(pack, "leaf", beyond)
    levels = devices.bit_length() - 1
    stages = [(1, 1)] + [(base, min(2, levels - base)) for base in range(2, levels, 2)]
    total = near(pack, None, None, 0, (0, 2), 2)
    inters, node = climb_stage([pack, pack_chip], 0, 1, parent_map, feats)
    nodes = relatives(node, *stages[0])
    total = near(pack, total, node, 0, (2, 4), 2)
    for stage, following in zip(stages[:-1], stages[1:]):
        fresh, node = climb_stage(nodes, *stage, parent_map, feats)
        inters += fresh
        nodes = relatives(node, *following)
    total = near(pack, total, node, 0, (4, every), 3)
    total = near(pack_chip, total, None, 1, (0, every), 6)
    total = near(pack_beyond, total, None, 2, (0, every), 6)
    packs = (pack, pack_chip, pack_beyond)
    return finish(
        far_list, total, packs, interp, order, group_map, parent_map, nodes, inters, *stages[-1], feats
    )


def solution(mesh):
    placed = (
        P(None, ("fleet", "leaf")),
        P(None, ("fleet", "leaf")),
        P("fleet"),
        P(("fleet", "leaf")),
        P(("fleet", "leaf"), None),
        P(("fleet", "leaf")),
        P(("fleet", "leaf"), None),
        P(("fleet", "leaf"), None),
        P(None, ("fleet", "leaf")),
        P(("fleet", "leaf"), None),
        P("fleet", None),
    )
    return jax.shard_map(
        body, mesh=mesh, in_specs=placed, out_specs=P(None, ("fleet", "leaf")), check_vma=False
    )
```

```python
import functools
import math

import jax
import jax.numpy as jnp
from jax import lax
from jax.experimental import pallas as pl
from jax.experimental.pallas import tpu as pltpu
from jax.sharding import PartitionSpec as P

BF = jnp.bfloat16
F32 = jnp.float32
LANES = 128
BLOCK = 256
ROWS = 512
VMEM = pl.BlockSpec(memory_space=pltpu.VMEM)
SMEM = pl.BlockSpec(memory_space=pltpu.SMEM)


def params():
    return pltpu.CompilerParams(vmem_limit_bytes=48 * 2**20)


def halves(z):
    hi = z.astype(BF)
    return hi, (z - hi.astype(F32)).astype(BF)


def stacked_rows(z):
    hi, mid = halves(z)
    norm = -0.5 * jnp.sum(z * z, 0, keepdims=True)
    n1 = norm.astype(BF).astype(F32)
    n2 = (norm - n1).astype(BF).astype(F32)
    n3 = norm - n1 - n2
    shape = (16, z.shape[1])
    row = lax.broadcasted_iota(jnp.int32, shape, 0)

    def extra(first):
        out = jnp.where((row >= 3 - first) & (row < 6 - first), 1.0, 0.0)
        for i, piece in enumerate((n1, n2, n3)):
            out = jnp.where(row == first + i, jnp.broadcast_to(piece, shape), out)
        return out.astype(BF)

    source = jnp.concatenate([hi, mid, hi, mid, extra(3)], 0)
    target = jnp.concatenate([hi, hi, mid, mid, extra(0)], 0)
    return source, target


def tile_of(source, target):
    e = lax.dot_general(source, target, (((0,), (0,)), ((), ())), preferred_element_type=F32)
    return jnp.exp2(e).astype(BF)


def dot_t(a, b):
    return lax.dot_general(a, b, (((1,), (1,)), ((), ())), preferred_element_type=F32)


def dot(a, b):
    return jnp.dot(a, b, preferred_element_type=F32)


def one_hot(low, size):
    rows = lax.broadcasted_iota(jnp.int32, (size, low.shape[1]), 0)
    return (rows == low).astype(F32).astype(BF)


def pick_lanes(blocks, index):
    rows = blocks[0].shape[0]
    parts = []
    for top in range(0, rows, 8):
        idx = jnp.broadcast_to(index, (8, LANES))
        high, low = idx >> 7, idx & (LANES - 1)
        out = jnp.zeros((8, LANES), F32)
        for k, block in enumerate(blocks):
            got = jnp.take_along_axis(block[top : top + 8], low, axis=1, mode="promise_in_bounds")
            out = jnp.where(high == k, got, out)
        parts.append(out)
    return jnp.concatenate(parts, 0)


def index_kernel(order_ref, out_ref):
    out_ref[...] = order_ref[...] - lax.axis_index("leaf") * order_ref.shape[1]


def local_index(order):
    return pl.pallas_call(
        index_kernel,
        out_shape=jax.ShapeDtypeStruct(order.shape, jnp.int32),
        in_specs=[VMEM],
        out_specs=VMEM,
        compiler_params=params(),
        cost_estimate=pl.CostEstimate(flops=10**9, bytes_accessed=10**6, transcendentals=0),
        name="local_index",
    )(order)


def prepare_kernel(
    scale_ref, points_ref, charges_ref, order_ref, skel_ref, map_ref, interp_ref,
    pack_ref, node_ref, source_ref, target_ref, zs_ref, bs_ref,
):
    feats, total = points_ref.shape
    rhs = charges_ref.shape[0]
    leaves, rank = skel_ref.shape
    width = total // leaves
    blocks = total // BLOCK
    shift = BLOCK.bit_length() - 1
    row = lax.broadcasted_iota(jnp.int32, (feats, LANES), 0)
    scale = jnp.zeros((feats, LANES), F32)
    for r in range(feats):
        scale = jnp.where(row == r, scale_ref[r], scale)
    scale = scale[:, :1] * math.sqrt(math.log2(math.e))
    for k in range(blocks):
        span = slice(k * BLOCK, (k + 1) * BLOCK)
        hi, mid = halves(points_ref[:, span] * scale)
        zs_ref[k * feats : (k + 1) * feats, :BLOCK] = hi
        zs_ref[k * feats : (k + 1) * feats, BLOCK:] = mid
        bs_ref[k * rhs : (k + 1) * rhs, :] = charges_ref[:, span].astype(BF)

    def step(j, carry):
        start = pl.multiple_of(j * width, width)
        index = order_ref[:, pl.ds(start, width)]
        hot = one_hot(index & (BLOCK - 1), BLOCK)
        yz = dot(zs_ref[...], jnp.concatenate([hot, hot], 0))
        yb = dot(bs_ref[...], hot)
        high = jnp.broadcast_to(index >> shift, (feats, width))
        az = jnp.zeros((feats, width), F32)
        ab = jnp.zeros((rhs, width), F32)
        for k in range(blocks):
            mask = high == k
            az = jnp.where(mask, yz[k * feats : (k + 1) * feats], az)
            ab = jnp.where(mask, yb[k * rhs : (k + 1) * rhs], ab)
        pack_ref[:feats, pl.ds(start, width)] = az
        pack_ref[feats:, pl.ds(start, width)] = ab
        source, target = stacked_rows(az)
        source_ref[:, pl.ds(start, width)] = source
        target_ref[:, pl.ds(start, width)] = target
        return carry

    lax.fori_loop(0, leaves, step, 0)
    group_q = jnp.zeros((rhs, rank), F32)
    for leaf in range(leaves):
        span = slice(leaf * width, (leaf + 1) * width)
        out = slice(total + leaf * rank, total + (leaf + 1) * rank)
        columns = [
            pack_ref[:feats, leaf * width + k : leaf * width + k + LANES]
            for k in range(0, width, LANES)
        ]
        pack_ref[:feats, out] = pick_lanes(columns, skel_ref[leaf : leaf + 1, :])
        charge = dot_t(pack_ref[feats:, span].astype(BF), interp_ref[:, span]).astype(BF)
        pack_ref[feats:, out] = charge.astype(F32)
        group_q += dot(charge, map_ref[leaf * rank : (leaf + 1) * rank, :])
    columns = [pack_ref[:feats, total + k : total + k + LANES] for k in range(0, leaves * rank, LANES)]
    node_ref[:feats, :] = pick_lanes(
        columns, lax.broadcasted_iota(jnp.int32, (1, rank), 1) * leaves
    )
    node_ref[feats:, :] = group_q


def prepare(inv_scale, points, charges, order, skel_idx, interp, group_map):
    feats, total = points.shape
    rhs = charges.shape[0]
    leaves, rank = skel_idx.shape
    blocks = total // BLOCK
    stack = 4 * feats + 16
    return pl.pallas_call(
        prepare_kernel,
        out_shape=(
            jax.ShapeDtypeStruct((feats + rhs, total + leaves * rank), F32),
            jax.ShapeDtypeStruct((feats + rhs, rank), F32),
            jax.ShapeDtypeStruct((stack, total), BF),
            jax.ShapeDtypeStruct((stack, total), BF),
        ),
        in_specs=[SMEM] + [VMEM] * 6,
        out_specs=(VMEM,) * 4,
        scratch_shapes=[
            pltpu.VMEM((blocks * feats, 2 * BLOCK), BF),
            pltpu.VMEM((blocks * rhs, BLOCK), BF),
        ],
        compiler_params=params(),
        name="prepare",
    )(inv_scale, points, charges, order, skel_idx, group_map, interp)


def region_of(leaf_id, leaves):
    device = lax.axis_index("leaf")
    rel = leaf_id - (device - 1) * leaves
    side = (rel >= leaves).astype(jnp.int32) + (rel >= 2 * leaves).astype(jnp.int32)
    odd = device & 1
    region = jnp.where(side == 1, 0, jnp.where(side == 2 * (1 - odd), 1, 2))
    return region, rel - side * leaves


def near_kernel(list_ref, count_ref, target_ref, src_ref, *refs, feats, region, limits, first, after):
    refs = list(refs)
    acc_ref = None if first else refs.pop(0)
    if after:
        refs.pop(0)
    if region == 0:
        stack_ref, out_ref = refs
    else:
        out_ref, stack_ref = refs
    out_ref[...] = jnp.zeros_like(out_ref) if first else acc_ref[...]
    slots, leaves = list_ref.shape
    width = target_ref.shape[1] // leaves
    low, high = limits

    def per_leaf(leaf, seen):
        start = pl.multiple_of(leaf * width, width)

        def per_slot(slot, seen):
            found, place = region_of(list_ref[slot, leaf], leaves)
            match = found == region

            @pl.when(match & (seen >= low) & (seen < high))
            def _():
                at = pl.multiple_of(place * width, width)
                if region == 0:
                    source = stack_ref[:, pl.ds(at, width)]
                else:
                    source, _ = stacked_rows(src_ref[:feats, pl.ds(at, width)])
                    stack_ref[...] = source
                    source = stack_ref[...]
                charge = src_ref[feats:, pl.ds(at, width)].astype(BF)
                target = target_ref[:, pl.ds(start, width)]
                acc = out_ref[:, pl.ds(start, width)]
                for row in range(0, width, ROWS):
                    tile = tile_of(source[:, row : row + ROWS], target)
                    acc = acc + dot(charge[:, row : row + ROWS], tile)
                out_ref[:, pl.ds(start, width)] = acc

            return seen + match.astype(jnp.int32)

        return lax.fori_loop(0, count_ref[leaf], per_slot, seen)

    lax.fori_loop(0, leaves, per_leaf, jnp.int32(0))


def near_part(near_list, near_count, targets, source, acc, after, stack, feats, region, limits, tiles):
    slots, leaves = near_list.shape
    rhs = source.shape[0] - feats
    total = targets.shape[1]
    width = total // leaves
    extra = [value for value in (acc, after, stack) if value is not None]
    return pl.pallas_call(
        functools.partial(
            near_kernel,
            feats=feats,
            region=region,
            limits=limits,
            first=acc is None,
            after=after is not None,
        ),
        out_shape=jax.ShapeDtypeStruct((rhs, total), F32),
        in_specs=[SMEM, SMEM] + [VMEM] * (2 + len(extra)),
        out_specs=VMEM,
        scratch_shapes=[] if region == 0 else [pltpu.VMEM((targets.shape[0], width), BF)],
        compiler_params=params(),
        cost_estimate=pl.CostEstimate(
            flops=tiles * width * width * 1024,
            bytes_accessed=tiles * 48 * width * 4,
            transcendentals=tiles * width * width,
        ),
        name=f"near_{region}_{limits[0]}",
    )(near_list, near_count, targets, source, *extra)


def climb(nodes, base, levels, parent_map, feats, top=False):
    device = lax.axis_index("leaf")
    rank = nodes[0].shape[1]
    lane = lax.broadcasted_iota(jnp.int32, (1, rank), 1)
    inters = []
    for level in range(levels):
        own, other = nodes[0], nodes[1]
        source, _ = stacked_rows(other[:feats])
        _, target = stacked_rows(own[:feats])
        inters.append(dot(other[feats:].astype(BF), tile_of(source, target)))
        if top and level == levels - 1:
            break
        odd = (device >> (base + level)) & 1
        parents = []
        for k in range(0, len(nodes), 2):
            left = jnp.where(odd == 1, nodes[k + 1], nodes[k])
            right = jnp.where(odd == 1, nodes[k], nodes[k + 1])
            z = pick_lanes([left[:feats], right[:feats]], lane * 2)
            q = dot(left[feats:].astype(BF), parent_map[:rank, :])
            q += dot(right[feats:].astype(BF), parent_map[rank:, :])
            parents.append(jnp.concatenate([z, q], 0))
        nodes = parents
    return inters, nodes[0]


def climb_kernel(*refs, base, levels, feats):
    count = 2**levels
    nodes = [ref[...] for ref in refs[:count]]
    inters, node = climb(nodes, base, levels, refs[count][...], feats)
    for ref, value in zip(refs[count + 1 :], inters + [node]):
        ref[...] = value


def climb_stage(nodes, base, levels, parent_map, feats):
    rows, rank = nodes[0].shape
    small = jax.ShapeDtypeStruct((rows - feats, rank), F32)
    outs = pl.pallas_call(
        functools.partial(climb_kernel, base=base, levels=levels, feats=feats),
        out_shape=(small,) * levels + (jax.ShapeDtypeStruct((rows, rank), F32),),
        in_specs=[VMEM] * (len(nodes) + 1),
        out_specs=(VMEM,) * (levels + 1),
        compiler_params=params(),
        name=f"climb_{base}",
    )(*nodes, parent_map)
    return list(outs[:-1]), outs[-1]


def finish_kernel(
    far_ref, near_ref, own_ref, chip_ref, beyond_ref, interp_ref, order_ref, map_ref, parent_ref,
    *refs, feats, base, levels, done,
):
    count = 2**levels
    nodes = [ref[...] for ref in refs[:count]]
    inters = [ref[...] for ref in refs[count : count + done]]
    out_ref, skel_ref, charge_ref, acc_ref = refs[count + done :]
    leaves, slots = far_ref.shape
    rank = interp_ref.shape[0]
    rhs, total = near_ref.shape
    width = total // leaves
    device = lax.axis_index("leaf")
    parent_map = parent_ref[...]
    fresh, _ = climb(nodes, base, levels, parent_map, feats, top=True)
    inters = inters + fresh
    down = inters[-1]
    for level in range(len(inters) - 2, -1, -1):
        spread = dot_t(down.astype(BF), parent_map)
        odd = (device >> level) & 1
        down = inters[level] + jnp.where(odd == 1, spread[:, rank:], spread[:, :rank])
    leaf_out = dot_t(down.astype(BF), map_ref[...])

    targets = []
    for region, ref in enumerate((own_ref, chip_ref, beyond_ref)):
        skels = slice(total, total + leaves * rank)
        source, target = stacked_rows(ref[:feats, skels])
        charge = ref[feats:, skels].astype(BF)
        for leaf in range(leaves):
            span = slice(leaf * rank, (leaf + 1) * rank)
            skel_ref[region * leaves + leaf] = source[:, span]
            charge_ref[region * leaves + leaf] = charge[:, span]
            if region == 0:
                targets.append(target[:, span])
    pieces = []
    for leaf in range(leaves):
        field = leaf_out[:, leaf * rank : (leaf + 1) * rank]
        where = []
        for slot in range(slots):
            region, place = region_of(far_ref[leaf, slot], leaves)
            where.append(region * leaves + place)
        sources = jnp.concatenate([skel_ref[w] for w in where], 1)
        charges = jnp.concatenate([charge_ref[w] for w in where], 1)
        field += dot(charges, tile_of(sources, targets[leaf]))
        span = slice(leaf * width, (leaf + 1) * width)
        pieces.append(near_ref[:, span] + dot(field.astype(BF), interp_ref[:, span]))

    blocks = total // BLOCK
    shift = BLOCK.bit_length() - 1
    for leaf in range(leaves):
        index = order_ref[:, leaf * width : (leaf + 1) * width]
        hot = one_hot(index & (BLOCK - 1), BLOCK)
        high = jnp.broadcast_to(index >> shift, (rhs, width))
        hi, mid = halves(pieces[leaf])
        hi, mid = hi.astype(F32), mid.astype(F32)
        rows = []
        for k in range(blocks):
            mask = high == k
            rows.append(jnp.where(mask, hi, 0.0).astype(BF))
            rows.append(jnp.where(mask, mid, 0.0).astype(BF))
        part = dot_t(jnp.concatenate(rows, 0), hot)
        acc_ref[...] = part if leaf == 0 else acc_ref[...] + part
    for k in range(blocks):
        top = 2 * rhs * k
        out_ref[:, k * BLOCK : (k + 1) * BLOCK] = (
            acc_ref[top : top + rhs, :] + acc_ref[top + rhs : top + 2 * rhs, :]
        )


def finish(far_list, near, packs, interp, order, group_map, parent_map, nodes, inters, base, levels, feats):
    rhs, total = near.shape
    leaves = far_list.shape[0]
    rank = interp.shape[0]
    return pl.pallas_call(
        functools.partial(finish_kernel, feats=feats, base=base, levels=levels, done=len(inters)),
        out_shape=jax.ShapeDtypeStruct((rhs, total), F32),
        in_specs=[SMEM] + [VMEM] * (8 + len(nodes) + len(inters)),
        out_specs=VMEM,
        scratch_shapes=[
            pltpu.VMEM((3 * leaves, 4 * feats + 16, rank), BF),
            pltpu.VMEM((3 * leaves, rhs, rank), BF),
            pltpu.VMEM((total // BLOCK * 2 * rhs, BLOCK), F32),
        ],
        compiler_params=params(),
        name="finish",
    )(far_list, near, *packs, interp, order, group_map, parent_map, *nodes, *inters)


def body(
    points,
    charges,
    inv_scale,
    order,
    near_list,
    near_count,
    far_list,
    skel_idx,
    interp,
    group_map,
    parent_map,
):
    feats = points.shape[0]
    leaves = near_list.shape[0]
    devices = lax.axis_size("leaf")
    order = local_index(order.reshape(1, -1))
    near_list = near_list.T
    chip = [(i, i ^ 1) for i in range(devices)]
    beyond = []
    for i in range(1, devices - 1, 2):
        beyond += [(i, i + 1), (i + 1, i)]

    def relatives(node, base, levels):
        out = [node]
        for k in range(1, 2**levels):
            pairs = [(i, i ^ (k << base)) for i in range(devices)]
            out.append(lax.ppermute(node, "leaf", pairs))
        return out

    pack, node, sources, targets = prepare(
        inv_scale, points, charges, order, skel_idx, interp, group_map
    )

    def near(source, acc, after, region, limits, tiles):
        stack = sources if region == 0 else None
        return near_part(
            near_list, near_count, targets, source, acc, after, stack, feats, region, limits, tiles
        )

    every = near_list.shape[0] * leaves
    levels = devices.bit_length() - 1
    stages = [(base, min(2, levels - base)) for base in range(0, levels, 2)]
    nodes = relatives(node, *stages[0])
    pack_beyond = lax.ppermute(pack, "leaf", beyond)
    pack_chip = lax.ppermute(pack, "leaf", chip)
    total = near(pack, None, None, 0, (0, 2), 2)
    inters = []
    for stage, following in zip(stages[:-1], stages[1:]):
        fresh, node = climb_stage(nodes, *stage, parent_map, feats)
        inters += fresh
        nodes = relatives(node, *following)
    total = near(pack, total, node, 0, (2, every), 4)
    total = near(pack_chip, total, None, 1, (0, every), 6)
    total = near(pack_beyond, total, None, 2, (0, every), 6)
    packs = (pack, pack_chip, pack_beyond)
    return finish(
        far_list, total, packs, interp, order, group_map, parent_map, nodes, inters, *stages[-1], feats
    )


def solution(mesh):
    placed = (
        P(None, ("fleet", "leaf")),
        P(None, ("fleet", "leaf")),
        P("fleet"),
        P(("fleet", "leaf")),
        P(("fleet", "leaf"), None),
        P(("fleet", "leaf")),
        P(("fleet", "leaf"), None),
        P(("fleet", "leaf"), None),
        P(None, ("fleet", "leaf")),
        P(("fleet", "leaf"), None),
        P("fleet", None),
    )
    return jax.shard_map(
        body, mesh=mesh, in_specs=placed, out_specs=P(None, ("fleet", "leaf")), check_vma=False
    )
```

```python
import functools
import math

import jax
import jax.numpy as jnp
from jax import lax
from jax.experimental import pallas as pl
from jax.experimental.pallas import tpu as pltpu
from jax.sharding import PartitionSpec as P

BF = jnp.bfloat16
F32 = jnp.float32
LANES = 128
BLOCK = 256
CHUNK = 1024
ROWS = 512
VMEM = pl.BlockSpec(memory_space=pltpu.VMEM)
SMEM = pl.BlockSpec(memory_space=pltpu.SMEM)


def params():
    return pltpu.CompilerParams(vmem_limit_bytes=48 * 2**20)


def halves(z):
    hi = z.astype(BF)
    return hi, (z - hi.astype(F32)).astype(BF)


def stacked_rows(z):
    hi, mid = halves(z)
    norm = -0.5 * jnp.sum(z * z, 0, keepdims=True)
    n1 = norm.astype(BF).astype(F32)
    n2 = (norm - n1).astype(BF).astype(F32)
    n3 = norm - n1 - n2
    shape = (16, z.shape[1])
    row = lax.broadcasted_iota(jnp.int32, shape, 0)

    def extra(first):
        out = jnp.where((row >= 3 - first) & (row < 6 - first), 1.0, 0.0)
        for i, piece in enumerate((n1, n2, n3)):
            out = jnp.where(row == first + i, jnp.broadcast_to(piece, shape), out)
        return out.astype(BF)

    source = jnp.concatenate([hi, mid, hi, mid, extra(3)], 0)
    target = jnp.concatenate([hi, hi, mid, mid, extra(0)], 0)
    return source, target


def tile_of(source, target):
    e = lax.dot_general(source, target, (((0,), (0,)), ((), ())), preferred_element_type=F32)
    return jnp.exp2(e).astype(BF)


def dot_t(a, b):
    return lax.dot_general(a, b, (((1,), (1,)), ((), ())), preferred_element_type=F32)


def dot(a, b):
    return jnp.dot(a, b, preferred_element_type=F32)


def one_hot(low, size):
    rows = lax.broadcasted_iota(jnp.int32, (size, low.shape[1]), 0)
    return (rows == low).astype(F32).astype(BF)


def pick_lanes(blocks, index):
    rows = blocks[0].shape[0]
    parts = []
    for top in range(0, rows, 8):
        idx = jnp.broadcast_to(index, (8, LANES))
        high, low = idx >> 7, idx & (LANES - 1)
        out = jnp.zeros((8, LANES), F32)
        for k, block in enumerate(blocks):
            got = jnp.take_along_axis(block[top : top + 8], low, axis=1, mode="promise_in_bounds")
            out = jnp.where(high == k, got, out)
        parts.append(out)
    return jnp.concatenate(parts, 0)


def index_kernel(order_ref, out_ref):
    out_ref[...] = order_ref[...] - lax.axis_index("leaf") * order_ref.shape[1]


def local_index(order):
    return pl.pallas_call(
        index_kernel,
        out_shape=jax.ShapeDtypeStruct(order.shape, jnp.int32),
        in_specs=[VMEM],
        out_specs=VMEM,
        compiler_params=params(),
        cost_estimate=pl.CostEstimate(flops=10**9, bytes_accessed=10**6, transcendentals=0),
        name="local_index",
    )(order)


def sort_kernel(
    scale_ref, points_ref, charges_ref, order_ref,
    pack_ref, source_ref, target_ref, zs_ref, bs_ref,
):
    feats, total = points_ref.shape
    rhs = charges_ref.shape[0]
    blocks = total // BLOCK
    shift = BLOCK.bit_length() - 1
    row = lax.broadcasted_iota(jnp.int32, (feats, LANES), 0)
    scale = jnp.zeros((feats, LANES), F32)
    for r in range(feats):
        scale = jnp.where(row == r, scale_ref[r], scale)
    scale = scale[:, :1] * math.sqrt(math.log2(math.e))
    for k in range(blocks):
        span = slice(k * BLOCK, (k + 1) * BLOCK)
        hi, mid = halves(points_ref[:, span] * scale)
        zs_ref[k * feats : (k + 1) * feats, :BLOCK] = hi
        zs_ref[k * feats : (k + 1) * feats, BLOCK:] = mid
        bs_ref[k * rhs : (k + 1) * rhs, :] = charges_ref[:, span].astype(BF)

    def step(j, carry):
        start = pl.multiple_of(j * CHUNK, CHUNK)
        index = order_ref[:, pl.ds(start, CHUNK)]
        hot = one_hot(index & (BLOCK - 1), BLOCK)
        yz = dot(zs_ref[...], jnp.concatenate([hot, hot], 0))
        yb = dot(bs_ref[...], hot)
        high = jnp.broadcast_to(index >> shift, (feats, CHUNK))
        az = jnp.zeros((feats, CHUNK), F32)
        ab = jnp.zeros((rhs, CHUNK), F32)
        for k in range(blocks):
            mask = high == k
            az = jnp.where(mask, yz[k * feats : (k + 1) * feats], az)
            ab = jnp.where(mask, yb[k * rhs : (k + 1) * rhs], ab)
        pack_ref[:feats, pl.ds(start, CHUNK)] = az
        pack_ref[feats:, pl.ds(start, CHUNK)] = ab
        source, target = stacked_rows(az)
        source_ref[:, pl.ds(start, CHUNK)] = source
        target_ref[:, pl.ds(start, CHUNK)] = target
        return carry

    lax.fori_loop(0, total // CHUNK, step, 0)


def sort_points(inv_scale, points, charges, order):
    feats, total = points.shape
    rhs = charges.shape[0]
    blocks = total // BLOCK
    stack = 4 * feats + 16
    return pl.pallas_call(
        sort_kernel,
        out_shape=(
            jax.ShapeDtypeStruct((feats + rhs, total), F32),
            jax.ShapeDtypeStruct((stack, total), BF),
            jax.ShapeDtypeStruct((stack, total), BF),
        ),
        in_specs=[SMEM] + [VMEM] * 3,
        out_specs=(VMEM,) * 3,
        scratch_shapes=[
            pltpu.VMEM((blocks * feats, 2 * BLOCK), BF),
            pltpu.VMEM((blocks * rhs, BLOCK), BF),
        ],
        compiler_params=params(),
        cost_estimate=pl.CostEstimate(
            flops=6 * total * total * 16, bytes_accessed=4 * 10**6, transcendentals=0
        ),
        name="sort_points",
    )(inv_scale, points, charges, order)


def skeleton_kernel(
    sorted_ref, skel_ref, map_ref, interp_ref, pack_ref, first_ref, rest_ref, node_ref, *, feats
):
    leaves, rank = skel_ref.shape
    rows, total = sorted_ref.shape
    width = total // leaves
    group_q = jnp.zeros((rows - feats, rank), F32)
    for leaf in range(leaves):
        span = slice(leaf * width, (leaf + 1) * width)
        out = slice(total + leaf * rank, total + (leaf + 1) * rank)
        columns = [
            sorted_ref[:feats, leaf * width + k : leaf * width + k + LANES]
            for k in range(0, width, LANES)
        ]
        pack_ref[:feats, out] = pick_lanes(columns, skel_ref[leaf : leaf + 1, :])
        charge = dot_t(sorted_ref[feats:, span].astype(BF), interp_ref[:, span]).astype(BF)
        pack_ref[feats:, out] = charge.astype(F32)
        group_q += dot(charge, map_ref[leaf * rank : (leaf + 1) * rank, :])
        pack_ref[:, span] = sorted_ref[:, span]
    columns = [pack_ref[:feats, total + k : total + k + LANES] for k in range(0, leaves * rank, LANES)]
    node_ref[:feats, :] = pick_lanes(
        columns, lax.broadcasted_iota(jnp.int32, (1, rank), 1) * leaves
    )
    node_ref[feats:, :] = group_q
    pack_ref[:, total + leaves * rank :] = node_ref[...]
    early = total - rest_ref.shape[1]
    first_ref[:, :early] = sorted_ref[:, :early]
    first_ref[:, early:] = pack_ref[:, total : total + leaves * rank]
    rest_ref[...] = sorted_ref[:, early:]


def skeletons(points, skel_idx, group_map, interp, feats, early):
    rows, total = points.shape
    leaves, rank = skel_idx.shape
    skels = leaves * rank
    return pl.pallas_call(
        functools.partial(skeleton_kernel, feats=feats),
        out_shape=(
            jax.ShapeDtypeStruct((rows, total + skels + rank), F32),
            jax.ShapeDtypeStruct((rows, early + skels), F32),
            jax.ShapeDtypeStruct((rows, total - early), F32),
            jax.ShapeDtypeStruct((rows, rank), F32),
        ),
        in_specs=[VMEM] * 4,
        out_specs=(VMEM,) * 4,
        compiler_params=params(),
        name="skeletons",
    )(points, skel_idx, group_map, interp)


def region_of(leaf_id, leaves):
    device = lax.axis_index("leaf")
    rel = leaf_id - (device - 1) * leaves
    side = (rel >= leaves).astype(jnp.int32) + (rel >= 2 * leaves).astype(jnp.int32)
    odd = device & 1
    region = jnp.where(side == 1, 0, jnp.where(side == 2 * (1 - odd), 1, 2))
    return region, rel - side * leaves


def near_kernel(list_ref, count_ref, target_ref, src_ref, *refs, feats, region, limits, places, first, after):
    refs = list(refs)
    acc_ref = None if first else refs.pop(0)
    if after:
        refs.pop(0)
    if region == 0:
        stack_ref, out_ref = refs
    else:
        out_ref, stack_ref = refs
    out_ref[...] = jnp.zeros_like(out_ref) if first else acc_ref[...]
    slots, leaves = list_ref.shape
    width = target_ref.shape[1] // leaves
    low, high = limits

    def per_leaf(leaf, seen):
        start = pl.multiple_of(leaf * width, width)

        def per_slot(slot, seen):
            found, place = region_of(list_ref[slot, leaf], leaves)
            match = (found == region) & (place >= places[0]) & (place < places[1])

            @pl.when(match & (seen >= low) & (seen < high))
            def _():
                at = pl.multiple_of((place - places[0]) * width, width)
                if region == 0:
                    source = stack_ref[:, pl.ds(at, width)]
                else:
                    source, _ = stacked_rows(src_ref[:feats, pl.ds(at, width)])
                    stack_ref[...] = source
                    source = stack_ref[...]
                charge = src_ref[feats:, pl.ds(at, width)].astype(BF)
                target = target_ref[:, pl.ds(start, width)]
                acc = out_ref[:, pl.ds(start, width)]
                for row in range(0, width, ROWS):
                    tile = tile_of(source[:, row : row + ROWS], target)
                    acc = acc + dot(charge[:, row : row + ROWS], tile)
                out_ref[:, pl.ds(start, width)] = acc

            return seen + match.astype(jnp.int32)

        return lax.fori_loop(0, count_ref[leaf], per_slot, seen)

    lax.fori_loop(0, leaves, per_leaf, jnp.int32(0))


def near_part(near_list, near_count, targets, source, acc, after, stack, feats, region, limits, places, tiles):
    slots, leaves = near_list.shape
    rhs = source.shape[0] - feats
    total = targets.shape[1]
    width = total // leaves
    extra = [value for value in (acc, after, stack) if value is not None]
    return pl.pallas_call(
        functools.partial(
            near_kernel,
            feats=feats,
            region=region,
            limits=limits,
            places=places,
            first=acc is None,
            after=after is not None,
        ),
        out_shape=jax.ShapeDtypeStruct((rhs, total), F32),
        in_specs=[SMEM, SMEM] + [VMEM] * (2 + len(extra)),
        out_specs=VMEM,
        scratch_shapes=[] if region == 0 else [pltpu.VMEM((targets.shape[0], width), BF)],
        compiler_params=params(),
        cost_estimate=pl.CostEstimate(
            flops=tiles * width * width * 1024,
            bytes_accessed=tiles * 48 * width * 4,
            transcendentals=tiles * width * width,
        ),
        name=f"near_{region}_{limits[0]}_{places[0]}",
    )(near_list, near_count, targets, source, *extra)


def climb(nodes, base, levels, parent_map, feats, top=False):
    device = lax.axis_index("leaf")
    rank = nodes[0].shape[1]
    lane = lax.broadcasted_iota(jnp.int32, (1, rank), 1)
    inters = []
    for level in range(levels):
        own, other = nodes[0], nodes[1]
        source, _ = stacked_rows(other[:feats])
        _, target = stacked_rows(own[:feats])
        inters.append(dot(other[feats:].astype(BF), tile_of(source, target)))
        if top and level == levels - 1:
            break
        odd = (device >> (base + level)) & 1
        parents = []
        for k in range(0, len(nodes), 2):
            left = jnp.where(odd == 1, nodes[k + 1], nodes[k])
            right = jnp.where(odd == 1, nodes[k], nodes[k + 1])
            z = pick_lanes([left[:feats], right[:feats]], lane * 2)
            q = dot(left[feats:].astype(BF), parent_map[:rank, :])
            q += dot(right[feats:].astype(BF), parent_map[rank:, :])
            parents.append(jnp.concatenate([z, q], 0))
        nodes = parents
    return inters, nodes[0]


def climb_kernel(*refs, base, levels, feats):
    count = 2**levels
    rank = refs[count].shape[1]
    nodes = [ref[:, ref.shape[1] - rank :] for ref in refs[:count]]
    inters, node = climb(nodes, base, levels, refs[count][...], feats)
    for ref, value in zip(refs[count + 1 :], inters + [node]):
        ref[...] = value


def climb_stage(nodes, base, levels, parent_map, feats):
    rows, rank = nodes[0].shape[0], parent_map.shape[1]
    small = jax.ShapeDtypeStruct((rows - feats, rank), F32)
    outs = pl.pallas_call(
        functools.partial(climb_kernel, base=base, levels=levels, feats=feats),
        out_shape=(small,) * levels + (jax.ShapeDtypeStruct((rows, rank), F32),),
        in_specs=[VMEM] * (len(nodes) + 1),
        out_specs=(VMEM,) * (levels + 1),
        compiler_params=params(),
        name=f"climb_{base}",
    )(*nodes, parent_map)
    return list(outs[:-1]), outs[-1]


def finish_kernel(
    far_ref, near_ref, own_ref, chip_ref, beyond_ref, interp_ref, order_ref, map_ref, parent_ref,
    *refs, feats, base, levels, done,
):
    count = 2**levels
    nodes = [ref[...] for ref in refs[:count]]
    inters = [ref[...] for ref in refs[count : count + done]]
    out_ref, skel_ref, charge_ref, acc_ref = refs[count + done :]
    leaves, slots = far_ref.shape
    rank = interp_ref.shape[0]
    rhs, total = near_ref.shape
    width = total // leaves
    device = lax.axis_index("leaf")
    parent_map = parent_ref[...]
    fresh, _ = climb(nodes, base, levels, parent_map, feats, top=True)
    inters = inters + fresh
    down = inters[-1]
    for level in range(len(inters) - 2, -1, -1):
        spread = dot_t(down.astype(BF), parent_map)
        odd = (device >> level) & 1
        down = inters[level] + jnp.where(odd == 1, spread[:, rank:], spread[:, :rank])
    leaf_out = dot_t(down.astype(BF), map_ref[...])

    targets = []
    for region, ref in enumerate((own_ref, chip_ref, beyond_ref)):
        first = ref.shape[1] - leaves * rank if region == 2 else total
        skels = slice(first, first + leaves * rank)
        source, target = stacked_rows(ref[:feats, skels])
        charge = ref[feats:, skels].astype(BF)
        for leaf in range(leaves):
            span = slice(leaf * rank, (leaf + 1) * rank)
            skel_ref[region * leaves + leaf] = source[:, span]
            charge_ref[region * leaves + leaf] = charge[:, span]
            if region == 0:
                targets.append(target[:, span])
    pieces = []
    for leaf in range(leaves):
        field = leaf_out[:, leaf * rank : (leaf + 1) * rank]
        where = []
        for slot in range(slots):
            region, place = region_of(far_ref[leaf, slot], leaves)
            where.append(region * leaves + place)
        sources = jnp.concatenate([skel_ref[w] for w in where], 1)
        charges = jnp.concatenate([charge_ref[w] for w in where], 1)
        field += dot(charges, tile_of(sources, targets[leaf]))
        span = slice(leaf * width, (leaf + 1) * width)
        pieces.append(near_ref[:, span] + dot(field.astype(BF), interp_ref[:, span]))

    blocks = total // BLOCK
    shift = BLOCK.bit_length() - 1
    for leaf in range(leaves):
        index = order_ref[:, leaf * width : (leaf + 1) * width]
        hot = one_hot(index & (BLOCK - 1), BLOCK)
        high = jnp.broadcast_to(index >> shift, (rhs, width))
        hi, mid = halves(pieces[leaf])
        hi, mid = hi.astype(F32), mid.astype(F32)
        rows = []
        for k in range(blocks):
            mask = high == k
            rows.append(jnp.where(mask, hi, 0.0).astype(BF))
            rows.append(jnp.where(mask, mid, 0.0).astype(BF))
        part = dot_t(jnp.concatenate(rows, 0), hot)
        acc_ref[...] = part if leaf == 0 else acc_ref[...] + part
    for k in range(blocks):
        top = 2 * rhs * k
        out_ref[:, k * BLOCK : (k + 1) * BLOCK] = (
            acc_ref[top : top + rhs, :] + acc_ref[top + rhs : top + 2 * rhs, :]
        )


def finish(far_list, near, packs, interp, order, group_map, parent_map, nodes, inters, base, levels, feats):
    rhs, total = near.shape
    leaves = far_list.shape[0]
    rank = interp.shape[0]
    return pl.pallas_call(
        functools.partial(finish_kernel, feats=feats, base=base, levels=levels, done=len(inters)),
        out_shape=jax.ShapeDtypeStruct((rhs, total), F32),
        in_specs=[SMEM] + [VMEM] * (8 + len(nodes) + len(inters)),
        out_specs=VMEM,
        scratch_shapes=[
            pltpu.VMEM((3 * leaves, 4 * feats + 16, rank), BF),
            pltpu.VMEM((3 * leaves, rhs, rank), BF),
            pltpu.VMEM((total // BLOCK * 2 * rhs, BLOCK), F32),
        ],
        compiler_params=params(),
        name="finish",
    )(far_list, near, *packs, interp, order, group_map, parent_map, *nodes, *inters)


def body(
    points,
    charges,
    inv_scale,
    order,
    near_list,
    near_count,
    far_list,
    skel_idx,
    interp,
    group_map,
    parent_map,
):
    feats = points.shape[0]
    leaves = near_list.shape[0]
    devices = lax.axis_size("leaf")
    order = local_index(order.reshape(1, -1))
    near_list = near_list.T
    chip = [(i, i ^ 1) for i in range(devices)]
    beyond = []
    for i in range(1, devices - 1, 2):
        beyond += [(i, i + 1), (i + 1, i)]

    def send(value, mask):
        return lax.ppermute(value, "leaf", [(i, i ^ mask) for i in range(devices)])

    width = points.shape[1] // leaves
    early = leaves // 2
    placed, sources, targets = sort_points(inv_scale, points, charges, order)
    pack, first, rest, node = skeletons(placed, skel_idx, group_map, interp, feats, early * width)

    def near(source, acc, after, region, limits, places, tiles):
        stack = sources if region == 0 else None
        return near_part(
            near_list, near_count, targets, source, acc, after, stack, feats, region, limits, places, tiles
        )

    every = near_list.shape[0] * leaves
    levels = devices.bit_length() - 1
    stages = [(base, min(2, levels - base)) for base in range(0, levels, 2)]
    pack_chip = send(pack, 1)
    nodes = [node, pack_chip] + [send(node, mask) for mask in range(2, 2 ** stages[0][1])]
    first = lax.ppermute(first, "leaf", beyond)
    rest = lax.ppermute(rest, "leaf", beyond)
    total = near(pack, None, None, 0, (0, 2), (0, leaves), 2)
    inters = []
    for stage, (base, count) in zip(stages[:-1], stages[1:]):
        fresh, node = climb_stage(nodes, *stage, parent_map, feats)
        inters += fresh
        nodes = [node] + [send(node, mask << base) for mask in range(1, 2**count)]
    total = near(pack, total, node, 0, (2, every), (0, leaves), 4)
    total = near(pack_chip, total, None, 1, (0, every), (0, leaves), 6)
    total = near(rest, total, None, 2, (0, every), (early, leaves), 3)
    total = near(first, total, None, 2, (0, every), (0, early), 3)
    packs = (pack, pack_chip, first)
    return finish(
        far_list, total, packs, interp, order, group_map, parent_map, nodes, inters, *stages[-1], feats
    )


def solution(mesh):
    placed = (
        P(None, ("fleet", "leaf")),
        P(None, ("fleet", "leaf")),
        P("fleet"),
        P(("fleet", "leaf")),
        P(("fleet", "leaf"), None),
        P(("fleet", "leaf")),
        P(("fleet", "leaf"), None),
        P(("fleet", "leaf"), None),
        P(None, ("fleet", "leaf")),
        P(("fleet", "leaf"), None),
        P("fleet", None),
    )
    return jax.shard_map(
        body, mesh=mesh, in_specs=placed, out_specs=P(None, ("fleet", "leaf")), check_vma=False
    )
```

```python
import functools
import math

import jax
import jax.numpy as jnp
from jax import lax
from jax.experimental import pallas as pl
from jax.experimental.pallas import tpu as pltpu
from jax.sharding import PartitionSpec as P

BF = jnp.bfloat16
F32 = jnp.float32
LANES = 128
BLOCK = 256
CHUNK = 512
VMEM = pl.BlockSpec(memory_space=pltpu.VMEM)
SMEM = pl.BlockSpec(memory_space=pltpu.SMEM)


def params():
    return pltpu.CompilerParams(vmem_limit_bytes=48 * 2**20)


def halves(z):
    hi = z.astype(BF)
    return hi, (z - hi.astype(F32)).astype(BF)


def stacked_rows(z):
    hi, mid = halves(z)
    norm = -0.5 * jnp.sum(z * z, 0, keepdims=True)
    n1 = norm.astype(BF).astype(F32)
    n2 = (norm - n1).astype(BF).astype(F32)
    n3 = norm - n1 - n2
    shape = (16, z.shape[1])
    row = lax.broadcasted_iota(jnp.int32, shape, 0)

    def extra(first):
        out = jnp.where((row >= 3 - first) & (row < 6 - first), 1.0, 0.0)
        for i, piece in enumerate((n1, n2, n3)):
            out = jnp.where(row == first + i, jnp.broadcast_to(piece, shape), out)
        return out.astype(BF)

    source = jnp.concatenate([hi, mid, hi, mid, extra(3)], 0)
    target = jnp.concatenate([hi, hi, mid, mid, extra(0)], 0)
    return source, target


def tile_of(source, target):
    e = lax.dot_general(source, target, (((0,), (0,)), ((), ())), preferred_element_type=F32)
    return jnp.exp2(e).astype(BF)


def dot_t(a, b):
    return lax.dot_general(a, b, (((1,), (1,)), ((), ())), preferred_element_type=F32)


def dot(a, b):
    return jnp.dot(a, b, preferred_element_type=F32)


def one_hot(low, size):
    rows = lax.broadcasted_iota(jnp.int32, (size, low.shape[1]), 0)
    return (rows == low).astype(F32).astype(BF)


def pick_lanes(blocks, index):
    rows = blocks[0].shape[0]
    parts = []
    for top in range(0, rows, 8):
        idx = jnp.broadcast_to(index, (8, LANES))
        high, low = idx >> 7, idx & (LANES - 1)
        out = jnp.zeros((8, LANES), F32)
        for k, block in enumerate(blocks):
            got = jnp.take_along_axis(block[top : top + 8], low, axis=1, mode="promise_in_bounds")
            out = jnp.where(high == k, got, out)
        parts.append(out)
    return jnp.concatenate(parts, 0)


def index_kernel(order_ref, out_ref):
    out_ref[...] = order_ref[...] - lax.axis_index("leaf") * order_ref.shape[1]


def local_index(order):
    return pl.pallas_call(
        index_kernel,
        out_shape=jax.ShapeDtypeStruct(order.shape, jnp.int32),
        in_specs=[VMEM],
        out_specs=VMEM,
        compiler_params=params(),
        cost_estimate=pl.CostEstimate(flops=10**9, bytes_accessed=10**6, transcendentals=0),
        name="local_index",
    )(order)


def sort_kernel(
    scale_ref, points_ref, charges_ref, order_ref,
    pack_ref, source_ref, target_ref, zs_ref, bs_ref,
):
    feats, total = points_ref.shape
    rhs = charges_ref.shape[0]
    blocks = total // BLOCK
    shift = BLOCK.bit_length() - 1
    row = lax.broadcasted_iota(jnp.int32, (feats, LANES), 0)
    scale = jnp.zeros((feats, LANES), F32)
    for r in range(feats):
        scale = jnp.where(row == r, scale_ref[r], scale)
    scale = scale[:, :1] * math.sqrt(math.log2(math.e))
    for k in range(blocks):
        span = slice(k * BLOCK, (k + 1) * BLOCK)
        hi, mid = halves(points_ref[:, span] * scale)
        zs_ref[k * feats : (k + 1) * feats, :BLOCK] = hi
        zs_ref[k * feats : (k + 1) * feats, BLOCK:] = mid
        bs_ref[k * rhs : (k + 1) * rhs, :] = charges_ref[:, span].astype(BF)

    def step(j, carry):
        start = pl.multiple_of(j * CHUNK, CHUNK)
        index = order_ref[:, pl.ds(start, CHUNK)]
        hot = one_hot(index & (BLOCK - 1), BLOCK)
        yz = dot(zs_ref[...], jnp.concatenate([hot, hot], 0))
        yb = dot(bs_ref[...], hot)
        high = jnp.broadcast_to(index >> shift, (feats, CHUNK))
        az = jnp.zeros((feats, CHUNK), F32)
        ab = jnp.zeros((rhs, CHUNK), F32)
        for k in range(blocks):
            mask = high == k
            az = jnp.where(mask, yz[k * feats : (k + 1) * feats], az)
            ab = jnp.where(mask, yb[k * rhs : (k + 1) * rhs], ab)
        pack_ref[:feats, pl.ds(start, CHUNK)] = az
        pack_ref[feats:, pl.ds(start, CHUNK)] = ab
        source, target = stacked_rows(az)
        source_ref[:, pl.ds(start, CHUNK)] = source
        target_ref[:, pl.ds(start, CHUNK)] = target
        return carry

    lax.fori_loop(0, total // CHUNK, step, 0, unroll=True)


def sort_points(inv_scale, points, charges, order):
    feats, total = points.shape
    rhs = charges.shape[0]
    blocks = total // BLOCK
    stack = 4 * feats + 16
    return pl.pallas_call(
        sort_kernel,
        out_shape=(
            jax.ShapeDtypeStruct((feats + rhs, total), F32),
            jax.ShapeDtypeStruct((stack, total), BF),
            jax.ShapeDtypeStruct((stack, total), BF),
        ),
        in_specs=[SMEM] + [VMEM] * 3,
        out_specs=(VMEM,) * 3,
        scratch_shapes=[
            pltpu.VMEM((blocks * feats, 2 * BLOCK), BF),
            pltpu.VMEM((blocks * rhs, BLOCK), BF),
        ],
        compiler_params=params(),
        cost_estimate=pl.CostEstimate(
            flops=6 * total * total * 16, bytes_accessed=4 * 10**6, transcendentals=0
        ),
        name="sort_points",
    )(inv_scale, points, charges, order)


def skeleton_kernel(
    sorted_ref, skel_ref, map_ref, interp_ref, list_ref, count_ref, far_ref,
    pack_ref, first_ref, rest_ref, node_ref, near_code_ref, far_code_ref, *, feats
):
    leaves, rank = skel_ref.shape
    rows, total = sorted_ref.shape
    width = total // leaves
    group_q = jnp.zeros((rows - feats, rank), F32)
    for leaf in range(leaves):
        span = slice(leaf * width, (leaf + 1) * width)
        out = slice(total + leaf * rank, total + (leaf + 1) * rank)
        columns = [
            sorted_ref[:feats, leaf * width + k : leaf * width + k + LANES]
            for k in range(0, width, LANES)
        ]
        pack_ref[:feats, out] = pick_lanes(columns, skel_ref[leaf : leaf + 1, :])
        charge = dot_t(sorted_ref[feats:, span].astype(BF), interp_ref[:, span]).astype(BF)
        pack_ref[feats:, out] = charge.astype(F32)
        group_q += dot(charge, map_ref[leaf * rank : (leaf + 1) * rank, :])
        pack_ref[:, span] = sorted_ref[:, span]
    columns = [pack_ref[:feats, total + k : total + k + LANES] for k in range(0, leaves * rank, LANES)]
    node_ref[:feats, :] = pick_lanes(
        columns, lax.broadcasted_iota(jnp.int32, (1, rank), 1) * leaves
    )
    node_ref[feats:, :] = group_q
    pack_ref[:, total + leaves * rank :] = node_ref[...]
    early = total - rest_ref.shape[1]
    first_ref[:, :early] = sorted_ref[:, :early]
    first_ref[:, early:] = pack_ref[:, total : total + leaves * rank]
    rest_ref[...] = sorted_ref[:, early:]
    used = lax.broadcasted_iota(jnp.int32, list_ref.shape, 0) < count_ref[...]
    near_code_ref[...] = jnp.where(used, code_of(list_ref[...], leaves), -1)
    far_code_ref[...] = code_of(far_ref[...], leaves)


def skeletons(points, skel_idx, group_map, interp, near_list, near_count, far_list, feats, early):
    rows, total = points.shape
    leaves, rank = skel_idx.shape
    skels = leaves * rank
    return pl.pallas_call(
        functools.partial(skeleton_kernel, feats=feats),
        out_shape=(
            jax.ShapeDtypeStruct((rows, total + skels + rank), F32),
            jax.ShapeDtypeStruct((rows, early + skels), F32),
            jax.ShapeDtypeStruct((rows, total - early), F32),
            jax.ShapeDtypeStruct((rows, rank), F32),
            jax.ShapeDtypeStruct(near_list.shape, jnp.int32),
            jax.ShapeDtypeStruct(far_list.shape, jnp.int32),
        ),
        in_specs=[VMEM] * 7,
        out_specs=(VMEM,) * 6,
        compiler_params=params(),
        name="skeletons",
    )(points, skel_idx, group_map, interp, near_list, near_count, far_list)


def code_of(leaf_id, leaves):
    device = lax.axis_index("leaf")
    rel = leaf_id - (device - 1) * leaves
    side = (rel >= leaves).astype(jnp.int32) + (rel >= 2 * leaves).astype(jnp.int32)
    chip = 2 * (1 - (device & 1))
    region = jnp.where(side == 1, 0, jnp.where(side == chip, 1, 2))
    return rel + (region - side) * leaves


def near_kernel(code_ref, target_ref, *refs, feats, parts, first):
    refs = list(refs)
    acc_ref = None if first else refs.pop(0)
    sources = [[refs.pop(0) for _ in range(1 + ready)] for _, _, ready in parts]
    out_ref, stack_ref = refs
    out_ref[...] = jnp.zeros_like(out_ref) if first else acc_ref[...]
    slots, leaves = code_ref.shape
    width = target_ref.shape[1] // leaves

    def add(leaf, place, refs):
        start = pl.multiple_of(leaf * width, width)
        at = pl.multiple_of(place * width, width)
        if len(refs) == 2:
            source = refs[1][:, pl.ds(at, width)]
        else:
            stack_ref[...] = stacked_rows(refs[0][:feats, pl.ds(at, width)])[0]
            source = stack_ref[...]
        charge = refs[0][feats:, pl.ds(at, width)].astype(BF)
        tile = tile_of(source, target_ref[:, pl.ds(start, width)])
        out_ref[:, pl.ds(start, width)] += dot(charge, tile)

    def per_leaf(leaf, carry):
        def per_slot(slot, carry):
            code = code_ref[slot, leaf]
            for (low, high, _), refs in zip(parts, sources):

                @pl.when((code >= low) & (code < high))
                def _():
                    add(leaf, code - low, refs)

            return carry

        return lax.fori_loop(0, slots, per_slot, carry)

    lax.fori_loop(0, leaves, per_leaf, 0)


def near_part(codes, targets, acc, parts, feats, tiles):
    slots, leaves = codes.shape
    rhs = parts[0][2].shape[0] - feats
    total = targets.shape[1]
    width = total // leaves
    operands = [] if acc is None else [acc]
    for _, _, pack, stack in parts:
        operands += [pack] if stack is None else [pack, stack]
    return pl.pallas_call(
        functools.partial(
            near_kernel,
            feats=feats,
            parts=[(low, high, stack is not None) for low, high, _, stack in parts],
            first=acc is None,
        ),
        out_shape=jax.ShapeDtypeStruct((rhs, total), F32),
        in_specs=[SMEM] + [VMEM] * (1 + len(operands)),
        out_specs=VMEM,
        scratch_shapes=[pltpu.VMEM((targets.shape[0], width), BF)],
        compiler_params=params(),
        cost_estimate=pl.CostEstimate(
            flops=tiles * width * width * 1024,
            bytes_accessed=tiles * 48 * width * 4,
            transcendentals=tiles * width * width,
        ),
        name=f"near_{parts[0][0]}",
    )(codes, targets, *operands)


def climb(nodes, base, levels, parent_map, feats, top=False):
    device = lax.axis_index("leaf")
    rank = nodes[0].shape[1]
    lane = lax.broadcasted_iota(jnp.int32, (1, rank), 1)
    inters = []
    for level in range(levels):
        own, other = nodes[0], nodes[1]
        source, _ = stacked_rows(other[:feats])
        _, target = stacked_rows(own[:feats])
        inters.append(dot(other[feats:].astype(BF), tile_of(source, target)))
        if top and level == levels - 1:
            break
        odd = (device >> (base + level)) & 1
        parents = []
        for k in range(0, len(nodes), 2):
            left = jnp.where(odd == 1, nodes[k + 1], nodes[k])
            right = jnp.where(odd == 1, nodes[k], nodes[k + 1])
            z = pick_lanes([left[:feats], right[:feats]], lane * 2)
            q = dot(left[feats:].astype(BF), parent_map[:rank, :])
            q += dot(right[feats:].astype(BF), parent_map[rank:, :])
            parents.append(jnp.concatenate([z, q], 0))
        nodes = parents
    return inters, nodes[0]


def climb_kernel(*refs, base, levels, feats):
    count = 2**levels
    rank = refs[count].shape[1]
    nodes = [ref[:, ref.shape[1] - rank :] for ref in refs[:count]]
    inters, node = climb(nodes, base, levels, refs[count][...], feats)
    for ref, value in zip(refs[count + 1 :], inters + [node]):
        ref[...] = value


def climb_stage(nodes, base, levels, parent_map, feats):
    rows, rank = nodes[0].shape[0], parent_map.shape[1]
    small = jax.ShapeDtypeStruct((rows - feats, rank), F32)
    outs = pl.pallas_call(
        functools.partial(climb_kernel, base=base, levels=levels, feats=feats),
        out_shape=(small,) * levels + (jax.ShapeDtypeStruct((rows, rank), F32),),
        in_specs=[VMEM] * (len(nodes) + 1),
        out_specs=(VMEM,) * (levels + 1),
        compiler_params=params(),
        name=f"climb_{base}",
    )(*nodes, parent_map)
    return list(outs[:-1]), outs[-1]


def finish_kernel(
    far_ref, near_ref, own_ref, chip_ref, beyond_ref, interp_ref, order_ref, map_ref, parent_ref,
    *refs, feats, base, levels, done,
):
    count = 2**levels
    nodes = [ref[...] for ref in refs[:count]]
    inters = [ref[...] for ref in refs[count : count + done]]
    out_ref, skel_ref, charge_ref, acc_ref = refs[count + done :]
    leaves, slots = far_ref.shape
    rank = interp_ref.shape[0]
    rhs, total = near_ref.shape
    width = total // leaves
    device = lax.axis_index("leaf")
    parent_map = parent_ref[...]
    fresh, _ = climb(nodes, base, levels, parent_map, feats, top=True)
    inters = inters + fresh
    down = inters[-1]
    for level in range(len(inters) - 2, -1, -1):
        spread = dot_t(down.astype(BF), parent_map)
        odd = (device >> level) & 1
        down = inters[level] + jnp.where(odd == 1, spread[:, rank:], spread[:, :rank])
    leaf_out = dot_t(down.astype(BF), map_ref[...])

    targets = []
    for region, ref in enumerate((own_ref, chip_ref, beyond_ref)):
        first = ref.shape[1] - leaves * rank if region == 2 else total
        skels = slice(first, first + leaves * rank)
        source, target = stacked_rows(ref[:feats, skels])
        charge = ref[feats:, skels].astype(BF)
        for leaf in range(leaves):
            span = slice(leaf * rank, (leaf + 1) * rank)
            skel_ref[region * leaves + leaf] = source[:, span]
            charge_ref[region * leaves + leaf] = charge[:, span]
            if region == 0:
                targets.append(target[:, span])
    fields = []
    for leaf in range(leaves):
        field = leaf_out[:, leaf * rank : (leaf + 1) * rank]
        where = [far_ref[leaf, slot] for slot in range(slots)]
        sources = jnp.concatenate([skel_ref[w] for w in where], 1)
        charges = jnp.concatenate([charge_ref[w] for w in where], 1)
        field += dot_t(charges, tile_of(targets[leaf], sources))
        fields.append(field.astype(BF))
    pieces = []
    for leaf in range(leaves):
        span = slice(leaf * width, (leaf + 1) * width)
        pieces.append(near_ref[:, span] + dot(fields[leaf], interp_ref[:, span]))

    blocks = total // BLOCK
    shift = BLOCK.bit_length() - 1
    for leaf in range(leaves):
        index = order_ref[:, leaf * width : (leaf + 1) * width]
        hot = one_hot(index & (BLOCK - 1), BLOCK)
        high = jnp.broadcast_to(index >> shift, (rhs, width))
        rows = []
        for k in range(blocks):
            rows.append(jnp.where(high == k, pieces[leaf], 0.0).astype(BF))
        part = dot_t(jnp.concatenate(rows, 0), hot)
        acc_ref[...] = part if leaf == 0 else acc_ref[...] + part
    for k in range(blocks):
        out_ref[:, k * BLOCK : (k + 1) * BLOCK] = acc_ref[k * rhs : (k + 1) * rhs, :]


def finish(far_list, near, packs, interp, order, group_map, parent_map, nodes, inters, base, levels, feats):
    rhs, total = near.shape
    leaves = far_list.shape[0]
    rank = interp.shape[0]
    return pl.pallas_call(
        functools.partial(finish_kernel, feats=feats, base=base, levels=levels, done=len(inters)),
        out_shape=jax.ShapeDtypeStruct((rhs, total), F32),
        in_specs=[SMEM] + [VMEM] * (8 + len(nodes) + len(inters)),
        out_specs=VMEM,
        scratch_shapes=[
            pltpu.VMEM((3 * leaves, 4 * feats + 16, rank), BF),
            pltpu.VMEM((3 * leaves, rhs, rank), BF),
            pltpu.VMEM((total // BLOCK * rhs, BLOCK), F32),
        ],
        compiler_params=params(),
        name="finish",
    )(far_list, near, *packs, interp, order, group_map, parent_map, *nodes, *inters)


def body(
    points,
    charges,
    inv_scale,
    order,
    near_list,
    near_count,
    far_list,
    skel_idx,
    interp,
    group_map,
    parent_map,
):
    feats = points.shape[0]
    leaves = near_list.shape[0]
    devices = lax.axis_size("leaf")
    order = local_index(order.reshape(1, -1))
    chip = [(i, i ^ 1) for i in range(devices)]
    beyond = []
    for i in range(1, devices - 1, 2):
        beyond += [(i, i + 1), (i + 1, i)]

    def send(value, mask):
        return lax.ppermute(value, "leaf", [(i, i ^ mask) for i in range(devices)])

    width = points.shape[1] // leaves
    early = leaves // 2
    placed, sources, targets = sort_points(inv_scale, points, charges, order)
    pack, first, rest, node, near_codes, far_codes = skeletons(
        placed,
        skel_idx,
        group_map,
        interp,
        near_list.T,
        near_count.reshape(1, -1),
        far_list,
        feats,
        early * width,
    )
    levels = devices.bit_length() - 1
    stages = [(base, min(2, levels - base)) for base in range(0, levels, 2)]
    pack_chip = send(pack, 1)
    nodes = [node, pack_chip] + [send(node, mask) for mask in range(2, 2 ** stages[0][1])]
    first = lax.ppermute(first, "leaf", beyond)
    rest = lax.ppermute(rest, "leaf", beyond)
    inters = []
    for stage, (base, count) in zip(stages[:-1], stages[1:]):
        fresh, node = climb_stage(nodes, *stage, parent_map, feats)
        inters += fresh
        nodes = [node] + [send(node, mask << base) for mask in range(1, 2**count)]
    parts = [(0, leaves, pack, sources), (leaves, 2 * leaves, pack_chip, None)]
    cut = 2 * leaves + early
    total = near_part(near_codes, targets, None, parts, feats, 2 * leaves)
    total = near_part(near_codes, targets, total, [(cut, 3 * leaves, rest, None)], feats, leaves // 2)
    total = near_part(near_codes, targets, total, [(2 * leaves, cut, first, None)], feats, leaves // 2)
    packs = (pack, pack_chip, first)
    return finish(
        far_codes, total, packs, interp, order, group_map, parent_map, nodes, inters, *stages[-1], feats
    )


def solution(mesh):
    placed = (
        P(None, ("fleet", "leaf")),
        P(None, ("fleet", "leaf")),
        P("fleet"),
        P(("fleet", "leaf")),
        P(("fleet", "leaf"), None),
        P(("fleet", "leaf")),
        P(("fleet", "leaf"), None),
        P(("fleet", "leaf"), None),
        P(None, ("fleet", "leaf")),
        P(("fleet", "leaf"), None),
        P("fleet", None),
    )
    return jax.shard_map(
        body, mesh=mesh, in_specs=placed, out_specs=P(None, ("fleet", "leaf")), check_vma=False
    )
```

```python
import functools
import math

import jax
import jax.numpy as jnp
from jax import lax
from jax.experimental import pallas as pl
from jax.experimental.pallas import tpu as pltpu
from jax.sharding import PartitionSpec as P

BF = jnp.bfloat16
F32 = jnp.float32
LANES = 128
BLOCK = 256
CHUNK = 512
VMEM = pl.BlockSpec(memory_space=pltpu.VMEM)
SMEM = pl.BlockSpec(memory_space=pltpu.SMEM)


def params():
    return pltpu.CompilerParams(vmem_limit_bytes=48 * 2**20)


def halves(z):
    hi = z.astype(BF)
    return hi, (z - hi.astype(F32)).astype(BF)


def stacked_rows(z):
    hi, mid = halves(z)
    norm = -0.5 * jnp.sum(z * z, 0, keepdims=True)
    n1 = norm.astype(BF).astype(F32)
    n2 = (norm - n1).astype(BF).astype(F32)
    n3 = norm - n1 - n2
    shape = (16, z.shape[1])
    row = lax.broadcasted_iota(jnp.int32, shape, 0)

    def extra(first):
        out = jnp.where((row >= 3 - first) & (row < 6 - first), 1.0, 0.0)
        for i, piece in enumerate((n1, n2, n3)):
            out = jnp.where(row == first + i, jnp.broadcast_to(piece, shape), out)
        return out.astype(BF)

    source = jnp.concatenate([hi, mid, hi, mid, extra(3)], 0)
    target = jnp.concatenate([hi, hi, mid, mid, extra(0)], 0)
    return source, target


def tile_of(source, target):
    e = lax.dot_general(source, target, (((0,), (0,)), ((), ())), preferred_element_type=F32)
    return jnp.exp2(e).astype(BF)


def dot_t(a, b):
    return lax.dot_general(a, b, (((1,), (1,)), ((), ())), preferred_element_type=F32)


def dot(a, b):
    return jnp.dot(a, b, preferred_element_type=F32)


def one_hot(low, size):
    rows = lax.broadcasted_iota(jnp.int32, (size, low.shape[1]), 0)
    return (rows == low).astype(F32).astype(BF)


def pick_lanes(blocks, index):
    rows = blocks[0].shape[0]
    parts = []
    for top in range(0, rows, 8):
        idx = jnp.broadcast_to(index, (8, LANES))
        high, low = idx >> 7, idx & (LANES - 1)
        out = jnp.zeros((8, LANES), F32)
        for k, block in enumerate(blocks):
            got = jnp.take_along_axis(block[top : top + 8], low, axis=1, mode="promise_in_bounds")
            out = jnp.where(high == k, got, out)
        parts.append(out)
    return jnp.concatenate(parts, 0)


def base_kernel(out_ref, *, total):
    out_ref[...] = jnp.full(out_ref.shape, lax.axis_index("leaf") * total, jnp.int32)


def first_point(total):
    return pl.pallas_call(
        functools.partial(base_kernel, total=total),
        out_shape=jax.ShapeDtypeStruct((1, LANES), jnp.int32),
        out_specs=VMEM,
        compiler_params=params(),
        cost_estimate=pl.CostEstimate(flops=10**9, bytes_accessed=10**6, transcendentals=0),
        name="first_point",
    )()


def sort_kernel(
    scale_ref, points_ref, charges_ref, order_ref, base_ref,
    pack_ref, source_ref, target_ref, zs_ref, bs_ref,
):
    feats, total = points_ref.shape
    rhs = charges_ref.shape[0]
    base = base_ref[:, :1]
    blocks = total // BLOCK
    shift = BLOCK.bit_length() - 1
    row = lax.broadcasted_iota(jnp.int32, (feats, LANES), 0)
    scale = jnp.zeros((feats, LANES), F32)
    for r in range(feats):
        scale = jnp.where(row == r, scale_ref[r], scale)
    scale = scale[:, :1] * math.sqrt(math.log2(math.e))
    for k in range(blocks):
        span = slice(k * BLOCK, (k + 1) * BLOCK)
        hi, mid = halves(points_ref[:, span] * scale)
        zs_ref[k * feats : (k + 1) * feats, :BLOCK] = hi
        zs_ref[k * feats : (k + 1) * feats, BLOCK:] = mid
        bs_ref[k * rhs : (k + 1) * rhs, :] = charges_ref[:, span].astype(BF)

    def step(j, carry):
        start = pl.multiple_of(j * CHUNK, CHUNK)
        index = order_ref[:, pl.ds(start, CHUNK)] - base
        hot = one_hot(index & (BLOCK - 1), BLOCK)
        yz = dot(zs_ref[...], jnp.concatenate([hot, hot], 0))
        yb = dot(bs_ref[...], hot)
        high = jnp.broadcast_to(index >> shift, (feats, CHUNK))
        az = jnp.zeros((feats, CHUNK), F32)
        ab = jnp.zeros((rhs, CHUNK), F32)
        for k in range(blocks):
            mask = high == k
            az = jnp.where(mask, yz[k * feats : (k + 1) * feats], az)
            ab = jnp.where(mask, yb[k * rhs : (k + 1) * rhs], ab)
        pack_ref[:feats, pl.ds(start, CHUNK)] = az
        pack_ref[feats:, pl.ds(start, CHUNK)] = ab
        source, target = stacked_rows(az)
        source_ref[:, pl.ds(start, CHUNK)] = source
        target_ref[:, pl.ds(start, CHUNK)] = target
        return carry

    lax.fori_loop(0, total // CHUNK, step, 0, unroll=True)


def sort_points(inv_scale, points, charges, order, base):
    feats, total = points.shape
    rhs = charges.shape[0]
    blocks = total // BLOCK
    stack = 4 * feats + 16
    return pl.pallas_call(
        sort_kernel,
        out_shape=(
            jax.ShapeDtypeStruct((feats + rhs, total), F32),
            jax.ShapeDtypeStruct((stack, total), BF),
            jax.ShapeDtypeStruct((stack, total), BF),
        ),
        in_specs=[SMEM] + [VMEM] * 4,
        out_specs=(VMEM,) * 3,
        scratch_shapes=[
            pltpu.VMEM((blocks * feats, 2 * BLOCK), BF),
            pltpu.VMEM((blocks * rhs, BLOCK), BF),
        ],
        compiler_params=params(),
        cost_estimate=pl.CostEstimate(
            flops=6 * total * total * 16, bytes_accessed=4 * 10**6, transcendentals=0
        ),
        name="sort_points",
    )(inv_scale, points, charges, order, base)


def skeleton_kernel(
    sorted_ref, skel_ref, map_ref, interp_ref, list_ref, count_ref, far_ref,
    pack_ref, first_ref, rest_ref, node_ref, near_code_ref, far_code_ref, *, feats
):
    leaves, rank = skel_ref.shape
    rows, total = sorted_ref.shape
    width = total // leaves
    group_q = jnp.zeros((rows - feats, rank), F32)
    for leaf in range(leaves):
        span = slice(leaf * width, (leaf + 1) * width)
        out = slice(total + leaf * rank, total + (leaf + 1) * rank)
        columns = [
            sorted_ref[:feats, leaf * width + k : leaf * width + k + LANES]
            for k in range(0, width, LANES)
        ]
        pack_ref[:feats, out] = pick_lanes(columns, skel_ref[leaf : leaf + 1, :])
        charge = dot_t(sorted_ref[feats:, span].astype(BF), interp_ref[:, span]).astype(BF)
        pack_ref[feats:, out] = charge.astype(F32)
        group_q += dot(charge, map_ref[leaf * rank : (leaf + 1) * rank, :])
        pack_ref[:, span] = sorted_ref[:, span]
    columns = [pack_ref[:feats, total + k : total + k + LANES] for k in range(0, leaves * rank, LANES)]
    node_ref[:feats, :] = pick_lanes(
        columns, lax.broadcasted_iota(jnp.int32, (1, rank), 1) * leaves
    )
    node_ref[feats:, :] = group_q
    pack_ref[:, total + leaves * rank :] = node_ref[...]
    early = total - rest_ref.shape[1]
    first_ref[:, :early] = sorted_ref[:, :early]
    first_ref[:, early:] = pack_ref[:, total : total + leaves * rank]
    rest_ref[...] = sorted_ref[:, early:]
    used = lax.broadcasted_iota(jnp.int32, list_ref.shape, 0) < count_ref[...]
    near_code_ref[...] = jnp.where(used, code_of(list_ref[...], leaves), -1)
    far_code_ref[...] = code_of(far_ref[...], leaves)


def skeletons(points, skel_idx, group_map, interp, near_list, near_count, far_list, feats, early):
    rows, total = points.shape
    leaves, rank = skel_idx.shape
    skels = leaves * rank
    return pl.pallas_call(
        functools.partial(skeleton_kernel, feats=feats),
        out_shape=(
            jax.ShapeDtypeStruct((rows, total + skels + rank), F32),
            jax.ShapeDtypeStruct((rows, early + skels), F32),
            jax.ShapeDtypeStruct((rows, total - early), F32),
            jax.ShapeDtypeStruct((rows, rank), F32),
            jax.ShapeDtypeStruct(near_list.shape, jnp.int32),
            jax.ShapeDtypeStruct(far_list.shape, jnp.int32),
        ),
        in_specs=[VMEM] * 7,
        out_specs=(VMEM,) * 6,
        compiler_params=params(),
        name="skeletons",
    )(points, skel_idx, group_map, interp, near_list, near_count, far_list)


def code_of(leaf_id, leaves):
    device = lax.axis_index("leaf")
    rel = leaf_id - (device - 1) * leaves
    side = (rel >= leaves).astype(jnp.int32) + (rel >= 2 * leaves).astype(jnp.int32)
    chip = 2 * (1 - (device & 1))
    region = jnp.where(side == 1, 0, jnp.where(side == chip, 1, 2))
    return rel + (region - side) * leaves


def near_kernel(code_ref, target_ref, *refs, feats, parts, first):
    refs = list(refs)
    acc_ref = None if first else refs.pop(0)
    sources = [[refs.pop(0) for _ in range(1 + ready)] for _, _, ready in parts]
    out_ref, stack_ref = refs
    out_ref[...] = jnp.zeros_like(out_ref) if first else acc_ref[...]
    slots, leaves = code_ref.shape
    width = target_ref.shape[1] // leaves

    def add(leaf, place, refs):
        start = pl.multiple_of(leaf * width, width)
        at = pl.multiple_of(place * width, width)
        if len(refs) == 2:
            source = refs[1][:, pl.ds(at, width)]
        else:
            stack_ref[...] = stacked_rows(refs[0][:feats, pl.ds(at, width)])[0]
            source = stack_ref[...]
        charge = refs[0][feats:, pl.ds(at, width)].astype(BF)
        tile = tile_of(source, target_ref[:, pl.ds(start, width)])
        out_ref[:, pl.ds(start, width)] += dot(charge, tile)

    def per_leaf(leaf, carry):
        def per_slot(slot, carry):
            code = code_ref[slot, leaf]
            for (low, high, _), refs in zip(parts, sources):

                @pl.when((code >= low) & (code < high))
                def _():
                    add(leaf, code - low, refs)

            return carry

        return lax.fori_loop(0, slots, per_slot, carry)

    lax.fori_loop(0, leaves, per_leaf, 0)


def near_part(codes, targets, acc, parts, feats, tiles):
    slots, leaves = codes.shape
    rhs = parts[0][2].shape[0] - feats
    total = targets.shape[1]
    width = total // leaves
    operands = [] if acc is None else [acc]
    for _, _, pack, stack in parts:
        operands += [pack] if stack is None else [pack, stack]
    return pl.pallas_call(
        functools.partial(
            near_kernel,
            feats=feats,
            parts=[(low, high, stack is not None) for low, high, _, stack in parts],
            first=acc is None,
        ),
        out_shape=jax.ShapeDtypeStruct((rhs, total), F32),
        in_specs=[SMEM] + [VMEM] * (1 + len(operands)),
        out_specs=VMEM,
        scratch_shapes=[pltpu.VMEM((targets.shape[0], width), BF)],
        compiler_params=params(),
        cost_estimate=pl.CostEstimate(
            flops=tiles * width * width * 1024,
            bytes_accessed=tiles * 48 * width * 4,
            transcendentals=tiles * width * width,
        ),
        name=f"near_{parts[0][0]}",
    )(codes, targets, *operands)


def climb(nodes, base, levels, parent_map, feats, top=False):
    device = lax.axis_index("leaf")
    rank = nodes[0].shape[1]
    lane = lax.broadcasted_iota(jnp.int32, (1, rank), 1)
    inters = []
    for level in range(levels):
        own, other = nodes[0], nodes[1]
        source, _ = stacked_rows(other[:feats])
        _, target = stacked_rows(own[:feats])
        inters.append(dot(other[feats:].astype(BF), tile_of(source, target)))
        if top and level == levels - 1:
            break
        odd = (device >> (base + level)) & 1
        parents = []
        for k in range(0, len(nodes), 2):
            left = jnp.where(odd == 1, nodes[k + 1], nodes[k])
            right = jnp.where(odd == 1, nodes[k], nodes[k + 1])
            z = pick_lanes([left[:feats], right[:feats]], lane * 2)
            q = dot(left[feats:].astype(BF), parent_map[:rank, :])
            q += dot(right[feats:].astype(BF), parent_map[rank:, :])
            parents.append(jnp.concatenate([z, q], 0))
        nodes = parents
    return inters, nodes[0]


def climb_kernel(*refs, base, levels, feats):
    count = 2**levels
    rank = refs[count].shape[1]
    nodes = [ref[:, ref.shape[1] - rank :] for ref in refs[:count]]
    inters, node = climb(nodes, base, levels, refs[count][...], feats)
    for ref, value in zip(refs[count + 1 :], inters + [node]):
        ref[...] = value


def climb_stage(nodes, base, levels, parent_map, feats):
    rows, rank = nodes[0].shape[0], parent_map.shape[1]
    small = jax.ShapeDtypeStruct((rows - feats, rank), F32)
    outs = pl.pallas_call(
        functools.partial(climb_kernel, base=base, levels=levels, feats=feats),
        out_shape=(small,) * levels + (jax.ShapeDtypeStruct((rows, rank), F32),),
        in_specs=[VMEM] * (len(nodes) + 1),
        out_specs=(VMEM,) * (levels + 1),
        compiler_params=params(),
        name=f"climb_{base}",
    )(*nodes, parent_map)
    return list(outs[:-1]), outs[-1]


def finish_kernel(
    far_ref, near_ref, own_ref, chip_ref, beyond_ref, interp_ref, order_ref, map_ref, parent_ref,
    *refs, feats, base, levels, done,
):
    count = 2**levels
    nodes = [ref[...] for ref in refs[:count]]
    inters = [ref[...] for ref in refs[count : count + done]]
    out_ref, skel_ref, charge_ref, acc_ref = refs[count + done :]
    leaves, slots = far_ref.shape
    rank = interp_ref.shape[0]
    rhs, total = near_ref.shape
    width = total // leaves
    device = lax.axis_index("leaf")
    parent_map = parent_ref[...]
    fresh, _ = climb(nodes, base, levels, parent_map, feats, top=True)
    inters = inters + fresh
    down = inters[-1]
    for level in range(len(inters) - 2, -1, -1):
        spread = dot_t(down.astype(BF), parent_map)
        odd = (device >> level) & 1
        down = inters[level] + jnp.where(odd == 1, spread[:, rank:], spread[:, :rank])
    leaf_out = dot_t(down.astype(BF), map_ref[...])

    targets = []
    for region, ref in enumerate((own_ref, chip_ref, beyond_ref)):
        first = ref.shape[1] - leaves * rank if region == 2 else total
        skels = slice(first, first + leaves * rank)
        source, target = stacked_rows(ref[:feats, skels])
        charge = ref[feats:, skels].astype(BF)
        for leaf in range(leaves):
            span = slice(leaf * rank, (leaf + 1) * rank)
            skel_ref[region * leaves + leaf] = source[:, span]
            charge_ref[region * leaves + leaf] = charge[:, span]
            if region == 0:
                targets.append(target[:, span])
    fields = []
    for leaf in range(leaves):
        field = leaf_out[:, leaf * rank : (leaf + 1) * rank]
        where = [far_ref[leaf, slot] for slot in range(slots)]
        sources = jnp.concatenate([skel_ref[w] for w in where], 1)
        charges = jnp.concatenate([charge_ref[w] for w in where], 1)
        field += dot_t(charges, tile_of(targets[leaf], sources))
        fields.append(field.astype(BF))
    pieces = []
    for leaf in range(leaves):
        span = slice(leaf * width, (leaf + 1) * width)
        pieces.append(near_ref[:, span] + dot(fields[leaf], interp_ref[:, span]))

    blocks = total // BLOCK
    shift = BLOCK.bit_length() - 1
    for leaf in range(leaves):
        index = order_ref[:, leaf * width : (leaf + 1) * width] - device * total
        hot = one_hot(index & (BLOCK - 1), BLOCK)
        high = jnp.broadcast_to(index >> shift, (rhs, width))
        rows = []
        for k in range(blocks):
            rows.append(jnp.where(high == k, pieces[leaf], 0.0).astype(BF))
        part = dot_t(jnp.concatenate(rows, 0), hot)
        acc_ref[...] = part if leaf == 0 else acc_ref[...] + part
    for k in range(blocks):
        out_ref[:, k * BLOCK : (k + 1) * BLOCK] = acc_ref[k * rhs : (k + 1) * rhs, :]


def finish(far_list, near, packs, interp, order, group_map, parent_map, nodes, inters, base, levels, feats):
    rhs, total = near.shape
    leaves = far_list.shape[0]
    rank = interp.shape[0]
    return pl.pallas_call(
        functools.partial(finish_kernel, feats=feats, base=base, levels=levels, done=len(inters)),
        out_shape=jax.ShapeDtypeStruct((rhs, total), F32),
        in_specs=[SMEM] + [VMEM] * (8 + len(nodes) + len(inters)),
        out_specs=VMEM,
        scratch_shapes=[
            pltpu.VMEM((3 * leaves, 4 * feats + 16, rank), BF),
            pltpu.VMEM((3 * leaves, rhs, rank), BF),
            pltpu.VMEM((total // BLOCK * rhs, BLOCK), F32),
        ],
        compiler_params=params(),
        name="finish",
    )(far_list, near, *packs, interp, order, group_map, parent_map, *nodes, *inters)


def body(
    points,
    charges,
    inv_scale,
    order,
    near_list,
    near_count,
    far_list,
    skel_idx,
    interp,
    group_map,
    parent_map,
):
    feats = points.shape[0]
    leaves = near_list.shape[0]
    devices = lax.axis_size("leaf")
    order = order.reshape(1, -1)
    base = first_point(points.shape[1])
    chip = [(i, i ^ 1) for i in range(devices)]
    beyond = []
    for i in range(1, devices, 2):
        beyond += [(i, (i + 1) % devices), ((i + 1) % devices, i)]

    def send(value, mask):
        return lax.ppermute(value, "leaf", [(i, i ^ mask) for i in range(devices)])

    width = points.shape[1] // leaves
    early = leaves // 2
    placed, sources, targets = sort_points(inv_scale, points, charges, order, base)
    pack, first, rest, node, near_codes, far_codes = skeletons(
        placed,
        skel_idx,
        group_map,
        interp,
        near_list.T,
        near_count.reshape(1, -1),
        far_list,
        feats,
        early * width,
    )
    levels = devices.bit_length() - 1
    stages = [(base, min(2, levels - base)) for base in range(0, levels, 2)]
    pack_chip = send(pack, 1)
    nodes = [node, pack_chip] + [send(node, mask) for mask in range(2, 2 ** stages[0][1])]
    first = lax.ppermute(first, "leaf", beyond)
    rest = lax.ppermute(rest, "leaf", beyond)
    inters = []
    for stage, (base, count) in zip(stages[:-1], stages[1:]):
        fresh, node = climb_stage(nodes, *stage, parent_map, feats)
        inters += fresh
        nodes = [node] + [send(node, mask << base) for mask in range(1, 2**count)]
    parts = [(0, leaves, pack, sources), (leaves, 2 * leaves, pack_chip, None)]
    cut = 2 * leaves + early
    total = near_part(near_codes, targets, None, parts, feats, 2 * leaves)
    total = near_part(near_codes, targets, total, [(cut, 3 * leaves, rest, None)], feats, leaves // 2)
    total = near_part(near_codes, targets, total, [(2 * leaves, cut, first, None)], feats, leaves // 2)
    packs = (pack, pack_chip, first)
    return finish(
        far_codes, total, packs, interp, order, group_map, parent_map, nodes, inters, *stages[-1], feats
    )


def solution(mesh):
    placed = (
        P(None, ("fleet", "leaf")),
        P(None, ("fleet", "leaf")),
        P("fleet"),
        P(("fleet", "leaf")),
        P(("fleet", "leaf"), None),
        P(("fleet", "leaf")),
        P(("fleet", "leaf"), None),
        P(("fleet", "leaf"), None),
        P(None, ("fleet", "leaf")),
        P(("fleet", "leaf"), None),
        P("fleet", None),
    )
    return jax.shard_map(
        body, mesh=mesh, in_specs=placed, out_specs=P(None, ("fleet", "leaf")), check_vma=False
    )
```

```python
import functools
import math

import jax
import jax.numpy as jnp
from jax import lax
from jax.experimental import pallas as pl
from jax.experimental.pallas import tpu as pltpu
from jax.sharding import PartitionSpec as P

BF = jnp.bfloat16
F32 = jnp.float32
LANES = 128
BLOCK = 256
CHUNK = 512
VMEM = pl.BlockSpec(memory_space=pltpu.VMEM)
SMEM = pl.BlockSpec(memory_space=pltpu.SMEM)


def params():
    return pltpu.CompilerParams(vmem_limit_bytes=48 * 2**20)


def halves(z):
    hi = z.astype(BF)
    return hi, (z - hi.astype(F32)).astype(BF)


def stacked_rows(z):
    hi, mid = halves(z)
    norm = -0.5 * jnp.sum(z * z, 0, keepdims=True)
    n1 = norm.astype(BF).astype(F32)
    n2 = (norm - n1).astype(BF).astype(F32)
    n3 = norm - n1 - n2
    shape = (16, z.shape[1])
    row = lax.broadcasted_iota(jnp.int32, shape, 0)

    def extra(first):
        out = jnp.where((row >= 3 - first) & (row < 6 - first), 1.0, 0.0)
        for i, piece in enumerate((n1, n2, n3)):
            out = jnp.where(row == first + i, jnp.broadcast_to(piece, shape), out)
        return out.astype(BF)

    source = jnp.concatenate([hi, mid, hi, mid, extra(3)], 0)
    target = jnp.concatenate([hi, hi, mid, mid, extra(0)], 0)
    return source, target


def tile_of(source, target):
    e = lax.dot_general(source, target, (((0,), (0,)), ((), ())), preferred_element_type=F32)
    return jnp.exp2(e).astype(BF)


def dot_t(a, b):
    return lax.dot_general(a, b, (((1,), (1,)), ((), ())), preferred_element_type=F32)


def dot(a, b):
    return jnp.dot(a, b, preferred_element_type=F32)


def one_hot(low, size):
    rows = lax.broadcasted_iota(jnp.int32, (size, low.shape[1]), 0)
    return (rows == low).astype(F32).astype(BF)


def pick_lanes(blocks, index):
    rows = blocks[0].shape[0]
    parts = []
    for top in range(0, rows, 8):
        idx = jnp.broadcast_to(index, (8, LANES))
        high, low = idx >> 7, idx & (LANES - 1)
        out = jnp.zeros((8, LANES), F32)
        for k, block in enumerate(blocks):
            got = jnp.take_along_axis(block[top : top + 8], low, axis=1, mode="promise_in_bounds")
            out = jnp.where(high == k, got, out)
        parts.append(out)
    return jnp.concatenate(parts, 0)


def base_kernel(out_ref, *, total):
    out_ref[...] = jnp.full(out_ref.shape, lax.axis_index("leaf") * total, jnp.int32)


def first_point(total):
    return pl.pallas_call(
        functools.partial(base_kernel, total=total),
        out_shape=jax.ShapeDtypeStruct((1, LANES), jnp.int32),
        out_specs=VMEM,
        compiler_params=params(),
        cost_estimate=pl.CostEstimate(flops=10**9, bytes_accessed=10**6, transcendentals=0),
        name="first_point",
    )()


def sort_kernel(
    scale_ref, points_ref, charges_ref, order_ref, base_ref,
    pack_ref, source_ref, target_ref, zs_ref, bs_ref,
):
    feats, total = points_ref.shape
    rhs = charges_ref.shape[0]
    width = source_ref.shape[2]
    base = base_ref[:, :1]
    blocks = total // BLOCK
    shift = BLOCK.bit_length() - 1
    row = lax.broadcasted_iota(jnp.int32, (feats, LANES), 0)
    scale = jnp.zeros((feats, LANES), F32)
    for r in range(feats):
        scale = jnp.where(row == r, scale_ref[r], scale)
    scale = scale[:, :1] * math.sqrt(math.log2(math.e))
    for k in range(blocks):
        span = slice(k * BLOCK, (k + 1) * BLOCK)
        hi, mid = halves(points_ref[:, span] * scale)
        zs_ref[k * feats : (k + 1) * feats, :BLOCK] = hi
        zs_ref[k * feats : (k + 1) * feats, BLOCK:] = mid
        bs_ref[k * rhs : (k + 1) * rhs, :] = charges_ref[:, span].astype(BF)

    def step(j, carry):
        start = pl.multiple_of(j * CHUNK, CHUNK)
        index = order_ref[:, pl.ds(start, CHUNK)] - base
        hot = one_hot(index & (BLOCK - 1), BLOCK)
        yz = dot(zs_ref[...], jnp.concatenate([hot, hot], 0))
        yb = dot(bs_ref[...], hot)
        high = jnp.broadcast_to(index >> shift, (feats, CHUNK))
        az = jnp.zeros((feats, CHUNK), F32)
        ab = jnp.zeros((rhs, CHUNK), F32)
        for k in range(blocks):
            mask = high == k
            az = jnp.where(mask, yz[k * feats : (k + 1) * feats], az)
            ab = jnp.where(mask, yb[k * rhs : (k + 1) * rhs], ab)
        pack_ref[:feats, pl.ds(start, CHUNK)] = az
        pack_ref[feats:, pl.ds(start, CHUNK)] = ab
        source, target = stacked_rows(az)
        leaf, at = j * CHUNK // width, pl.multiple_of(j * CHUNK % width, CHUNK)
        source_ref[leaf, :, pl.ds(at, CHUNK)] = source
        target_ref[:, pl.ds(start, CHUNK)] = target
        return carry

    lax.fori_loop(0, total // CHUNK, step, 0, unroll=True)


def sort_points(inv_scale, points, charges, order, base, leaves):
    feats, total = points.shape
    rhs = charges.shape[0]
    blocks = total // BLOCK
    stack = 4 * feats + 16
    return pl.pallas_call(
        sort_kernel,
        out_shape=(
            jax.ShapeDtypeStruct((feats + rhs, total), F32),
            jax.ShapeDtypeStruct((leaves, stack, total // leaves), BF),
            jax.ShapeDtypeStruct((stack, total), BF),
        ),
        in_specs=[SMEM] + [VMEM] * 4,
        out_specs=(VMEM,) * 3,
        scratch_shapes=[
            pltpu.VMEM((blocks * feats, 2 * BLOCK), BF),
            pltpu.VMEM((blocks * rhs, BLOCK), BF),
        ],
        compiler_params=params(),
        cost_estimate=pl.CostEstimate(
            flops=6 * total * total * 16, bytes_accessed=4 * 10**6, transcendentals=0
        ),
        name="sort_points",
    )(inv_scale, points, charges, order, base)


def skeleton_kernel(
    sorted_ref, skel_ref, map_ref, interp_ref, list_ref, count_ref, far_ref,
    pack_ref, first_ref, rest_ref, node_ref, near_code_ref, far_code_ref, *, feats
):
    leaves, rank = skel_ref.shape
    rows, total = sorted_ref.shape
    width = total // leaves
    group_q = jnp.zeros((rows - feats, rank), F32)
    for leaf in range(leaves):
        span = slice(leaf * width, (leaf + 1) * width)
        out = slice(total + leaf * rank, total + (leaf + 1) * rank)
        columns = [
            sorted_ref[:feats, leaf * width + k : leaf * width + k + LANES]
            for k in range(0, width, LANES)
        ]
        pack_ref[:feats, out] = pick_lanes(columns, skel_ref[leaf : leaf + 1, :])
        charge = dot_t(sorted_ref[feats:, span].astype(BF), interp_ref[:, span]).astype(BF)
        pack_ref[feats:, out] = charge.astype(F32)
        group_q += dot(charge, map_ref[leaf * rank : (leaf + 1) * rank, :])
        pack_ref[:, span] = sorted_ref[:, span]
    columns = [pack_ref[:feats, total + k : total + k + LANES] for k in range(0, leaves * rank, LANES)]
    node_ref[:feats, :] = pick_lanes(
        columns, lax.broadcasted_iota(jnp.int32, (1, rank), 1) * leaves
    )
    node_ref[feats:, :] = group_q
    pack_ref[:, total + leaves * rank :] = node_ref[...]
    early = total - rest_ref.shape[1]
    first_ref[:, :early] = sorted_ref[:, :early]
    first_ref[:, early:] = pack_ref[:, total : total + leaves * rank]
    rest_ref[...] = sorted_ref[:, early:]
    used = lax.broadcasted_iota(jnp.int32, list_ref.shape, 0) < count_ref[...]
    near_code_ref[...] = jnp.where(used, code_of(list_ref[...], leaves), -1)
    far_code_ref[...] = code_of(far_ref[...], leaves)


def skeletons(points, skel_idx, group_map, interp, near_list, near_count, far_list, feats, early):
    rows, total = points.shape
    leaves, rank = skel_idx.shape
    skels = leaves * rank
    return pl.pallas_call(
        functools.partial(skeleton_kernel, feats=feats),
        out_shape=(
            jax.ShapeDtypeStruct((rows, total + skels + rank), F32),
            jax.ShapeDtypeStruct((rows, early + skels), F32),
            jax.ShapeDtypeStruct((rows, total - early), F32),
            jax.ShapeDtypeStruct((rows, rank), F32),
            jax.ShapeDtypeStruct(near_list.shape, jnp.int32),
            jax.ShapeDtypeStruct(far_list.shape, jnp.int32),
        ),
        in_specs=[VMEM] * 7,
        out_specs=(VMEM,) * 6,
        compiler_params=params(),
        name="skeletons",
    )(points, skel_idx, group_map, interp, near_list, near_count, far_list)


def code_of(leaf_id, leaves):
    device = lax.axis_index("leaf")
    rel = leaf_id - (device - 1) * leaves
    side = (rel >= leaves).astype(jnp.int32) + (rel >= 2 * leaves).astype(jnp.int32)
    chip = 2 * (1 - (device & 1))
    region = jnp.where(side == 1, 0, jnp.where(side == chip, 1, 2))
    return rel + (region - side) * leaves


def build_stacks(src_ref, stack_ref, feats):
    width = stack_ref.shape[2]
    for place in range(stack_ref.shape[0]):
        stack_ref[place] = stacked_rows(src_ref[:feats, place * width : (place + 1) * width])[0]


def add_tiles(code_ref, target_ref, out_ref, parts, feats):
    slots, leaves = code_ref.shape
    width = out_ref.shape[1] // leaves

    def add(leaf, place, src_ref, stack_ref):
        start = pl.multiple_of(leaf * width, width)
        at = pl.multiple_of(place * width, width)
        charge = src_ref[feats:, pl.ds(at, width)].astype(BF)
        tile = tile_of(stack_ref[place], target_ref[:, pl.ds(start, width)])
        out_ref[:, pl.ds(start, width)] += dot(charge, tile)

    def per_leaf(leaf, carry):
        def per_slot(slot, carry):
            code = code_ref[slot, leaf]
            for low, src_ref, stack_ref in parts:

                @pl.when((code >= low) & (code < low + stack_ref.shape[0]))
                def _():
                    add(leaf, code - low, src_ref, stack_ref)

            return carry

        return lax.fori_loop(0, slots, per_slot, carry)

    lax.fori_loop(0, leaves, per_leaf, 0)


def near_own_kernel(
    code_vmem, target_ref, own_ref, own_stack, chip_ref, out_ref, code_ref, chip_stack, sem, *, feats
):
    copy = pltpu.make_async_copy(code_vmem, code_ref, sem)
    copy.start()
    leaves = own_stack.shape[0]
    out_ref[...] = jnp.zeros_like(out_ref)
    build_stacks(chip_ref, chip_stack, feats)
    copy.wait()
    parts = [(0, own_ref, own_stack), (leaves, chip_ref, chip_stack)]
    add_tiles(code_ref, target_ref, out_ref, parts, feats)


def near_more_kernel(
    code_vmem, target_ref, acc_ref, src_ref, out_ref, code_ref, stack_ref, sem, *, feats, low
):
    copy = pltpu.make_async_copy(code_vmem, code_ref, sem)
    copy.start()
    out_ref[...] = acc_ref[...]
    build_stacks(src_ref, stack_ref, feats)
    copy.wait()
    add_tiles(code_ref, target_ref, out_ref, [(low, src_ref, stack_ref)], feats)


def near_part(kernel, codes, targets, operands, count, rhs, tiles, name):
    leaves = codes.shape[1]
    total = targets.shape[1]
    width = total // leaves
    return pl.pallas_call(
        kernel,
        out_shape=jax.ShapeDtypeStruct((rhs, total), F32),
        in_specs=[VMEM] * (2 + len(operands)),
        out_specs=VMEM,
        scratch_shapes=[
            pltpu.SMEM(codes.shape, jnp.int32),
            pltpu.VMEM((count, targets.shape[0], width), BF),
            pltpu.SemaphoreType.DMA,
        ],
        compiler_params=params(),
        cost_estimate=pl.CostEstimate(
            flops=tiles * width * width * 1024,
            bytes_accessed=tiles * 48 * width * 4,
            transcendentals=tiles * width * width,
        ),
        name=name,
    )(codes, targets, *operands)


def climb(nodes, base, levels, parent_map, feats, top=False):
    device = lax.axis_index("leaf")
    rank = nodes[0].shape[1]
    lane = lax.broadcasted_iota(jnp.int32, (1, rank), 1)
    inters = []
    for level in range(levels):
        own, other = nodes[0], nodes[1]
        source, _ = stacked_rows(other[:feats])
        _, target = stacked_rows(own[:feats])
        inters.append(dot(other[feats:].astype(BF), tile_of(source, target)))
        if top and level == levels - 1:
            break
        odd = (device >> (base + level)) & 1
        parents = []
        for k in range(0, len(nodes), 2):
            left = jnp.where(odd == 1, nodes[k + 1], nodes[k])
            right = jnp.where(odd == 1, nodes[k], nodes[k + 1])
            z = pick_lanes([left[:feats], right[:feats]], lane * 2)
            q = dot(left[feats:].astype(BF), parent_map[:rank, :])
            q += dot(right[feats:].astype(BF), parent_map[rank:, :])
            parents.append(jnp.concatenate([z, q], 0))
        nodes = parents
    return inters, nodes[0]


def climb_kernel(*refs, base, levels, feats):
    count = 2**levels
    rank = refs[count].shape[1]
    nodes = [ref[:, ref.shape[1] - rank :] for ref in refs[:count]]
    inters, node = climb(nodes, base, levels, refs[count][...], feats)
    for ref, value in zip(refs[count + 1 :], inters + [node]):
        ref[...] = value


def climb_stage(nodes, base, levels, parent_map, feats):
    rows, rank = nodes[0].shape[0], parent_map.shape[1]
    small = jax.ShapeDtypeStruct((rows - feats, rank), F32)
    outs = pl.pallas_call(
        functools.partial(climb_kernel, base=base, levels=levels, feats=feats),
        out_shape=(small,) * levels + (jax.ShapeDtypeStruct((rows, rank), F32),),
        in_specs=[VMEM] * (len(nodes) + 1),
        out_specs=(VMEM,) * (levels + 1),
        compiler_params=params(),
        name=f"climb_{base}",
    )(*nodes, parent_map)
    return list(outs[:-1]), outs[-1]


def finish_kernel(
    near_vmem, far_vmem, near_ref, target_ref, own_ref, chip_ref, beyond_ref, interp_ref, order_ref,
    map_ref, parent_ref, *refs, feats, base, levels, done, low,
):
    count = 2**levels
    nodes = [ref[...] for ref in refs[:count]]
    inters = [ref[...] for ref in refs[count : count + done]]
    out_ref, code_ref, far_ref, sum_ref, stack_ref, skel_ref, charge_ref, acc_ref, sems = refs[count + done :]
    copies = [
        pltpu.make_async_copy(near_vmem, code_ref, sems.at[0]),
        pltpu.make_async_copy(far_vmem, far_ref, sems.at[1]),
    ]
    for copy in copies:
        copy.start()
    leaves, slots = far_ref.shape
    rank = interp_ref.shape[0]
    rhs, total = near_ref.shape
    width = total // leaves
    device = lax.axis_index("leaf")
    parent_map = parent_ref[...]
    fresh, _ = climb(nodes, base, levels, parent_map, feats, top=True)
    inters = inters + fresh
    down = inters[-1]
    for level in range(len(inters) - 2, -1, -1):
        spread = dot_t(down.astype(BF), parent_map)
        odd = (device >> level) & 1
        down = inters[level] + jnp.where(odd == 1, spread[:, rank:], spread[:, :rank])
    leaf_out = dot_t(down.astype(BF), map_ref[...])

    targets = []
    for region, ref in enumerate((own_ref, chip_ref, beyond_ref)):
        first = ref.shape[1] - leaves * rank if region == 2 else total
        skels = slice(first, first + leaves * rank)
        source, target = stacked_rows(ref[:feats, skels])
        charge = ref[feats:, skels].astype(BF)
        for leaf in range(leaves):
            span = slice(leaf * rank, (leaf + 1) * rank)
            skel_ref[region * leaves + leaf] = source[:, span]
            charge_ref[region * leaves + leaf] = charge[:, span]
            if region == 0:
                targets.append(target[:, span])
    sum_ref[...] = near_ref[...]
    build_stacks(beyond_ref, stack_ref, feats)
    for copy in copies:
        copy.wait()
    add_tiles(code_ref, target_ref, sum_ref, [(low, beyond_ref, stack_ref)], feats)
    fields = []
    for leaf in range(leaves):
        field = leaf_out[:, leaf * rank : (leaf + 1) * rank]
        where = [far_ref[leaf, slot] for slot in range(slots)]
        sources = jnp.concatenate([skel_ref[w] for w in where], 1)
        charges = jnp.concatenate([charge_ref[w] for w in where], 1)
        field += dot_t(charges, tile_of(targets[leaf], sources))
        fields.append(field.astype(BF))
    pieces = []
    for leaf in range(leaves):
        span = slice(leaf * width, (leaf + 1) * width)
        pieces.append(sum_ref[:, span] + dot(fields[leaf], interp_ref[:, span]))

    blocks = total // BLOCK
    shift = BLOCK.bit_length() - 1
    for leaf in range(leaves):
        index = order_ref[:, leaf * width : (leaf + 1) * width] - device * total
        hot = one_hot(index & (BLOCK - 1), BLOCK)
        high = jnp.broadcast_to(index >> shift, (rhs, width))
        rows = []
        for k in range(blocks):
            rows.append(jnp.where(high == k, pieces[leaf], 0.0).astype(BF))
        part = dot_t(jnp.concatenate(rows, 0), hot)
        acc_ref[...] = part if leaf == 0 else acc_ref[...] + part
    for k in range(blocks):
        out_ref[:, k * BLOCK : (k + 1) * BLOCK] = acc_ref[k * rhs : (k + 1) * rhs, :]


def finish(codes, sums, targets, packs, interp, order, maps, nodes, inters, base, levels, feats, low):
    rhs, total = sums.shape
    leaves = codes[1].shape[0]
    rank = interp.shape[0]
    stack, width = targets.shape[0], total // leaves
    fresh = (packs[2].shape[1] - leaves * rank) // width
    operands = [*codes, sums, targets, *packs, interp, order, *maps, *nodes, *inters]
    return pl.pallas_call(
        functools.partial(
            finish_kernel, feats=feats, base=base, levels=levels, done=len(inters), low=low
        ),
        out_shape=jax.ShapeDtypeStruct((rhs, total), F32),
        in_specs=[VMEM] * len(operands),
        out_specs=VMEM,
        scratch_shapes=[
            pltpu.SMEM(codes[0].shape, jnp.int32),
            pltpu.SMEM(codes[1].shape, jnp.int32),
            pltpu.VMEM((rhs, total), F32),
            pltpu.VMEM((fresh, stack, width), BF),
            pltpu.VMEM((3 * leaves, stack, rank), BF),
            pltpu.VMEM((3 * leaves, rhs, rank), BF),
            pltpu.VMEM((total // BLOCK * rhs, BLOCK), F32),
            pltpu.SemaphoreType.DMA((2,)),
        ],
        compiler_params=params(),
        name="finish",
    )(*operands)


def body(
    points,
    charges,
    inv_scale,
    order,
    near_list,
    near_count,
    far_list,
    skel_idx,
    interp,
    group_map,
    parent_map,
):
    feats = points.shape[0]
    leaves = near_list.shape[0]
    devices = lax.axis_size("leaf")
    order = order.reshape(1, -1)
    base = first_point(points.shape[1])
    chip = [(i, i ^ 1) for i in range(devices)]
    beyond = []
    for i in range(1, devices, 2):
        beyond += [(i, (i + 1) % devices), ((i + 1) % devices, i)]

    def send(value, mask):
        return lax.ppermute(value, "leaf", [(i, i ^ mask) for i in range(devices)])

    width = points.shape[1] // leaves
    early = leaves // 2
    placed, sources, targets = sort_points(inv_scale, points, charges, order, base, leaves)
    pack, first, rest, node, near_codes, far_codes = skeletons(
        placed,
        skel_idx,
        group_map,
        interp,
        near_list.T,
        near_count.reshape(1, -1),
        far_list,
        feats,
        early * width,
    )
    levels = devices.bit_length() - 1
    stages = [(base, min(2, levels - base)) for base in range(0, levels, 2)]
    pack_chip = send(pack, 1)
    nodes = [node, pack_chip] + [send(node, mask) for mask in range(2, 2 ** stages[0][1])]
    first = lax.ppermute(first, "leaf", beyond)
    rest = lax.ppermute(rest, "leaf", beyond)
    inters = []
    for stage, (base, count) in zip(stages[:-1], stages[1:]):
        fresh, node = climb_stage(nodes, *stage, parent_map, feats)
        inters += fresh
        nodes = [node] + [send(node, mask << base) for mask in range(1, 2**count)]
    rhs = charges.shape[0]
    low = 2 * leaves
    total = near_part(
        functools.partial(near_own_kernel, feats=feats),
        near_codes,
        targets,
        (pack, sources, pack_chip),
        leaves,
        rhs,
        2 * leaves,
        "near_own",
    )
    total = near_part(
        functools.partial(near_more_kernel, feats=feats, low=low + early),
        near_codes,
        targets,
        (total, rest),
        leaves - early,
        rhs,
        leaves // 2,
        "near_beyond",
    )
    return finish(
        (near_codes, far_codes),
        total,
        targets,
        (pack, pack_chip, first),
        interp,
        order,
        (group_map, parent_map),
        nodes,
        inters,
        *stages[-1],
        feats,
        low,
    )


def solution(mesh):
    placed = (
        P(None, ("fleet", "leaf")),
        P(None, ("fleet", "leaf")),
        P("fleet"),
        P(("fleet", "leaf")),
        P(("fleet", "leaf"), None),
        P(("fleet", "leaf")),
        P(("fleet", "leaf"), None),
        P(("fleet", "leaf"), None),
        P(None, ("fleet", "leaf")),
        P(("fleet", "leaf"), None),
        P("fleet", None),
    )
    return jax.shard_map(
        body, mesh=mesh, in_specs=placed, out_specs=P(None, ("fleet", "leaf")), check_vma=False
    )
```

```python
import functools
import math

import jax
import jax.numpy as jnp
from jax import lax
from jax.experimental import pallas as pl
from jax.experimental.pallas import tpu as pltpu
from jax.sharding import PartitionSpec as P

BF = jnp.bfloat16
F32 = jnp.float32
LANES = 128
BLOCK = 256
CHUNK = 512
VMEM = pl.BlockSpec(memory_space=pltpu.VMEM)
SMEM = pl.BlockSpec(memory_space=pltpu.SMEM)


def params():
    return pltpu.CompilerParams(vmem_limit_bytes=48 * 2**20)


def halves(z):
    hi = z.astype(BF)
    return hi, (z - hi.astype(F32)).astype(BF)


def stacked_rows(z):
    hi, mid = halves(z)
    norm = -0.5 * jnp.sum(z * z, 0, keepdims=True)
    n1 = norm.astype(BF).astype(F32)
    n2 = (norm - n1).astype(BF).astype(F32)
    n3 = norm - n1 - n2
    shape = (16, z.shape[1])
    row = lax.broadcasted_iota(jnp.int32, shape, 0)

    def extra(first):
        out = jnp.where((row >= 3 - first) & (row < 6 - first), 1.0, 0.0)
        for i, piece in enumerate((n1, n2, n3)):
            out = jnp.where(row == first + i, jnp.broadcast_to(piece, shape), out)
        return out.astype(BF)

    source = jnp.concatenate([hi, mid, hi, mid, extra(3)], 0)
    target = jnp.concatenate([hi, hi, mid, mid, extra(0)], 0)
    return source, target


def tile_of(source, target):
    e = lax.dot_general(source, target, (((0,), (0,)), ((), ())), preferred_element_type=F32)
    return jnp.exp2(e).astype(BF)


def dot_t(a, b):
    return lax.dot_general(a, b, (((1,), (1,)), ((), ())), preferred_element_type=F32)


def dot(a, b):
    return jnp.dot(a, b, preferred_element_type=F32)


def one_hot(low, size):
    rows = lax.broadcasted_iota(jnp.int32, (size, low.shape[1]), 0)
    return (rows == low).astype(F32).astype(BF)


def pick_lanes(blocks, index):
    rows = blocks[0].shape[0]
    parts = []
    for top in range(0, rows, 8):
        idx = jnp.broadcast_to(index, (8, LANES))
        high, low = idx >> 7, idx & (LANES - 1)
        out = jnp.zeros((8, LANES), F32)
        for k, block in enumerate(blocks):
            got = jnp.take_along_axis(block[top : top + 8], low, axis=1, mode="promise_in_bounds")
            out = jnp.where(high == k, got, out)
        parts.append(out)
    return jnp.concatenate(parts, 0)


def base_kernel(out_ref, *, total):
    out_ref[...] = jnp.full(out_ref.shape, lax.axis_index("leaf") * total, jnp.int32)


def first_point(total):
    return pl.pallas_call(
        functools.partial(base_kernel, total=total),
        out_shape=jax.ShapeDtypeStruct((1, LANES), jnp.int32),
        out_specs=VMEM,
        compiler_params=params(),
        cost_estimate=pl.CostEstimate(flops=10**9, bytes_accessed=10**6, transcendentals=0),
        name="first_point",
    )()


def sort_kernel(
    scale_ref, points_ref, charges_ref, order_ref, base_ref,
    pack_ref, source_ref, target_ref, zs_ref, bs_ref,
):
    feats, total = points_ref.shape
    rhs = charges_ref.shape[0]
    width = source_ref.shape[2]
    base = base_ref[:, :1]
    blocks = total // BLOCK
    shift = BLOCK.bit_length() - 1
    row = lax.broadcasted_iota(jnp.int32, (feats, LANES), 0)
    scale = jnp.zeros((feats, LANES), F32)
    for r in range(feats):
        scale = jnp.where(row == r, scale_ref[r], scale)
    scale = scale[:, :1] * math.sqrt(math.log2(math.e))
    for k in range(blocks):
        span = slice(k * BLOCK, (k + 1) * BLOCK)
        hi, mid = halves(points_ref[:, span] * scale)
        zs_ref[k * feats : (k + 1) * feats, :BLOCK] = hi
        zs_ref[k * feats : (k + 1) * feats, BLOCK:] = mid
        bs_ref[k * rhs : (k + 1) * rhs, :] = charges_ref[:, span].astype(BF)

    def step(j, carry):
        start = pl.multiple_of(j * CHUNK, CHUNK)
        index = order_ref[:, pl.ds(start, CHUNK)] - base
        hot = one_hot(index & (BLOCK - 1), BLOCK)
        yz = dot(zs_ref[...], jnp.concatenate([hot, hot], 0))
        yb = dot(bs_ref[...], hot)
        high = jnp.broadcast_to(index >> shift, (feats, CHUNK))
        az = jnp.zeros((feats, CHUNK), F32)
        ab = jnp.zeros((rhs, CHUNK), F32)
        for k in range(blocks):
            mask = high == k
            az = jnp.where(mask, yz[k * feats : (k + 1) * feats], az)
            ab = jnp.where(mask, yb[k * rhs : (k + 1) * rhs], ab)
        pack_ref[:feats, pl.ds(start, CHUNK)] = az
        pack_ref[feats:, pl.ds(start, CHUNK)] = ab
        source, target = stacked_rows(az)
        leaf, at = j * CHUNK // width, pl.multiple_of(j * CHUNK % width, CHUNK)
        source_ref[leaf, :, pl.ds(at, CHUNK)] = source
        target_ref[:, pl.ds(start, CHUNK)] = target
        return carry

    lax.fori_loop(0, total // CHUNK, step, 0, unroll=True)


def sort_points(inv_scale, points, charges, order, base, leaves):
    feats, total = points.shape
    rhs = charges.shape[0]
    blocks = total // BLOCK
    stack = 4 * feats + 16
    return pl.pallas_call(
        sort_kernel,
        out_shape=(
            jax.ShapeDtypeStruct((feats + rhs, total), F32),
            jax.ShapeDtypeStruct((leaves, stack, total // leaves), BF),
            jax.ShapeDtypeStruct((stack, total), BF),
        ),
        in_specs=[SMEM] + [VMEM] * 4,
        out_specs=(VMEM,) * 3,
        scratch_shapes=[
            pltpu.VMEM((blocks * feats, 2 * BLOCK), BF),
            pltpu.VMEM((blocks * rhs, BLOCK), BF),
        ],
        compiler_params=params(),
        cost_estimate=pl.CostEstimate(
            flops=6 * total * total * 16, bytes_accessed=4 * 10**6, transcendentals=0
        ),
        name="sort_points",
    )(inv_scale, points, charges, order, base)


def skeleton_kernel(
    sorted_ref, skel_ref, map_ref, interp_ref, list_ref, count_ref, far_ref,
    pack_ref, first_ref, rest_ref, node_ref, near_code_ref, far_code_ref, *, feats
):
    leaves, rank = skel_ref.shape
    rows, total = sorted_ref.shape
    width = total // leaves
    group_q = jnp.zeros((rows - feats, rank), F32)
    for leaf in range(leaves):
        span = slice(leaf * width, (leaf + 1) * width)
        out = slice(total + leaf * rank, total + (leaf + 1) * rank)
        columns = [
            sorted_ref[:feats, leaf * width + k : leaf * width + k + LANES]
            for k in range(0, width, LANES)
        ]
        pack_ref[:feats, out] = pick_lanes(columns, skel_ref[leaf : leaf + 1, :])
        charge = dot_t(sorted_ref[feats:, span].astype(BF), interp_ref[:, span]).astype(BF)
        pack_ref[feats:, out] = charge.astype(F32)
        group_q += dot(charge, map_ref[leaf * rank : (leaf + 1) * rank, :])
        pack_ref[:, span] = sorted_ref[:, span]
    columns = [pack_ref[:feats, total + k : total + k + LANES] for k in range(0, leaves * rank, LANES)]
    node_ref[:feats, :] = pick_lanes(
        columns, lax.broadcasted_iota(jnp.int32, (1, rank), 1) * leaves
    )
    node_ref[feats:, :] = group_q
    pack_ref[:, total + leaves * rank :] = node_ref[...]
    early = total - rest_ref.shape[1]
    first_ref[:, :early] = sorted_ref[:, :early]
    first_ref[:, early:] = pack_ref[:, total : total + leaves * rank]
    rest_ref[...] = sorted_ref[:, early:]
    used = lax.broadcasted_iota(jnp.int32, list_ref.shape, 0) < count_ref[...]
    near_code_ref[...] = jnp.where(used, code_of(list_ref[...], leaves), -1)
    far_code_ref[...] = code_of(far_ref[...], leaves)


def skeletons(points, skel_idx, group_map, interp, near_list, near_count, far_list, feats, early):
    rows, total = points.shape
    leaves, rank = skel_idx.shape
    skels = leaves * rank
    return pl.pallas_call(
        functools.partial(skeleton_kernel, feats=feats),
        out_shape=(
            jax.ShapeDtypeStruct((rows, total + skels + rank), F32),
            jax.ShapeDtypeStruct((rows, early + skels), F32),
            jax.ShapeDtypeStruct((rows, total - early), F32),
            jax.ShapeDtypeStruct((rows, rank), F32),
            jax.ShapeDtypeStruct(near_list.shape, jnp.int32),
            jax.ShapeDtypeStruct(far_list.shape, jnp.int32),
        ),
        in_specs=[VMEM] * 7,
        out_specs=(VMEM,) * 6,
        compiler_params=params(),
        name="skeletons",
    )(points, skel_idx, group_map, interp, near_list, near_count, far_list)


def code_of(leaf_id, leaves):
    device = lax.axis_index("leaf")
    rel = leaf_id - (device - 1) * leaves
    side = (rel >= leaves).astype(jnp.int32) + (rel >= 2 * leaves).astype(jnp.int32)
    chip = 2 * (1 - (device & 1))
    region = jnp.where(side == 1, 0, jnp.where(side == chip, 1, 2))
    return rel + (region - side) * leaves


def build_stacks(src_ref, stack_ref, feats):
    width = stack_ref.shape[2]
    for place in range(stack_ref.shape[0]):
        stack_ref[place] = stacked_rows(src_ref[:feats, place * width : (place + 1) * width])[0]


def add_tiles(code_ref, target_ref, out_ref, parts, feats):
    slots, leaves = code_ref.shape
    width = out_ref.shape[1] // leaves

    def add(leaf, place, src_ref, stack_ref):
        start = pl.multiple_of(leaf * width, width)
        at = pl.multiple_of(place * width, width)
        charge = src_ref[feats:, pl.ds(at, width)].astype(BF)
        tile = tile_of(stack_ref[place], target_ref[:, pl.ds(start, width)])
        out_ref[:, pl.ds(start, width)] += dot(charge, tile)

    def per_leaf(leaf, carry):
        def per_slot(slot, carry):
            code = code_ref[slot, leaf]
            for low, src_ref, stack_ref in parts:

                @pl.when((code >= low) & (code < low + stack_ref.shape[0]))
                def _():
                    add(leaf, code - low, src_ref, stack_ref)

            return carry

        return lax.fori_loop(0, slots, per_slot, carry)

    lax.fori_loop(0, leaves, per_leaf, 0)


def near_own_kernel(
    code_vmem, target_ref, own_ref, own_stack, chip_ref, out_ref, code_ref, chip_stack, sem, *, feats
):
    copy = pltpu.make_async_copy(code_vmem, code_ref, sem)
    copy.start()
    leaves = own_stack.shape[0]
    out_ref[...] = jnp.zeros_like(out_ref)
    build_stacks(chip_ref, chip_stack, feats)
    copy.wait()
    parts = [(0, own_ref, own_stack), (leaves, chip_ref, chip_stack)]
    add_tiles(code_ref, target_ref, out_ref, parts, feats)


def near_more_kernel(
    code_vmem, target_ref, acc_ref, src_ref, out_ref, code_ref, stack_ref, sem, *, feats, low
):
    copy = pltpu.make_async_copy(code_vmem, code_ref, sem)
    copy.start()
    out_ref[...] = acc_ref[...]
    build_stacks(src_ref, stack_ref, feats)
    copy.wait()
    add_tiles(code_ref, target_ref, out_ref, [(low, src_ref, stack_ref)], feats)


def near_part(kernel, codes, targets, operands, count, rhs, tiles, name):
    leaves = codes.shape[1]
    total = targets.shape[1]
    width = total // leaves
    return pl.pallas_call(
        kernel,
        out_shape=jax.ShapeDtypeStruct((rhs, total), F32),
        in_specs=[VMEM] * (2 + len(operands)),
        out_specs=VMEM,
        scratch_shapes=[
            pltpu.SMEM(codes.shape, jnp.int32),
            pltpu.VMEM((count, targets.shape[0], width), BF),
            pltpu.SemaphoreType.DMA,
        ],
        compiler_params=params(),
        cost_estimate=pl.CostEstimate(
            flops=tiles * width * width * 1024,
            bytes_accessed=tiles * 48 * width * 4,
            transcendentals=tiles * width * width,
        ),
        name=name,
    )(codes, targets, *operands)


def climb(nodes, base, levels, parent_map, feats, top=False):
    device = lax.axis_index("leaf")
    rank = nodes[0].shape[1]
    lane = lax.broadcasted_iota(jnp.int32, (1, rank), 1)
    inters = []
    for level in range(levels):
        own, other = nodes[0], nodes[1]
        source, _ = stacked_rows(other[:feats])
        _, target = stacked_rows(own[:feats])
        inters.append(dot(other[feats:].astype(BF), tile_of(source, target)))
        if top and level == levels - 1:
            break
        odd = (device >> (base + level)) & 1
        parents = []
        for k in range(0, len(nodes), 2):
            left = jnp.where(odd == 1, nodes[k + 1], nodes[k])
            right = jnp.where(odd == 1, nodes[k], nodes[k + 1])
            z = pick_lanes([left[:feats], right[:feats]], lane * 2)
            q = dot(left[feats:].astype(BF), parent_map[:rank, :])
            q += dot(right[feats:].astype(BF), parent_map[rank:, :])
            parents.append(jnp.concatenate([z, q], 0))
        nodes = parents
    return inters, nodes[0]


def climb_kernel(*refs, base, levels, feats):
    count = 2**levels
    rank = refs[count].shape[1]
    nodes = [ref[:, ref.shape[1] - rank :] for ref in refs[:count]]
    inters, node = climb(nodes, base, levels, refs[count][...], feats)
    for ref, value in zip(refs[count + 1 :], inters + [node]):
        ref[...] = value


def climb_stage(nodes, base, levels, parent_map, feats):
    rows, rank = nodes[0].shape[0], parent_map.shape[1]
    small = jax.ShapeDtypeStruct((rows - feats, rank), F32)
    outs = pl.pallas_call(
        functools.partial(climb_kernel, base=base, levels=levels, feats=feats),
        out_shape=(small,) * levels + (jax.ShapeDtypeStruct((rows, rank), F32),),
        in_specs=[VMEM] * (len(nodes) + 1),
        out_specs=(VMEM,) * (levels + 1),
        compiler_params=params(),
        name=f"climb_{base}",
    )(*nodes, parent_map)
    return list(outs[:-1]), outs[-1]


def finish_kernel(
    near_vmem, far_vmem, near_ref, target_ref, own_ref, chip_ref, beyond_ref, interp_ref, order_ref,
    map_ref, parent_ref, *refs, feats, base, levels, done, low,
):
    count = 2**levels
    nodes = [ref[...] for ref in refs[:count]]
    inters = [ref[...] for ref in refs[count : count + done]]
    out_ref, code_ref, far_ref, sum_ref, stack_ref, skel_ref, charge_ref, acc_ref, sems = refs[count + done :]
    copies = [
        pltpu.make_async_copy(near_vmem, code_ref, sems.at[0]),
        pltpu.make_async_copy(far_vmem, far_ref, sems.at[1]),
    ]
    for copy in copies:
        copy.start()
    leaves, slots = far_ref.shape
    rank = interp_ref.shape[0]
    rhs, total = near_ref.shape
    width = total // leaves
    device = lax.axis_index("leaf")
    parent_map = parent_ref[...]
    fresh, _ = climb(nodes, base, levels, parent_map, feats, top=True)
    inters = inters + fresh
    down = inters[-1]
    for level in range(len(inters) - 2, -1, -1):
        spread = dot_t(down.astype(BF), parent_map)
        odd = (device >> level) & 1
        down = inters[level] + jnp.where(odd == 1, spread[:, rank:], spread[:, :rank])
    leaf_out = dot_t(down.astype(BF), map_ref[...])

    targets = []
    for region, ref in enumerate((own_ref, chip_ref, beyond_ref)):
        first = ref.shape[1] - leaves * rank if region == 2 else total
        skels = slice(first, first + leaves * rank)
        source, target = stacked_rows(ref[:feats, skels])
        charge = ref[feats:, skels].astype(BF)
        for leaf in range(leaves):
            span = slice(leaf * rank, (leaf + 1) * rank)
            skel_ref[region * leaves + leaf] = source[:, span]
            charge_ref[region * leaves + leaf] = charge[:, span]
            if region == 0:
                targets.append(target[:, span])
    sum_ref[...] = near_ref[...]
    build_stacks(beyond_ref, stack_ref, feats)
    for copy in copies:
        copy.wait()
    add_tiles(code_ref, target_ref, sum_ref, [(low, beyond_ref, stack_ref)], feats)
    fields = []
    for leaf in range(leaves):
        field = leaf_out[:, leaf * rank : (leaf + 1) * rank]
        where = [far_ref[leaf, slot] for slot in range(slots)]
        sources = jnp.concatenate([skel_ref[w] for w in where], 1)
        charges = jnp.concatenate([charge_ref[w] for w in where], 1)
        field += dot_t(charges, tile_of(targets[leaf], sources))
        fields.append(field.astype(BF))
    pieces = []
    for leaf in range(leaves):
        span = slice(leaf * width, (leaf + 1) * width)
        pieces.append(sum_ref[:, span] + dot(fields[leaf], interp_ref[:, span]))

    blocks = total // BLOCK
    shift = BLOCK.bit_length() - 1
    for leaf in range(leaves):
        index = order_ref[:, leaf * width : (leaf + 1) * width] - device * total
        hot = one_hot(index & (BLOCK - 1), BLOCK)
        high = jnp.broadcast_to(index >> shift, (rhs, width))
        rows = []
        for k in range(blocks):
            rows.append(jnp.where(high == k, pieces[leaf], 0.0).astype(BF))
        part = dot_t(jnp.concatenate(rows, 0), hot)
        acc_ref[...] = part if leaf == 0 else acc_ref[...] + part
    for k in range(blocks):
        out_ref[:, k * BLOCK : (k + 1) * BLOCK] = acc_ref[k * rhs : (k + 1) * rhs, :]


def finish(codes, sums, targets, packs, interp, order, maps, nodes, inters, base, levels, feats, low):
    rhs, total = sums.shape
    leaves = codes[1].shape[0]
    rank = interp.shape[0]
    stack, width = targets.shape[0], total // leaves
    fresh = (packs[2].shape[1] - leaves * rank) // width
    operands = [*codes, sums, targets, *packs, interp, order, *maps, *nodes, *inters]
    return pl.pallas_call(
        functools.partial(
            finish_kernel, feats=feats, base=base, levels=levels, done=len(inters), low=low
        ),
        out_shape=jax.ShapeDtypeStruct((rhs, total), F32),
        in_specs=[VMEM] * len(operands),
        out_specs=VMEM,
        scratch_shapes=[
            pltpu.SMEM(codes[0].shape, jnp.int32),
            pltpu.SMEM(codes[1].shape, jnp.int32),
            pltpu.VMEM((rhs, total), F32),
            pltpu.VMEM((fresh, stack, width), BF),
            pltpu.VMEM((3 * leaves, stack, rank), BF),
            pltpu.VMEM((3 * leaves, rhs, rank), BF),
            pltpu.VMEM((total // BLOCK * rhs, BLOCK), F32),
            pltpu.SemaphoreType.DMA((2,)),
        ],
        compiler_params=params(),
        name="finish",
    )(*operands)


def body(
    points,
    charges,
    inv_scale,
    order,
    near_list,
    near_count,
    far_list,
    skel_idx,
    interp,
    group_map,
    parent_map,
):
    feats = points.shape[0]
    leaves = near_list.shape[0]
    devices = lax.axis_size("leaf")
    order = order.reshape(1, -1)
    base = first_point(points.shape[1])
    chip = [(i, i ^ 1) for i in range(devices)]
    fleets = lax.axis_size("fleet")
    beyond = []
    for first in range(0, fleets * devices, devices):
        for i in range(first + 1, first + devices - 1, 2):
            beyond += [(i, i + 1), (i + 1, i)]
        other = first ^ devices if fleets % 2 == 0 else first
        beyond += [(first, other), (first + devices - 1, other + devices - 1)]

    def send(value, mask):
        return lax.ppermute(value, "leaf", [(i, i ^ mask) for i in range(devices)])

    width = points.shape[1] // leaves
    early = leaves // 3
    placed, sources, targets = sort_points(inv_scale, points, charges, order, base, leaves)
    pack, first, rest, node, near_codes, far_codes = skeletons(
        placed,
        skel_idx,
        group_map,
        interp,
        near_list.T,
        near_count.reshape(1, -1),
        far_list,
        feats,
        early * width,
    )
    levels = devices.bit_length() - 1
    stages = [(base, min(2, levels - base)) for base in range(0, levels, 2)]
    pack_chip = send(pack, 1)
    nodes = [node, pack_chip] + [send(node, mask) for mask in range(2, 2 ** stages[0][1])]
    first = lax.ppermute(first, ("fleet", "leaf"), beyond)
    rest = lax.ppermute(rest, ("fleet", "leaf"), beyond)
    inters = []
    for stage, (base, count) in zip(stages[:-1], stages[1:]):
        fresh, node = climb_stage(nodes, *stage, parent_map, feats)
        inters += fresh
        nodes = [node] + [send(node, mask << base) for mask in range(1, 2**count)]
    rhs = charges.shape[0]
    low = 2 * leaves
    total = near_part(
        functools.partial(near_own_kernel, feats=feats),
        near_codes,
        targets,
        (pack, sources, pack_chip),
        leaves,
        rhs,
        2 * leaves,
        "near_own",
    )
    total = near_part(
        functools.partial(near_more_kernel, feats=feats, low=low + early),
        near_codes,
        targets,
        (total, rest),
        leaves - early,
        rhs,
        leaves // 2,
        "near_beyond",
    )
    return finish(
        (near_codes, far_codes),
        total,
        targets,
        (pack, pack_chip, first),
        interp,
        order,
        (group_map, parent_map),
        nodes,
        inters,
        *stages[-1],
        feats,
        low,
    )


def solution(mesh):
    placed = (
        P(None, ("fleet", "leaf")),
        P(None, ("fleet", "leaf")),
        P("fleet"),
        P(("fleet", "leaf")),
        P(("fleet", "leaf"), None),
        P(("fleet", "leaf")),
        P(("fleet", "leaf"), None),
        P(("fleet", "leaf"), None),
        P(None, ("fleet", "leaf")),
        P(("fleet", "leaf"), None),
        P("fleet", None),
    )
    return jax.shard_map(
        body, mesh=mesh, in_specs=placed, out_specs=P(None, ("fleet", "leaf")), check_vma=False
    )
```

```python
import functools
import math

import jax
import jax.numpy as jnp
from jax import lax
from jax.experimental import pallas as pl
from jax.experimental.pallas import tpu as pltpu
from jax.sharding import PartitionSpec as P

BF = jnp.bfloat16
F32 = jnp.float32
LANES = 128
BLOCK = 256
CHUNK = 512
VMEM = pl.BlockSpec(memory_space=pltpu.VMEM)


def params():
    return pltpu.CompilerParams(vmem_limit_bytes=48 * 2**20)


def halves(z):
    hi = z.astype(BF)
    return hi, (z - hi.astype(F32)).astype(BF)


def stacked_rows(z):
    hi, mid = halves(z)
    norm = -0.5 * jnp.sum(z * z, 0, keepdims=True)
    n1 = norm.astype(BF).astype(F32)
    n2 = (norm - n1).astype(BF).astype(F32)
    n3 = norm - n1 - n2
    shape = (16, z.shape[1])
    row = lax.broadcasted_iota(jnp.int32, shape, 0)

    def extra(first):
        out = jnp.where((row >= 3 - first) & (row < 6 - first), 1.0, 0.0)
        for i, piece in enumerate((n1, n2, n3)):
            out = jnp.where(row == first + i, jnp.broadcast_to(piece, shape), out)
        return out.astype(BF)

    source = jnp.concatenate([hi, mid, hi, mid, extra(3)], 0)
    target = jnp.concatenate([hi, hi, mid, mid, extra(0)], 0)
    return source, target


def tile_of(source, target):
    e = lax.dot_general(source, target, (((0,), (0,)), ((), ())), preferred_element_type=F32)
    return jnp.exp2(e).astype(BF)


def dot_t(a, b):
    return lax.dot_general(a, b, (((1,), (1,)), ((), ())), preferred_element_type=F32)


def dot(a, b):
    return jnp.dot(a, b, preferred_element_type=F32)


def one_hot(low, size):
    rows = lax.broadcasted_iota(jnp.int32, (size, low.shape[1]), 0)
    return (rows == low).astype(F32).astype(BF)


def pick_lanes(blocks, index):
    rows = blocks[0].shape[0]
    parts = []
    for top in range(0, rows, 8):
        idx = jnp.broadcast_to(index, (8, LANES))
        high, low = idx >> 7, idx & (LANES - 1)
        out = jnp.zeros((8, LANES), F32)
        for k, block in enumerate(blocks):
            got = jnp.take_along_axis(block[top : top + 8], low, axis=1, mode="promise_in_bounds")
            out = jnp.where(high == k, got, out)
        parts.append(out)
    return jnp.concatenate(parts, 0)


def base_kernel(out_ref, *, total):
    out_ref[...] = jnp.full(out_ref.shape, lax.axis_index("leaf") * total, jnp.int32)


def first_point(total):
    return pl.pallas_call(
        functools.partial(base_kernel, total=total),
        out_shape=jax.ShapeDtypeStruct((1, LANES), jnp.int32),
        out_specs=VMEM,
        compiler_params=params(),
        cost_estimate=pl.CostEstimate(flops=10**9, bytes_accessed=10**6, transcendentals=0),
        name="first_point",
    )()


def sort_kernel(
    scale_ref, points_ref, charges_ref, order_ref, base_ref,
    pack_ref, source_ref, target_ref, zs_ref, bs_ref,
):
    feats, total = points_ref.shape
    rhs = charges_ref.shape[0]
    width = source_ref.shape[2]
    base = base_ref[:, :1]
    blocks = total // BLOCK
    shift = BLOCK.bit_length() - 1
    row = lax.broadcasted_iota(jnp.int32, (feats, feats), 0)
    lane = lax.broadcasted_iota(jnp.int32, (feats, feats), 1)
    scale = jnp.sum(jnp.where(row == lane, scale_ref[...], 0.0), 1, keepdims=True)
    scale = scale * math.sqrt(math.log2(math.e))
    for k in range(blocks):
        span = slice(k * BLOCK, (k + 1) * BLOCK)
        hi, mid = halves(points_ref[:, span] * scale)
        zs_ref[k * feats : (k + 1) * feats, :BLOCK] = hi
        zs_ref[k * feats : (k + 1) * feats, BLOCK:] = mid
        bs_ref[k * rhs : (k + 1) * rhs, :] = charges_ref[:, span].astype(BF)

    def step(j, carry):
        start = pl.multiple_of(j * CHUNK, CHUNK)
        index = order_ref[:, pl.ds(start, CHUNK)] - base
        hot = one_hot(index & (BLOCK - 1), BLOCK)
        yz = dot(zs_ref[...], jnp.concatenate([hot, hot], 0))
        yb = dot(bs_ref[...], hot)
        high = jnp.broadcast_to(index >> shift, (feats, CHUNK))
        az = jnp.zeros((feats, CHUNK), F32)
        ab = jnp.zeros((rhs, CHUNK), F32)
        for k in range(blocks):
            mask = high == k
            az = jnp.where(mask, yz[k * feats : (k + 1) * feats], az)
            ab = jnp.where(mask, yb[k * rhs : (k + 1) * rhs], ab)
        pack_ref[:feats, pl.ds(start, CHUNK)] = az
        pack_ref[feats:, pl.ds(start, CHUNK)] = ab
        source, target = stacked_rows(az)
        leaf, at = j * CHUNK // width, pl.multiple_of(j * CHUNK % width, CHUNK)
        source_ref[leaf, :, pl.ds(at, CHUNK)] = source
        target_ref[:, pl.ds(start, CHUNK)] = target
        return carry

    lax.fori_loop(0, total // CHUNK, step, 0, unroll=True)


def sort_points(inv_scale, points, charges, order, base, leaves):
    feats, total = points.shape
    rhs = charges.shape[0]
    blocks = total // BLOCK
    stack = 4 * feats + 16
    return pl.pallas_call(
        sort_kernel,
        out_shape=(
            jax.ShapeDtypeStruct((feats + rhs, total), F32),
            jax.ShapeDtypeStruct((leaves, stack, total // leaves), BF),
            jax.ShapeDtypeStruct((stack, total), BF),
        ),
        in_specs=[VMEM] * 5,
        out_specs=(VMEM,) * 3,
        scratch_shapes=[
            pltpu.VMEM((blocks * feats, 2 * BLOCK), BF),
            pltpu.VMEM((blocks * rhs, BLOCK), BF),
        ],
        compiler_params=params(),
        cost_estimate=pl.CostEstimate(
            flops=6 * total * total * 16, bytes_accessed=4 * 10**6, transcendentals=0
        ),
        name="sort_points",
    )(inv_scale, points, charges, order, base)


def skeleton_kernel(
    sorted_ref, skel_ref, map_ref, interp_ref, list_ref, count_ref, far_ref,
    pack_ref, first_ref, rest_ref, node_ref, near_code_ref, far_code_ref, *, feats
):
    leaves, rank = skel_ref.shape
    rows, total = sorted_ref.shape
    width = total // leaves
    group_q = jnp.zeros((rows - feats, rank), F32)
    for leaf in range(leaves):
        span = slice(leaf * width, (leaf + 1) * width)
        out = slice(total + leaf * rank, total + (leaf + 1) * rank)
        columns = [
            sorted_ref[:feats, leaf * width + k : leaf * width + k + LANES]
            for k in range(0, width, LANES)
        ]
        pack_ref[:feats, out] = pick_lanes(columns, skel_ref[leaf : leaf + 1, :])
        charge = dot_t(sorted_ref[feats:, span].astype(BF), interp_ref[:, span]).astype(BF)
        pack_ref[feats:, out] = charge.astype(F32)
        group_q += dot(charge, map_ref[leaf * rank : (leaf + 1) * rank, :])
        pack_ref[:, span] = sorted_ref[:, span]
    columns = [pack_ref[:feats, total + k : total + k + LANES] for k in range(0, leaves * rank, LANES)]
    node_ref[:feats, :] = pick_lanes(
        columns, lax.broadcasted_iota(jnp.int32, (1, rank), 1) * leaves
    )
    node_ref[feats:, :] = group_q
    pack_ref[:, total + leaves * rank :] = node_ref[...]
    early = total - rest_ref.shape[1]
    first_ref[:, :early] = sorted_ref[:, :early]
    first_ref[:, early:] = pack_ref[:, total : total + leaves * rank]
    rest_ref[...] = sorted_ref[:, early:]
    used = lax.broadcasted_iota(jnp.int32, list_ref.shape, 0) < count_ref[...]
    near_code_ref[...] = jnp.where(used, code_of(list_ref[...], leaves), -1)
    far_code_ref[...] = code_of(far_ref[...], leaves)


def skeletons(points, skel_idx, group_map, interp, near_list, near_count, far_list, feats, early):
    rows, total = points.shape
    leaves, rank = skel_idx.shape
    skels = leaves * rank
    return pl.pallas_call(
        functools.partial(skeleton_kernel, feats=feats),
        out_shape=(
            jax.ShapeDtypeStruct((rows, total + skels + rank), F32),
            jax.ShapeDtypeStruct((rows, early + skels), F32),
            jax.ShapeDtypeStruct((rows, total - early), F32),
            jax.ShapeDtypeStruct((rows, rank), F32),
            jax.ShapeDtypeStruct(near_list.shape, jnp.int32),
            jax.ShapeDtypeStruct(far_list.shape, jnp.int32),
        ),
        in_specs=[VMEM] * 7,
        out_specs=(VMEM,) * 6,
        compiler_params=params(),
        name="skeletons",
    )(points, skel_idx, group_map, interp, near_list, near_count, far_list)


def code_of(leaf_id, leaves):
    device = lax.axis_index("leaf")
    rel = leaf_id - (device - 1) * leaves
    side = (rel >= leaves).astype(jnp.int32) + (rel >= 2 * leaves).astype(jnp.int32)
    chip = 2 * (1 - (device & 1))
    region = jnp.where(side == 1, 0, jnp.where(side == chip, 1, 2))
    return rel + (region - side) * leaves


def build_stacks(src_ref, stack_ref, feats):
    width = stack_ref.shape[2]
    for place in range(stack_ref.shape[0]):
        stack_ref[place] = stacked_rows(src_ref[:feats, place * width : (place + 1) * width])[0]


def add_tiles(code_ref, target_ref, out_ref, parts, feats):
    slots, leaves = code_ref.shape
    width = out_ref.shape[1] // leaves

    def add(leaf, place, src_ref, stack_ref):
        start = pl.multiple_of(leaf * width, width)
        at = pl.multiple_of(place * width, width)
        charge = src_ref[feats:, pl.ds(at, width)].astype(BF)
        tile = tile_of(stack_ref[place], target_ref[:, pl.ds(start, width)])
        out_ref[:, pl.ds(start, width)] += dot(charge, tile)

    def per_leaf(leaf, carry):
        def per_slot(slot, carry):
            code = code_ref[slot, leaf]
            for low, src_ref, stack_ref in parts:

                @pl.when((code >= low) & (code < low + stack_ref.shape[0]))
                def _():
                    add(leaf, code - low, src_ref, stack_ref)

            return carry

        return lax.fori_loop(0, slots, per_slot, carry)

    lax.fori_loop(0, leaves, per_leaf, 0)


def near_own_kernel(
    code_vmem, target_ref, own_ref, own_stack, chip_ref, out_ref, code_ref, chip_stack, sem, *, feats
):
    copy = pltpu.make_async_copy(code_vmem, code_ref, sem)
    copy.start()
    leaves = own_stack.shape[0]
    out_ref[...] = jnp.zeros_like(out_ref)
    build_stacks(chip_ref, chip_stack, feats)
    copy.wait()
    parts = [(0, own_ref, own_stack), (leaves, chip_ref, chip_stack)]
    add_tiles(code_ref, target_ref, out_ref, parts, feats)


def near_more_kernel(
    code_vmem, target_ref, acc_ref, src_ref, out_ref, code_ref, stack_ref, sem, *, feats, low
):
    copy = pltpu.make_async_copy(code_vmem, code_ref, sem)
    copy.start()
    out_ref[...] = acc_ref[...]
    build_stacks(src_ref, stack_ref, feats)
    copy.wait()
    add_tiles(code_ref, target_ref, out_ref, [(low, src_ref, stack_ref)], feats)


def near_part(kernel, codes, targets, operands, count, rhs, tiles, name):
    leaves = codes.shape[1]
    total = targets.shape[1]
    width = total // leaves
    return pl.pallas_call(
        kernel,
        out_shape=jax.ShapeDtypeStruct((rhs, total), F32),
        in_specs=[VMEM] * (2 + len(operands)),
        out_specs=VMEM,
        scratch_shapes=[
            pltpu.SMEM(codes.shape, jnp.int32),
            pltpu.VMEM((count, targets.shape[0], width), BF),
            pltpu.SemaphoreType.DMA,
        ],
        compiler_params=params(),
        cost_estimate=pl.CostEstimate(
            flops=tiles * width * width * 1024,
            bytes_accessed=tiles * 48 * width * 4,
            transcendentals=tiles * width * width,
        ),
        name=name,
    )(codes, targets, *operands)


def climb(nodes, base, levels, parent_map, feats, top=False):
    device = lax.axis_index("leaf")
    rank = nodes[0].shape[1]
    lane = lax.broadcasted_iota(jnp.int32, (1, rank), 1)
    inters = []
    for level in range(levels):
        own, other = nodes[0], nodes[1]
        source, _ = stacked_rows(other[:feats])
        _, target = stacked_rows(own[:feats])
        inters.append(dot(other[feats:].astype(BF), tile_of(source, target)))
        if top and level == levels - 1:
            break
        odd = (device >> (base + level)) & 1
        parents = []
        for k in range(0, len(nodes), 2):
            left = jnp.where(odd == 1, nodes[k + 1], nodes[k])
            right = jnp.where(odd == 1, nodes[k], nodes[k + 1])
            z = pick_lanes([left[:feats], right[:feats]], lane * 2)
            q = dot(left[feats:].astype(BF), parent_map[:rank, :])
            q += dot(right[feats:].astype(BF), parent_map[rank:, :])
            parents.append(jnp.concatenate([z, q], 0))
        nodes = parents
    return inters, nodes[0]


def climb_kernel(*refs, base, levels, feats):
    count = 2**levels
    rank = refs[count].shape[1]
    nodes = [ref[:, ref.shape[1] - rank :] for ref in refs[:count]]
    inters, node = climb(nodes, base, levels, refs[count][...], feats)
    for ref, value in zip(refs[count + 1 :], inters + [node]):
        ref[...] = value


def climb_stage(nodes, base, levels, parent_map, feats):
    rows, rank = nodes[0].shape[0], parent_map.shape[1]
    small = jax.ShapeDtypeStruct((rows - feats, rank), F32)
    outs = pl.pallas_call(
        functools.partial(climb_kernel, base=base, levels=levels, feats=feats),
        out_shape=(small,) * levels + (jax.ShapeDtypeStruct((rows, rank), F32),),
        in_specs=[VMEM] * (len(nodes) + 1),
        out_specs=(VMEM,) * (levels + 1),
        compiler_params=params(),
        name=f"climb_{base}",
    )(*nodes, parent_map)
    return list(outs[:-1]), outs[-1]


def finish_kernel(
    near_vmem, far_vmem, near_ref, target_ref, own_ref, chip_ref, beyond_ref, interp_ref, order_ref,
    map_ref, parent_ref, *refs, feats, base, levels, done, low,
):
    count = 2**levels
    nodes = [ref[...] for ref in refs[:count]]
    inters = [ref[...] for ref in refs[count : count + done]]
    out_ref, code_ref, far_ref, sum_ref, stack_ref, skel_ref, charge_ref, acc_ref, sems = refs[count + done :]
    copies = [
        pltpu.make_async_copy(near_vmem, code_ref, sems.at[0]),
        pltpu.make_async_copy(far_vmem, far_ref, sems.at[1]),
    ]
    for copy in copies:
        copy.start()
    leaves, slots = far_ref.shape
    rank = interp_ref.shape[0]
    rhs, total = near_ref.shape
    width = total // leaves
    device = lax.axis_index("leaf")
    parent_map = parent_ref[...]
    fresh, _ = climb(nodes, base, levels, parent_map, feats, top=True)
    inters = inters + fresh
    down = inters[-1]
    for level in range(len(inters) - 2, -1, -1):
        spread = dot_t(down.astype(BF), parent_map)
        odd = (device >> level) & 1
        down = inters[level] + jnp.where(odd == 1, spread[:, rank:], spread[:, :rank])
    leaf_out = dot_t(down.astype(BF), map_ref[...])

    targets = []
    for region, ref in enumerate((own_ref, chip_ref, beyond_ref)):
        first = ref.shape[1] - leaves * rank if region == 2 else total
        skels = slice(first, first + leaves * rank)
        source, target = stacked_rows(ref[:feats, skels])
        charge = ref[feats:, skels].astype(BF)
        for leaf in range(leaves):
            span = slice(leaf * rank, (leaf + 1) * rank)
            skel_ref[region * leaves + leaf] = source[:, span]
            charge_ref[region * leaves + leaf] = charge[:, span]
            if region == 0:
                targets.append(target[:, span])
    sum_ref[...] = near_ref[...]
    build_stacks(beyond_ref, stack_ref, feats)
    for copy in copies:
        copy.wait()
    add_tiles(code_ref, target_ref, sum_ref, [(low, beyond_ref, stack_ref)], feats)
    fields = []
    for leaf in range(leaves):
        field = leaf_out[:, leaf * rank : (leaf + 1) * rank]
        where = [far_ref[leaf, slot] for slot in range(slots)]
        sources = jnp.concatenate([skel_ref[w] for w in where], 1)
        charges = jnp.concatenate([charge_ref[w] for w in where], 1)
        field += dot_t(charges, tile_of(targets[leaf], sources))
        fields.append(field.astype(BF))
    pieces = []
    for leaf in range(leaves):
        span = slice(leaf * width, (leaf + 1) * width)
        pieces.append(sum_ref[:, span] + dot(fields[leaf], interp_ref[:, span]))

    blocks = total // BLOCK
    shift = BLOCK.bit_length() - 1
    for leaf in range(leaves):
        index = order_ref[:, leaf * width : (leaf + 1) * width] - device * total
        hot = one_hot(index & (BLOCK - 1), BLOCK)
        high = jnp.broadcast_to(index >> shift, (rhs, width))
        rows = []
        for k in range(blocks):
            rows.append(jnp.where(high == k, pieces[leaf], 0.0).astype(BF))
        part = dot_t(jnp.concatenate(rows, 0), hot)
        acc_ref[...] = part if leaf == 0 else acc_ref[...] + part
    for k in range(blocks):
        out_ref[:, k * BLOCK : (k + 1) * BLOCK] = acc_ref[k * rhs : (k + 1) * rhs, :]


def finish(codes, sums, targets, packs, interp, order, maps, nodes, inters, base, levels, feats, low):
    rhs, total = sums.shape
    leaves = codes[1].shape[0]
    rank = interp.shape[0]
    stack, width = targets.shape[0], total // leaves
    fresh = (packs[2].shape[1] - leaves * rank) // width
    operands = [*codes, sums, targets, *packs, interp, order, *maps, *nodes, *inters]
    return pl.pallas_call(
        functools.partial(
            finish_kernel, feats=feats, base=base, levels=levels, done=len(inters), low=low
        ),
        out_shape=jax.ShapeDtypeStruct((rhs, total), F32),
        in_specs=[VMEM] * len(operands),
        out_specs=VMEM,
        scratch_shapes=[
            pltpu.SMEM(codes[0].shape, jnp.int32),
            pltpu.SMEM(codes[1].shape, jnp.int32),
            pltpu.VMEM((rhs, total), F32),
            pltpu.VMEM((fresh, stack, width), BF),
            pltpu.VMEM((3 * leaves, stack, rank), BF),
            pltpu.VMEM((3 * leaves, rhs, rank), BF),
            pltpu.VMEM((total // BLOCK * rhs, BLOCK), F32),
            pltpu.SemaphoreType.DMA((2,)),
        ],
        compiler_params=params(),
        name="finish",
    )(*operands)


def body(
    points,
    charges,
    inv_scale,
    order,
    near_list,
    near_count,
    far_list,
    skel_idx,
    interp,
    group_map,
    parent_map,
):
    feats = points.shape[0]
    leaves = near_list.shape[0]
    devices = lax.axis_size("leaf")
    order = order.reshape(1, -1)
    base = first_point(points.shape[1])
    chip = [(i, i ^ 1) for i in range(devices)]
    fleets = lax.axis_size("fleet")
    beyond = []
    for first in range(0, fleets * devices, devices):
        for i in range(first + 1, first + devices - 1, 2):
            beyond += [(i, i + 1), (i + 1, i)]
        other = first ^ devices if fleets % 2 == 0 else first
        beyond += [(first, other), (first + devices - 1, other + devices - 1)]

    def send(value, mask):
        return lax.ppermute(value, "leaf", [(i, i ^ mask) for i in range(devices)])

    width = points.shape[1] // leaves
    early = leaves // 2
    placed, sources, targets = sort_points(
        inv_scale.reshape(1, -1), points, charges, order, base, leaves
    )
    pack, first, rest, node, near_codes, far_codes = skeletons(
        placed,
        skel_idx,
        group_map,
        interp,
        near_list.T,
        near_count.reshape(1, -1),
        far_list,
        feats,
        early * width,
    )
    levels = devices.bit_length() - 1
    stages = [(base, min(2, levels - base)) for base in range(0, levels, 2)]
    pack_chip = send(pack, 1)
    nodes = [node, pack_chip] + [send(node, mask) for mask in range(2, 2 ** stages[0][1])]
    first = lax.ppermute(first, ("fleet", "leaf"), beyond)
    rest = lax.ppermute(rest, ("fleet", "leaf"), beyond)
    inters = []
    for stage, (base, count) in zip(stages[:-1], stages[1:]):
        fresh, node = climb_stage(nodes, *stage, parent_map, feats)
        inters += fresh
        nodes = [node] + [send(node, mask << base) for mask in range(1, 2**count)]
    rhs = charges.shape[0]
    low = 2 * leaves
    total = near_part(
        functools.partial(near_own_kernel, feats=feats),
        near_codes,
        targets,
        (pack, sources, pack_chip),
        leaves,
        rhs,
        2 * leaves,
        "near_own",
    )
    total = near_part(
        functools.partial(near_more_kernel, feats=feats, low=low + early),
        near_codes,
        targets,
        (total, rest),
        leaves - early,
        rhs,
        leaves // 2,
        "near_beyond",
    )
    return finish(
        (near_codes, far_codes),
        total,
        targets,
        (pack, pack_chip, first),
        interp,
        order,
        (group_map, parent_map),
        nodes,
        inters,
        *stages[-1],
        feats,
        low,
    )


def solution(mesh):
    placed = (
        P(None, ("fleet", "leaf")),
        P(None, ("fleet", "leaf")),
        P("fleet"),
        P(("fleet", "leaf")),
        P(("fleet", "leaf"), None),
        P(("fleet", "leaf")),
        P(("fleet", "leaf"), None),
        P(("fleet", "leaf"), None),
        P(None, ("fleet", "leaf")),
        P(("fleet", "leaf"), None),
        P("fleet", None),
    )
    return jax.shard_map(
        body, mesh=mesh, in_specs=placed, out_specs=P(None, ("fleet", "leaf")), check_vma=False
    )
```

```python
import functools
import math

import jax
import jax.numpy as jnp
from jax import lax
from jax.experimental import pallas as pl
from jax.experimental.pallas import tpu as pltpu
from jax.sharding import PartitionSpec as P

BF = jnp.bfloat16
F32 = jnp.float32
LANES = 128
BLOCK = 256
CHUNK = 256
VMEM = pl.BlockSpec(memory_space=pltpu.VMEM)


def params():
    return pltpu.CompilerParams(vmem_limit_bytes=48 * 2**20)


def halves(z):
    hi = z.astype(BF)
    return hi, (z - hi.astype(F32)).astype(BF)


def stacked_rows(z):
    hi, mid = halves(z)
    norm = -0.5 * jnp.sum(z * z, 0, keepdims=True)
    n1 = norm.astype(BF).astype(F32)
    n2 = (norm - n1).astype(BF).astype(F32)
    n3 = norm - n1 - n2
    shape = (16, z.shape[1])
    row = lax.broadcasted_iota(jnp.int32, shape, 0)

    def extra(first):
        out = jnp.where((row >= 3 - first) & (row < 6 - first), 1.0, 0.0)
        for i, piece in enumerate((n1, n2, n3)):
            out = jnp.where(row == first + i, jnp.broadcast_to(piece, shape), out)
        return out.astype(BF)

    source = jnp.concatenate([hi, mid, hi, mid, extra(3)], 0)
    target = jnp.concatenate([hi, hi, mid, mid, extra(0)], 0)
    return source, target


def tile_of(source, target):
    e = lax.dot_general(source, target, (((0,), (0,)), ((), ())), preferred_element_type=F32)
    return jnp.exp2(e).astype(BF)


def dot_t(a, b):
    return lax.dot_general(a, b, (((1,), (1,)), ((), ())), preferred_element_type=F32)


def dot(a, b):
    return jnp.dot(a, b, preferred_element_type=F32)


def one_hot(low, size):
    rows = lax.broadcasted_iota(jnp.int32, (size, low.shape[1]), 0)
    return (rows == low).astype(F32).astype(BF)


def pick_lanes(blocks, index):
    rows = blocks[0].shape[0]
    parts = []
    for top in range(0, rows, 8):
        idx = jnp.broadcast_to(index, (8, LANES))
        high, low = idx >> 7, idx & (LANES - 1)
        out = jnp.zeros((8, LANES), F32)
        for k, block in enumerate(blocks):
            got = jnp.take_along_axis(block[top : top + 8], low, axis=1, mode="promise_in_bounds")
            out = jnp.where(high == k, got, out)
        parts.append(out)
    return jnp.concatenate(parts, 0)


def base_kernel(out_ref, *, total):
    out_ref[...] = jnp.full(out_ref.shape, lax.axis_index("leaf") * total, jnp.int32)


def first_point(total):
    return pl.pallas_call(
        functools.partial(base_kernel, total=total),
        out_shape=jax.ShapeDtypeStruct((1, LANES), jnp.int32),
        out_specs=VMEM,
        compiler_params=params(),
        cost_estimate=pl.CostEstimate(flops=10**9, bytes_accessed=10**6, transcendentals=0),
        name="first_point",
    )()


def sort_kernel(
    scale_ref, points_ref, charges_ref, order_ref, base_ref,
    pack_ref, source_ref, target_ref, zs_ref, bs_ref,
):
    feats, total = points_ref.shape
    rhs = charges_ref.shape[0]
    width = source_ref.shape[2]
    base = base_ref[:, :1]
    blocks = total // BLOCK
    shift = BLOCK.bit_length() - 1
    row = lax.broadcasted_iota(jnp.int32, (feats, feats), 0)
    lane = lax.broadcasted_iota(jnp.int32, (feats, feats), 1)
    scale = jnp.sum(jnp.where(row == lane, scale_ref[...], 0.0), 1, keepdims=True)
    scale = scale * math.sqrt(math.log2(math.e))
    for k in range(blocks):
        span = slice(k * BLOCK, (k + 1) * BLOCK)
        hi, mid = halves(points_ref[:, span] * scale)
        zs_ref[k * feats : (k + 1) * feats, :BLOCK] = hi
        zs_ref[k * feats : (k + 1) * feats, BLOCK:] = mid
        bs_ref[k * rhs : (k + 1) * rhs, :] = charges_ref[:, span].astype(BF)

    def step(j, carry):
        start = pl.multiple_of(j * CHUNK, CHUNK)
        index = order_ref[:, pl.ds(start, CHUNK)] - base
        hot = one_hot(index & (BLOCK - 1), BLOCK)
        yz = dot(zs_ref[...], jnp.concatenate([hot, hot], 0))
        yb = dot(bs_ref[...], hot)
        high = jnp.broadcast_to(index >> shift, (feats, CHUNK))
        az = jnp.zeros((feats, CHUNK), F32)
        ab = jnp.zeros((rhs, CHUNK), F32)
        for k in range(blocks):
            mask = high == k
            az = jnp.where(mask, yz[k * feats : (k + 1) * feats], az)
            ab = jnp.where(mask, yb[k * rhs : (k + 1) * rhs], ab)
        pack_ref[:feats, pl.ds(start, CHUNK)] = az
        pack_ref[feats:, pl.ds(start, CHUNK)] = ab
        source, target = stacked_rows(az)
        leaf, at = j * CHUNK // width, pl.multiple_of(j * CHUNK % width, CHUNK)
        source_ref[leaf, :, pl.ds(at, CHUNK)] = source
        target_ref[:, pl.ds(start, CHUNK)] = target
        return carry

    lax.fori_loop(0, total // CHUNK, step, 0, unroll=True)


def sort_points(inv_scale, points, charges, order, base, leaves):
    feats, total = points.shape
    rhs = charges.shape[0]
    blocks = total // BLOCK
    stack = 4 * feats + 16
    return pl.pallas_call(
        sort_kernel,
        out_shape=(
            jax.ShapeDtypeStruct((feats + rhs, total), F32),
            jax.ShapeDtypeStruct((leaves, stack, total // leaves), BF),
            jax.ShapeDtypeStruct((stack, total), BF),
        ),
        in_specs=[VMEM] * 5,
        out_specs=(VMEM,) * 3,
        scratch_shapes=[
            pltpu.VMEM((blocks * feats, 2 * BLOCK), BF),
            pltpu.VMEM((blocks * rhs, BLOCK), BF),
        ],
        compiler_params=params(),
        cost_estimate=pl.CostEstimate(
            flops=6 * total * total * 16, bytes_accessed=4 * 10**6, transcendentals=0
        ),
        name="sort_points",
    )(inv_scale, points, charges, order, base)


def skeleton_kernel(
    sorted_ref, skel_ref, map_ref, interp_ref, list_ref, count_ref, far_ref,
    pack_ref, first_ref, rest_ref, node_ref, near_code_ref, far_code_ref, *, feats
):
    leaves, rank = skel_ref.shape
    rows, total = sorted_ref.shape
    width = total // leaves
    group_q = jnp.zeros((rows - feats, rank), F32)
    for leaf in range(leaves):
        span = slice(leaf * width, (leaf + 1) * width)
        out = slice(total + leaf * rank, total + (leaf + 1) * rank)
        columns = [
            sorted_ref[:feats, leaf * width + k : leaf * width + k + LANES]
            for k in range(0, width, LANES)
        ]
        pack_ref[:feats, out] = pick_lanes(columns, skel_ref[leaf : leaf + 1, :])
        charge = dot_t(sorted_ref[feats:, span].astype(BF), interp_ref[:, span]).astype(BF)
        pack_ref[feats:, out] = charge.astype(F32)
        group_q += dot(charge, map_ref[leaf * rank : (leaf + 1) * rank, :])
        pack_ref[:, span] = sorted_ref[:, span]
    columns = [pack_ref[:feats, total + k : total + k + LANES] for k in range(0, leaves * rank, LANES)]
    node_ref[:feats, :] = pick_lanes(
        columns, lax.broadcasted_iota(jnp.int32, (1, rank), 1) * leaves
    )
    node_ref[feats:, :] = group_q
    pack_ref[:, total + leaves * rank :] = node_ref[...]
    early = total - rest_ref.shape[1]
    first_ref[:, :early] = sorted_ref[:, :early]
    first_ref[:, early:] = pack_ref[:, total : total + leaves * rank]
    rest_ref[...] = sorted_ref[:, early:]
    used = lax.broadcasted_iota(jnp.int32, list_ref.shape, 0) < count_ref[...]
    near_code_ref[...] = jnp.where(used, code_of(list_ref[...], leaves), -1)
    far_code_ref[...] = code_of(far_ref[...], leaves)


def skeletons(points, skel_idx, group_map, interp, near_list, near_count, far_list, feats, early):
    rows, total = points.shape
    leaves, rank = skel_idx.shape
    skels = leaves * rank
    return pl.pallas_call(
        functools.partial(skeleton_kernel, feats=feats),
        out_shape=(
            jax.ShapeDtypeStruct((rows, total + skels + rank), F32),
            jax.ShapeDtypeStruct((rows, early + skels), F32),
            jax.ShapeDtypeStruct((rows, total - early), F32),
            jax.ShapeDtypeStruct((rows, rank), F32),
            jax.ShapeDtypeStruct(near_list.shape, jnp.int32),
            jax.ShapeDtypeStruct(far_list.shape, jnp.int32),
        ),
        in_specs=[VMEM] * 7,
        out_specs=(VMEM,) * 6,
        compiler_params=params(),
        name="skeletons",
    )(points, skel_idx, group_map, interp, near_list, near_count, far_list)


def code_of(leaf_id, leaves):
    device = lax.axis_index("leaf")
    rel = leaf_id - (device - 1) * leaves
    side = (rel >= leaves).astype(jnp.int32) + (rel >= 2 * leaves).astype(jnp.int32)
    chip = 2 * (1 - (device & 1))
    region = jnp.where(side == 1, 0, jnp.where(side == chip, 1, 2))
    return rel + (region - side) * leaves


def build_stacks(src_ref, stack_ref, feats):
    width = stack_ref.shape[2]
    for place in range(stack_ref.shape[0]):
        stack_ref[place] = stacked_rows(src_ref[:feats, place * width : (place + 1) * width])[0]


def add_tiles(code_ref, target_ref, out_ref, parts, feats):
    slots, leaves = code_ref.shape
    width = out_ref.shape[1] // leaves

    def add(leaf, place, src_ref, stack_ref):
        start = pl.multiple_of(leaf * width, width)
        at = pl.multiple_of(place * width, width)
        charge = src_ref[feats:, pl.ds(at, width)].astype(BF)
        tile = tile_of(stack_ref[place], target_ref[:, pl.ds(start, width)])
        out_ref[:, pl.ds(start, width)] += dot(charge, tile)

    def per_leaf(leaf, carry):
        def per_slot(slot, carry):
            code = code_ref[slot, leaf]
            for low, src_ref, stack_ref in parts:

                @pl.when((code >= low) & (code < low + stack_ref.shape[0]))
                def _():
                    add(leaf, code - low, src_ref, stack_ref)

            return carry

        return lax.fori_loop(0, slots, per_slot, carry)

    lax.fori_loop(0, leaves, per_leaf, 0)


def near_own_kernel(
    code_vmem, target_ref, own_ref, own_stack, chip_ref, out_ref, code_ref, chip_stack, sem, *, feats
):
    copy = pltpu.make_async_copy(code_vmem, code_ref, sem)
    copy.start()
    leaves = own_stack.shape[0]
    out_ref[...] = jnp.zeros_like(out_ref)
    build_stacks(chip_ref, chip_stack, feats)
    copy.wait()
    parts = [(0, own_ref, own_stack), (leaves, chip_ref, chip_stack)]
    add_tiles(code_ref, target_ref, out_ref, parts, feats)


def near_more_kernel(
    code_vmem, target_ref, acc_ref, src_ref, out_ref, code_ref, stack_ref, sem, *, feats, low
):
    copy = pltpu.make_async_copy(code_vmem, code_ref, sem)
    copy.start()
    out_ref[...] = acc_ref[...]
    build_stacks(src_ref, stack_ref, feats)
    copy.wait()
    add_tiles(code_ref, target_ref, out_ref, [(low, src_ref, stack_ref)], feats)


def near_part(kernel, codes, targets, operands, count, rhs, tiles, name):
    leaves = codes.shape[1]
    total = targets.shape[1]
    width = total // leaves
    return pl.pallas_call(
        kernel,
        out_shape=jax.ShapeDtypeStruct((rhs, total), F32),
        in_specs=[VMEM] * (2 + len(operands)),
        out_specs=VMEM,
        scratch_shapes=[
            pltpu.SMEM(codes.shape, jnp.int32),
            pltpu.VMEM((count, targets.shape[0], width), BF),
            pltpu.SemaphoreType.DMA,
        ],
        compiler_params=params(),
        cost_estimate=pl.CostEstimate(
            flops=tiles * width * width * 1024,
            bytes_accessed=tiles * 48 * width * 4,
            transcendentals=tiles * width * width,
        ),
        name=name,
    )(codes, targets, *operands)


def climb(nodes, base, levels, parent_map, feats, top=False):
    device = lax.axis_index("leaf")
    rank = nodes[0].shape[1]
    lane = lax.broadcasted_iota(jnp.int32, (1, rank), 1)
    inters = []
    for level in range(levels):
        own, other = nodes[0], nodes[1]
        source, _ = stacked_rows(other[:feats])
        _, target = stacked_rows(own[:feats])
        inters.append(dot(other[feats:].astype(BF), tile_of(source, target)))
        if top and level == levels - 1:
            break
        odd = (device >> (base + level)) & 1
        parents = []
        for k in range(0, len(nodes), 2):
            left = jnp.where(odd == 1, nodes[k + 1], nodes[k])
            right = jnp.where(odd == 1, nodes[k], nodes[k + 1])
            z = pick_lanes([left[:feats], right[:feats]], lane * 2)
            q = dot(left[feats:].astype(BF), parent_map[:rank, :])
            q += dot(right[feats:].astype(BF), parent_map[rank:, :])
            parents.append(jnp.concatenate([z, q], 0))
        nodes = parents
    return inters, nodes[0]


def climb_kernel(*refs, base, levels, feats):
    count = 2**levels
    rank = refs[count].shape[1]
    nodes = [ref[:, ref.shape[1] - rank :] for ref in refs[:count]]
    inters, node = climb(nodes, base, levels, refs[count][...], feats)
    for ref, value in zip(refs[count + 1 :], inters + [node]):
        ref[...] = value


def climb_stage(nodes, base, levels, parent_map, feats):
    rows, rank = nodes[0].shape[0], parent_map.shape[1]
    small = jax.ShapeDtypeStruct((rows - feats, rank), F32)
    outs = pl.pallas_call(
        functools.partial(climb_kernel, base=base, levels=levels, feats=feats),
        out_shape=(small,) * levels + (jax.ShapeDtypeStruct((rows, rank), F32),),
        in_specs=[VMEM] * (len(nodes) + 1),
        out_specs=(VMEM,) * (levels + 1),
        compiler_params=params(),
        name=f"climb_{base}",
    )(*nodes, parent_map)
    return list(outs[:-1]), outs[-1]


def finish_kernel(
    near_vmem, far_vmem, near_ref, target_ref, own_ref, chip_ref, beyond_ref, interp_ref, order_ref,
    map_ref, parent_ref, *refs, feats, base, levels, done, low,
):
    count = 2**levels
    nodes = [ref[...] for ref in refs[:count]]
    inters = [ref[...] for ref in refs[count : count + done]]
    out_ref, code_ref, far_ref, sum_ref, stack_ref, skel_ref, charge_ref, acc_ref, sems = refs[count + done :]
    copies = [
        pltpu.make_async_copy(near_vmem, code_ref, sems.at[0]),
        pltpu.make_async_copy(far_vmem, far_ref, sems.at[1]),
    ]
    for copy in copies:
        copy.start()
    leaves, slots = far_ref.shape
    rank = interp_ref.shape[0]
    rhs, total = near_ref.shape
    width = total // leaves
    device = lax.axis_index("leaf")
    parent_map = parent_ref[...]
    fresh, _ = climb(nodes, base, levels, parent_map, feats, top=True)
    inters = inters + fresh
    down = inters[-1]
    for level in range(len(inters) - 2, -1, -1):
        spread = dot_t(down.astype(BF), parent_map)
        odd = (device >> level) & 1
        down = inters[level] + jnp.where(odd == 1, spread[:, rank:], spread[:, :rank])
    leaf_out = dot_t(down.astype(BF), map_ref[...])

    targets = []
    for region, ref in enumerate((own_ref, chip_ref, beyond_ref)):
        first = ref.shape[1] - leaves * rank if region == 2 else total
        skels = slice(first, first + leaves * rank)
        source, target = stacked_rows(ref[:feats, skels])
        charge = ref[feats:, skels].astype(BF)
        for leaf in range(leaves):
            span = slice(leaf * rank, (leaf + 1) * rank)
            skel_ref[region * leaves + leaf] = source[:, span]
            charge_ref[region * leaves + leaf] = charge[:, span]
            if region == 0:
                targets.append(target[:, span])
    sum_ref[...] = near_ref[...]
    build_stacks(beyond_ref, stack_ref, feats)
    for copy in copies:
        copy.wait()
    add_tiles(code_ref, target_ref, sum_ref, [(low, beyond_ref, stack_ref)], feats)
    fields = []
    for leaf in range(leaves):
        field = leaf_out[:, leaf * rank : (leaf + 1) * rank]
        where = [far_ref[leaf, slot] for slot in range(slots)]
        sources = jnp.concatenate([skel_ref[w] for w in where], 1)
        charges = jnp.concatenate([charge_ref[w] for w in where], 1)
        field += dot_t(charges, tile_of(targets[leaf], sources))
        fields.append(field.astype(BF))
    pieces = []
    for leaf in range(leaves):
        span = slice(leaf * width, (leaf + 1) * width)
        pieces.append(sum_ref[:, span] + dot(fields[leaf], interp_ref[:, span]))

    blocks = total // BLOCK
    shift = BLOCK.bit_length() - 1
    for leaf in range(leaves):
        index = order_ref[:, leaf * width : (leaf + 1) * width] - device * total
        hot = one_hot(index & (BLOCK - 1), BLOCK)
        high = jnp.broadcast_to(index >> shift, (rhs, width))
        rows = []
        for k in range(blocks):
            rows.append(jnp.where(high == k, pieces[leaf], 0.0).astype(BF))
        part = dot_t(jnp.concatenate(rows, 0), hot)
        acc_ref[...] = part if leaf == 0 else acc_ref[...] + part
    for k in range(blocks):
        out_ref[:, k * BLOCK : (k + 1) * BLOCK] = acc_ref[k * rhs : (k + 1) * rhs, :]


def finish(codes, sums, targets, packs, interp, order, maps, nodes, inters, base, levels, feats, low):
    rhs, total = sums.shape
    leaves = codes[1].shape[0]
    rank = interp.shape[0]
    stack, width = targets.shape[0], total // leaves
    fresh = (packs[2].shape[1] - leaves * rank) // width
    operands = [*codes, sums, targets, *packs, interp, order, *maps, *nodes, *inters]
    return pl.pallas_call(
        functools.partial(
            finish_kernel, feats=feats, base=base, levels=levels, done=len(inters), low=low
        ),
        out_shape=jax.ShapeDtypeStruct((rhs, total), F32),
        in_specs=[VMEM] * len(operands),
        out_specs=VMEM,
        scratch_shapes=[
            pltpu.SMEM(codes[0].shape, jnp.int32),
            pltpu.SMEM(codes[1].shape, jnp.int32),
            pltpu.VMEM((rhs, total), F32),
            pltpu.VMEM((fresh, stack, width), BF),
            pltpu.VMEM((3 * leaves, stack, rank), BF),
            pltpu.VMEM((3 * leaves, rhs, rank), BF),
            pltpu.VMEM((total // BLOCK * rhs, BLOCK), F32),
            pltpu.SemaphoreType.DMA((2,)),
        ],
        compiler_params=params(),
        name="finish",
    )(*operands)


def body(
    points,
    charges,
    inv_scale,
    order,
    near_list,
    near_count,
    far_list,
    skel_idx,
    interp,
    group_map,
    parent_map,
):
    feats = points.shape[0]
    leaves = near_list.shape[0]
    devices = lax.axis_size("leaf")
    order = order.reshape(1, -1)
    base = first_point(points.shape[1])
    chip = [(i, i ^ 1) for i in range(devices)]
    fleets = lax.axis_size("fleet")
    beyond = []
    for first in range(0, fleets * devices, devices):
        for i in range(first + 1, first + devices - 1, 2):
            beyond += [(i, i + 1), (i + 1, i)]
        other = first ^ devices if fleets % 2 == 0 else first
        beyond += [(first, other), (first + devices - 1, other + devices - 1)]

    def send(value, mask):
        return lax.ppermute(value, "leaf", [(i, i ^ mask) for i in range(devices)])

    width = points.shape[1] // leaves
    early = leaves // 2
    placed, sources, targets = sort_points(
        inv_scale.reshape(1, -1), points, charges, order, base, leaves
    )
    pack, first, rest, node, near_codes, far_codes = skeletons(
        placed,
        skel_idx,
        group_map,
        interp,
        near_list.T,
        near_count.reshape(1, -1),
        far_list,
        feats,
        early * width,
    )
    levels = devices.bit_length() - 1
    stages = [(base, min(2, levels - base)) for base in range(0, levels, 2)]
    pack_chip = send(pack, 1)
    nodes = [node, pack_chip] + [send(node, mask) for mask in range(2, 2 ** stages[0][1])]
    first = lax.ppermute(first, ("fleet", "leaf"), beyond)
    rest = lax.ppermute(rest, ("fleet", "leaf"), beyond)
    inters = []
    for stage, (base, count) in zip(stages[:-1], stages[1:]):
        fresh, node = climb_stage(nodes, *stage, parent_map, feats)
        inters += fresh
        nodes = [node] + [send(node, mask << base) for mask in range(1, 2**count)]
    rhs = charges.shape[0]
    low = 2 * leaves
    total = near_part(
        functools.partial(near_own_kernel, feats=feats),
        near_codes,
        targets,
        (pack, sources, pack_chip),
        leaves,
        rhs,
        2 * leaves,
        "near_own",
    )
    total = near_part(
        functools.partial(near_more_kernel, feats=feats, low=low + early),
        near_codes,
        targets,
        (total, rest),
        leaves - early,
        rhs,
        leaves // 2,
        "near_beyond",
    )
    return finish(
        (near_codes, far_codes),
        total,
        targets,
        (pack, pack_chip, first),
        interp,
        order,
        (group_map, parent_map),
        nodes,
        inters,
        *stages[-1],
        feats,
        low,
    )


def solution(mesh):
    placed = (
        P(None, ("fleet", "leaf")),
        P(None, ("fleet", "leaf")),
        P("fleet"),
        P(("fleet", "leaf")),
        P(("fleet", "leaf"), None),
        P(("fleet", "leaf")),
        P(("fleet", "leaf"), None),
        P(("fleet", "leaf"), None),
        P(None, ("fleet", "leaf")),
        P(("fleet", "leaf"), None),
        P("fleet", None),
    )
    return jax.shard_map(
        body, mesh=mesh, in_specs=placed, out_specs=P(None, ("fleet", "leaf")), check_vma=False
    )
```

```python
import functools
import math

import jax
import jax.numpy as jnp
from jax import lax
from jax.experimental import pallas as pl
from jax.experimental.pallas import tpu as pltpu
from jax.sharding import PartitionSpec as P

BF = jnp.bfloat16
F32 = jnp.float32
LANES = 128
BLOCK = 256
CHUNK = 256
VMEM = pl.BlockSpec(memory_space=pltpu.VMEM)


def params():
    return pltpu.CompilerParams(vmem_limit_bytes=48 * 2**20)


def halves(z):
    hi = z.astype(BF)
    return hi, (z - hi.astype(F32)).astype(BF)


def stacked_rows(z):
    hi, mid = halves(z)
    norm = -0.5 * jnp.sum(z * z, 0, keepdims=True)
    n1 = norm.astype(BF).astype(F32)
    n2 = (norm - n1).astype(BF).astype(F32)
    n3 = norm - n1 - n2
    shape = (16, z.shape[1])
    row = lax.broadcasted_iota(jnp.int32, shape, 0)

    def extra(first):
        out = jnp.where((row >= 3 - first) & (row < 6 - first), 1.0, 0.0)
        for i, piece in enumerate((n1, n2, n3)):
            out = jnp.where(row == first + i, jnp.broadcast_to(piece, shape), out)
        return out.astype(BF)

    source = jnp.concatenate([hi, mid, hi, mid, extra(3)], 0)
    target = jnp.concatenate([hi, hi, mid, mid, extra(0)], 0)
    return source, target


def tile_of(source, target):
    e = lax.dot_general(source, target, (((0,), (0,)), ((), ())), preferred_element_type=F32)
    return jnp.exp2(e).astype(BF)


def dot_t(a, b):
    return lax.dot_general(a, b, (((1,), (1,)), ((), ())), preferred_element_type=F32)


def dot(a, b):
    return jnp.dot(a, b, preferred_element_type=F32)


def one_hot(low, size):
    rows = lax.broadcasted_iota(jnp.int32, (size, low.shape[1]), 0)
    return (rows == low).astype(F32).astype(BF)


def pick_lanes(blocks, index):
    rows = blocks[0].shape[0]
    parts = []
    for top in range(0, rows, 8):
        idx = jnp.broadcast_to(index, (8, LANES))
        high, low = idx >> 7, idx & (LANES - 1)
        out = jnp.zeros((8, LANES), F32)
        for k, block in enumerate(blocks):
            got = jnp.take_along_axis(block[top : top + 8], low, axis=1, mode="promise_in_bounds")
            out = jnp.where(high == k, got, out)
        parts.append(out)
    return jnp.concatenate(parts, 0)


def base_kernel(out_ref, *, total):
    out_ref[...] = jnp.full(out_ref.shape, lax.axis_index("leaf") * total, jnp.int32)


def first_point(total):
    return pl.pallas_call(
        functools.partial(base_kernel, total=total),
        out_shape=jax.ShapeDtypeStruct((1, LANES), jnp.int32),
        out_specs=VMEM,
        compiler_params=params(),
        cost_estimate=pl.CostEstimate(flops=10**9, bytes_accessed=10**6, transcendentals=0),
        name="first_point",
    )()


def sort_kernel(
    scale_ref, points_ref, charges_ref, order_ref, base_ref,
    pack_ref, source_ref, target_ref, zs_ref, bs_ref,
):
    feats, total = points_ref.shape
    rhs = charges_ref.shape[0]
    width = source_ref.shape[2]
    base = base_ref[:, :1]
    blocks = total // BLOCK
    shift = BLOCK.bit_length() - 1
    row = lax.broadcasted_iota(jnp.int32, (feats, feats), 0)
    lane = lax.broadcasted_iota(jnp.int32, (feats, feats), 1)
    scale = jnp.sum(jnp.where(row == lane, scale_ref[...], 0.0), 1, keepdims=True)
    scale = scale * math.sqrt(math.log2(math.e))
    for k in range(blocks):
        span = slice(k * BLOCK, (k + 1) * BLOCK)
        hi, mid = halves(points_ref[:, span] * scale)
        zs_ref[k * feats : (k + 1) * feats, :BLOCK] = hi
        zs_ref[k * feats : (k + 1) * feats, BLOCK:] = mid
        bs_ref[k * rhs : (k + 1) * rhs, :] = charges_ref[:, span].astype(BF)

    def step(j, carry):
        start = pl.multiple_of(j * CHUNK, CHUNK)
        index = order_ref[:, pl.ds(start, CHUNK)] - base
        hot = one_hot(index & (BLOCK - 1), BLOCK)
        yz = dot(zs_ref[...], jnp.concatenate([hot, hot], 0))
        yb = dot(bs_ref[...], hot)
        high = jnp.broadcast_to(index >> shift, (feats, CHUNK))
        az = jnp.zeros((feats, CHUNK), F32)
        ab = jnp.zeros((rhs, CHUNK), F32)
        for k in range(blocks):
            mask = high == k
            az = jnp.where(mask, yz[k * feats : (k + 1) * feats], az)
            ab = jnp.where(mask, yb[k * rhs : (k + 1) * rhs], ab)
        pack_ref[:feats, pl.ds(start, CHUNK)] = az
        pack_ref[feats:, pl.ds(start, CHUNK)] = ab
        source, target = stacked_rows(az)
        leaf, at = j * CHUNK // width, pl.multiple_of(j * CHUNK % width, CHUNK)
        source_ref[leaf, :, pl.ds(at, CHUNK)] = source
        target_ref[:, pl.ds(start, CHUNK)] = target
        return carry

    lax.fori_loop(0, total // CHUNK, step, 0, unroll=True)


def sort_points(inv_scale, points, charges, order, base, leaves):
    feats, total = points.shape
    rhs = charges.shape[0]
    blocks = total // BLOCK
    stack = 4 * feats + 16
    return pl.pallas_call(
        sort_kernel,
        out_shape=(
            jax.ShapeDtypeStruct((feats + rhs, total), F32),
            jax.ShapeDtypeStruct((leaves, stack, total // leaves), BF),
            jax.ShapeDtypeStruct((stack, total), BF),
        ),
        in_specs=[VMEM] * 5,
        out_specs=(VMEM,) * 3,
        scratch_shapes=[
            pltpu.VMEM((blocks * feats, 2 * BLOCK), BF),
            pltpu.VMEM((blocks * rhs, BLOCK), BF),
        ],
        compiler_params=params(),
        cost_estimate=pl.CostEstimate(
            flops=6 * total * total * 16, bytes_accessed=4 * 10**6, transcendentals=0
        ),
        name="sort_points",
    )(inv_scale, points, charges, order, base)


def skeleton_kernel(
    sorted_ref, skel_ref, map_ref, interp_ref, list_ref, count_ref, far_ref,
    pack_ref, first_ref, rest_ref, node_ref, near_code_ref, far_code_ref, *, feats
):
    leaves, rank = skel_ref.shape
    rows, total = sorted_ref.shape
    width = total // leaves
    group_q = jnp.zeros((rows - feats, rank), F32)
    for leaf in range(leaves):
        span = slice(leaf * width, (leaf + 1) * width)
        out = slice(total + leaf * rank, total + (leaf + 1) * rank)
        columns = [
            sorted_ref[:feats, leaf * width + k : leaf * width + k + LANES]
            for k in range(0, width, LANES)
        ]
        pack_ref[:feats, out] = pick_lanes(columns, skel_ref[leaf : leaf + 1, :])
        charge = dot_t(sorted_ref[feats:, span].astype(BF), interp_ref[:, span]).astype(BF)
        pack_ref[feats:, out] = charge.astype(F32)
        group_q += dot(charge, map_ref[leaf * rank : (leaf + 1) * rank, :])
        pack_ref[:, span] = sorted_ref[:, span]
    columns = [pack_ref[:feats, total + k : total + k + LANES] for k in range(0, leaves * rank, LANES)]
    node_ref[:feats, :] = pick_lanes(
        columns, lax.broadcasted_iota(jnp.int32, (1, rank), 1) * leaves
    )
    node_ref[feats:, :] = group_q
    pack_ref[:, total + leaves * rank :] = node_ref[...]
    early = total - rest_ref.shape[1]
    first_ref[:, :early] = sorted_ref[:, :early]
    first_ref[:, early:] = pack_ref[:, total : total + leaves * rank]
    rest_ref[...] = sorted_ref[:, early:]
    used = lax.broadcasted_iota(jnp.int32, list_ref.shape, 0) < count_ref[...]
    near_code_ref[...] = jnp.where(used, code_of(list_ref[...], leaves), -1)
    far_code_ref[...] = code_of(far_ref[...], leaves)


def skeletons(points, skel_idx, group_map, interp, near_list, near_count, far_list, feats, early):
    rows, total = points.shape
    leaves, rank = skel_idx.shape
    skels = leaves * rank
    return pl.pallas_call(
        functools.partial(skeleton_kernel, feats=feats),
        out_shape=(
            jax.ShapeDtypeStruct((rows, total + skels + rank), F32),
            jax.ShapeDtypeStruct((rows, early + skels), F32),
            jax.ShapeDtypeStruct((rows, total - early), F32),
            jax.ShapeDtypeStruct((rows, rank), F32),
            jax.ShapeDtypeStruct(near_list.shape, jnp.int32),
            jax.ShapeDtypeStruct(far_list.shape, jnp.int32),
        ),
        in_specs=[VMEM] * 7,
        out_specs=(VMEM,) * 6,
        compiler_params=params(),
        name="skeletons",
    )(points, skel_idx, group_map, interp, near_list, near_count, far_list)


def code_of(leaf_id, leaves):
    device = lax.axis_index("leaf")
    rel = leaf_id - (device - 1) * leaves
    side = (rel >= leaves).astype(jnp.int32) + (rel >= 2 * leaves).astype(jnp.int32)
    chip = 2 * (1 - (device & 1))
    region = jnp.where(side == 1, 0, jnp.where(side == chip, 1, 2))
    return rel + (region - side) * leaves


def build_stacks(src_ref, stack_ref, feats):
    width = stack_ref.shape[2]
    for place in range(stack_ref.shape[0]):
        stack_ref[place] = stacked_rows(src_ref[:feats, place * width : (place + 1) * width])[0]


def add_tiles(code_ref, target_ref, out_ref, parts, feats):
    slots, leaves = code_ref.shape
    width = out_ref.shape[1] // leaves

    def add(leaf, place, src_ref, stack_ref):
        start = pl.multiple_of(leaf * width, width)
        at = pl.multiple_of(place * width, width)
        charge = src_ref[feats:, pl.ds(at, width)].astype(BF)
        tile = tile_of(stack_ref[place], target_ref[:, pl.ds(start, width)])
        out_ref[:, pl.ds(start, width)] += dot(charge, tile)

    def per_leaf(leaf, carry):
        def per_slot(slot, carry):
            code = code_ref[slot, leaf]
            for low, src_ref, stack_ref in parts:

                @pl.when((code >= low) & (code < low + stack_ref.shape[0]))
                def _():
                    add(leaf, code - low, src_ref, stack_ref)

            return carry

        return lax.fori_loop(0, slots, per_slot, carry)

    lax.fori_loop(0, leaves, per_leaf, 0)


def near_own_kernel(
    code_vmem, target_ref, own_ref, own_stack, chip_ref, out_ref, code_ref, chip_stack, sem, *, feats
):
    copy = pltpu.make_async_copy(code_vmem, code_ref, sem)
    copy.start()
    leaves = own_stack.shape[0]
    out_ref[...] = jnp.zeros_like(out_ref)
    build_stacks(chip_ref, chip_stack, feats)
    copy.wait()
    parts = [(0, own_ref, own_stack), (leaves, chip_ref, chip_stack)]
    add_tiles(code_ref, target_ref, out_ref, parts, feats)


def near_more_kernel(
    code_vmem, target_ref, acc_ref, src_ref, out_ref, code_ref, stack_ref, sem, *, feats, low
):
    copy = pltpu.make_async_copy(code_vmem, code_ref, sem)
    copy.start()
    out_ref[...] = acc_ref[...]
    build_stacks(src_ref, stack_ref, feats)
    copy.wait()
    add_tiles(code_ref, target_ref, out_ref, [(low, src_ref, stack_ref)], feats)


def near_part(kernel, codes, targets, operands, count, rhs, tiles, name):
    leaves = codes.shape[1]
    total = targets.shape[1]
    width = total // leaves
    return pl.pallas_call(
        kernel,
        out_shape=jax.ShapeDtypeStruct((rhs, total), F32),
        in_specs=[VMEM] * (2 + len(operands)),
        out_specs=VMEM,
        scratch_shapes=[
            pltpu.SMEM(codes.shape, jnp.int32),
            pltpu.VMEM((count, targets.shape[0], width), BF),
            pltpu.SemaphoreType.DMA,
        ],
        compiler_params=params(),
        cost_estimate=pl.CostEstimate(
            flops=tiles * width * width * 1024,
            bytes_accessed=tiles * 48 * width * 4,
            transcendentals=tiles * width * width,
        ),
        name=name,
    )(codes, targets, *operands)


def climb(nodes, base, levels, parent_map, feats, top=False):
    device = lax.axis_index("leaf")
    rank = nodes[0].shape[1]
    lane = lax.broadcasted_iota(jnp.int32, (1, rank), 1)
    inters = []
    for level in range(levels):
        own, other = nodes[0], nodes[1]
        source, _ = stacked_rows(other[:feats])
        _, target = stacked_rows(own[:feats])
        inters.append(dot(other[feats:].astype(BF), tile_of(source, target)))
        if top and level == levels - 1:
            break
        odd = (device >> (base + level)) & 1
        parents = []
        for k in range(0, len(nodes), 2):
            left = jnp.where(odd == 1, nodes[k + 1], nodes[k])
            right = jnp.where(odd == 1, nodes[k], nodes[k + 1])
            z = pick_lanes([left[:feats], right[:feats]], lane * 2)
            q = dot(left[feats:].astype(BF), parent_map[:rank, :])
            q += dot(right[feats:].astype(BF), parent_map[rank:, :])
            parents.append(jnp.concatenate([z, q], 0))
        nodes = parents
    return inters, nodes[0]


def climb_kernel(*refs, base, levels, feats):
    count = 2**levels
    rank = refs[count].shape[1]
    nodes = [ref[:, ref.shape[1] - rank :] for ref in refs[:count]]
    inters, node = climb(nodes, base, levels, refs[count][...], feats)
    for ref, value in zip(refs[count + 1 :], inters + [node]):
        ref[...] = value


def climb_stage(nodes, base, levels, parent_map, feats):
    rows, rank = nodes[0].shape[0], parent_map.shape[1]
    small = jax.ShapeDtypeStruct((rows - feats, rank), F32)
    outs = pl.pallas_call(
        functools.partial(climb_kernel, base=base, levels=levels, feats=feats),
        out_shape=(small,) * levels + (jax.ShapeDtypeStruct((rows, rank), F32),),
        in_specs=[VMEM] * (len(nodes) + 1),
        out_specs=(VMEM,) * (levels + 1),
        compiler_params=params(),
        name=f"climb_{base}",
    )(*nodes, parent_map)
    return list(outs[:-1]), outs[-1]


def finish_kernel(
    near_vmem, far_vmem, near_ref, target_ref, own_ref, chip_ref, beyond_ref, interp_ref, order_ref,
    map_ref, parent_ref, *refs, feats, base, levels, done, low,
):
    count = 2**levels
    nodes = [ref[...] for ref in refs[:count]]
    inters = [ref[...] for ref in refs[count : count + done]]
    out_ref, code_ref, far_ref, sum_ref, stack_ref, skel_ref, charge_ref, acc_ref, sems = refs[count + done :]
    copies = [
        pltpu.make_async_copy(near_vmem, code_ref, sems.at[0]),
        pltpu.make_async_copy(far_vmem, far_ref, sems.at[1]),
    ]
    for copy in copies:
        copy.start()
    leaves, slots = far_ref.shape
    rank = interp_ref.shape[0]
    rhs, total = near_ref.shape
    width = total // leaves
    device = lax.axis_index("leaf")
    parent_map = parent_ref[...]
    fresh, _ = climb(nodes, base, levels, parent_map, feats, top=True)
    inters = inters + fresh
    down = inters[-1]
    for level in range(len(inters) - 2, -1, -1):
        spread = dot_t(down.astype(BF), parent_map)
        odd = (device >> level) & 1
        down = inters[level] + jnp.where(odd == 1, spread[:, rank:], spread[:, :rank])
    leaf_out = dot_t(down.astype(BF), map_ref[...])

    targets = []
    for region, ref in enumerate((own_ref, chip_ref, beyond_ref)):
        first = ref.shape[1] - leaves * rank if region == 2 else total
        skels = slice(first, first + leaves * rank)
        source, target = stacked_rows(ref[:feats, skels])
        charge = ref[feats:, skels].astype(BF)
        for leaf in range(leaves):
            span = slice(leaf * rank, (leaf + 1) * rank)
            skel_ref[region * leaves + leaf] = source[:, span]
            charge_ref[region * leaves + leaf] = charge[:, span]
            if region == 0:
                targets.append(target[:, span])
    sum_ref[...] = near_ref[...]
    build_stacks(beyond_ref, stack_ref, feats)
    for copy in copies:
        copy.wait()
    fields = []
    for leaf in range(leaves):
        field = leaf_out[:, leaf * rank : (leaf + 1) * rank]
        where = [far_ref[leaf, slot] for slot in range(slots)]
        sources = jnp.concatenate([skel_ref[w] for w in where], 1)
        charges = jnp.concatenate([charge_ref[w] for w in where], 1)
        field += dot_t(charges, tile_of(targets[leaf], sources))
        fields.append(field.astype(BF))
    add_tiles(code_ref, target_ref, sum_ref, [(low, beyond_ref, stack_ref)], feats)
    pieces = []
    for leaf in range(leaves):
        span = slice(leaf * width, (leaf + 1) * width)
        pieces.append(sum_ref[:, span] + dot(fields[leaf], interp_ref[:, span]))

    blocks = total // BLOCK
    shift = BLOCK.bit_length() - 1
    for leaf in range(leaves):
        index = order_ref[:, leaf * width : (leaf + 1) * width] - device * total
        hot = one_hot(index & (BLOCK - 1), BLOCK)
        high = jnp.broadcast_to(index >> shift, (rhs, width))
        rows = []
        piece = pieces[leaf].astype(BF)
        high = high.astype(jnp.int16)
        for k in range(blocks):
            rows.append(jnp.where(high == k, piece, jnp.zeros((), BF)))
        part = dot_t(jnp.concatenate(rows, 0), hot)
        acc_ref[...] = part if leaf == 0 else acc_ref[...] + part
    for k in range(blocks):
        out_ref[:, k * BLOCK : (k + 1) * BLOCK] = acc_ref[k * rhs : (k + 1) * rhs, :]


def finish(codes, sums, targets, packs, interp, order, maps, nodes, inters, base, levels, feats, low):
    rhs, total = sums.shape
    leaves = codes[1].shape[0]
    rank = interp.shape[0]
    stack, width = targets.shape[0], total // leaves
    fresh = (packs[2].shape[1] - leaves * rank) // width
    operands = [*codes, sums, targets, *packs, interp, order, *maps, *nodes, *inters]
    return pl.pallas_call(
        functools.partial(
            finish_kernel, feats=feats, base=base, levels=levels, done=len(inters), low=low
        ),
        out_shape=jax.ShapeDtypeStruct((rhs, total), F32),
        in_specs=[VMEM] * len(operands),
        out_specs=VMEM,
        scratch_shapes=[
            pltpu.SMEM(codes[0].shape, jnp.int32),
            pltpu.SMEM(codes[1].shape, jnp.int32),
            pltpu.VMEM((rhs, total), F32),
            pltpu.VMEM((fresh, stack, width), BF),
            pltpu.VMEM((3 * leaves, stack, rank), BF),
            pltpu.VMEM((3 * leaves, rhs, rank), BF),
            pltpu.VMEM((total // BLOCK * rhs, BLOCK), F32),
            pltpu.SemaphoreType.DMA((2,)),
        ],
        compiler_params=params(),
        name="finish",
    )(*operands)


def body(
    points,
    charges,
    inv_scale,
    order,
    near_list,
    near_count,
    far_list,
    skel_idx,
    interp,
    group_map,
    parent_map,
):
    feats = points.shape[0]
    leaves = near_list.shape[0]
    devices = lax.axis_size("leaf")
    order = order.reshape(1, -1)
    base = first_point(points.shape[1])
    chip = [(i, i ^ 1) for i in range(devices)]
    fleets = lax.axis_size("fleet")
    beyond = []
    for first in range(0, fleets * devices, devices):
        for i in range(first + 1, first + devices - 1, 2):
            beyond += [(i, i + 1), (i + 1, i)]
        other = first ^ devices if fleets % 2 == 0 else first
        beyond += [(first, other), (first + devices - 1, other + devices - 1)]

    def send(value, mask):
        return lax.ppermute(value, "leaf", [(i, i ^ mask) for i in range(devices)])

    width = points.shape[1] // leaves
    early = leaves // 2
    placed, sources, targets = sort_points(
        inv_scale.reshape(1, -1), points, charges, order, base, leaves
    )
    pack, first, rest, node, near_codes, far_codes = skeletons(
        placed,
        skel_idx,
        group_map,
        interp,
        near_list.T,
        near_count.reshape(1, -1),
        far_list,
        feats,
        early * width,
    )
    levels = devices.bit_length() - 1
    stages = [(base, min(2, levels - base)) for base in range(0, levels, 2)]
    pack_chip = send(pack, 1)
    nodes = [node, pack_chip] + [send(node, mask) for mask in range(2, 2 ** stages[0][1])]
    first = lax.ppermute(first, ("fleet", "leaf"), beyond)
    rest = lax.ppermute(rest, ("fleet", "leaf"), beyond)
    inters = []
    for stage, (base, count) in zip(stages[:-1], stages[1:]):
        fresh, node = climb_stage(nodes, *stage, parent_map, feats)
        inters += fresh
        nodes = [node] + [send(node, mask << base) for mask in range(1, 2**count)]
    rhs = charges.shape[0]
    low = 2 * leaves
    total = near_part(
        functools.partial(near_own_kernel, feats=feats),
        near_codes,
        targets,
        (pack, sources, pack_chip),
        leaves,
        rhs,
        2 * leaves,
        "near_own",
    )
    total = near_part(
        functools.partial(near_more_kernel, feats=feats, low=low + early),
        near_codes,
        targets,
        (total, rest),
        leaves - early,
        rhs,
        leaves // 2,
        "near_beyond",
    )
    return finish(
        (near_codes, far_codes),
        total,
        targets,
        (pack, pack_chip, first),
        interp,
        order,
        (group_map, parent_map),
        nodes,
        inters,
        *stages[-1],
        feats,
        low,
    )


def solution(mesh):
    placed = (
        P(None, ("fleet", "leaf")),
        P(None, ("fleet", "leaf")),
        P("fleet"),
        P(("fleet", "leaf")),
        P(("fleet", "leaf"), None),
        P(("fleet", "leaf")),
        P(("fleet", "leaf"), None),
        P(("fleet", "leaf"), None),
        P(None, ("fleet", "leaf")),
        P(("fleet", "leaf"), None),
        P("fleet", None),
    )
    return jax.shard_map(
        body, mesh=mesh, in_specs=placed, out_specs=P(None, ("fleet", "leaf")), check_vma=False
    )
```

```python
import functools
import math

import jax
import jax.numpy as jnp
from jax import lax
from jax.experimental import pallas as pl
from jax.experimental.pallas import tpu as pltpu
from jax.sharding import PartitionSpec as P

BF = jnp.bfloat16
F32 = jnp.float32
LANES = 128
BLOCK = 256
CHUNK = 256
VMEM = pl.BlockSpec(memory_space=pltpu.VMEM)


def params():
    return pltpu.CompilerParams(vmem_limit_bytes=48 * 2**20)


def halves(z):
    hi = z.astype(BF)
    return hi, (z - hi.astype(F32)).astype(BF)


def stacked_rows(z):
    hi, mid = halves(z)
    norm = -0.5 * jnp.sum(z * z, 0, keepdims=True)
    n1 = norm.astype(BF).astype(F32)
    n2 = (norm - n1).astype(BF).astype(F32)
    n3 = norm - n1 - n2
    shape = (16, z.shape[1])
    row = lax.broadcasted_iota(jnp.int32, shape, 0)

    def extra(first):
        out = jnp.where((row >= 3 - first) & (row < 6 - first), 1.0, 0.0)
        for i, piece in enumerate((n1, n2, n3)):
            out = jnp.where(row == first + i, jnp.broadcast_to(piece, shape), out)
        return out.astype(BF)

    source = jnp.concatenate([hi, mid, hi, mid, extra(3)], 0)
    target = jnp.concatenate([hi, hi, mid, mid, extra(0)], 0)
    return source, target


def tile_of(source, target):
    e = lax.dot_general(source, target, (((0,), (0,)), ((), ())), preferred_element_type=F32)
    return jnp.exp2(e).astype(BF)


def dot_t(a, b):
    return lax.dot_general(a, b, (((1,), (1,)), ((), ())), preferred_element_type=F32)


def dot(a, b):
    return jnp.dot(a, b, preferred_element_type=F32)


def one_hot(low, size):
    rows = lax.broadcasted_iota(jnp.int32, (size, low.shape[1]), 0)
    return (rows == low).astype(F32).astype(BF)


def pick_lanes(blocks, index):
    rows = blocks[0].shape[0]
    parts = []
    for top in range(0, rows, 8):
        idx = jnp.broadcast_to(index, (8, LANES))
        high, low = idx >> 7, idx & (LANES - 1)
        out = jnp.zeros((8, LANES), F32)
        for k, block in enumerate(blocks):
            got = jnp.take_along_axis(block[top : top + 8], low, axis=1, mode="promise_in_bounds")
            out = jnp.where(high == k, got, out)
        parts.append(out)
    return jnp.concatenate(parts, 0)


def base_kernel(out_ref, *, total):
    out_ref[...] = jnp.full(out_ref.shape, lax.axis_index("leaf") * total, jnp.int32)


def first_point(total):
    return pl.pallas_call(
        functools.partial(base_kernel, total=total),
        out_shape=jax.ShapeDtypeStruct((1, LANES), jnp.int32),
        out_specs=VMEM,
        compiler_params=params(),
        cost_estimate=pl.CostEstimate(flops=10**9, bytes_accessed=10**6, transcendentals=0),
        name="first_point",
    )()


def sort_kernel(
    scale_ref, points_ref, charges_ref, order_ref, base_ref,
    pack_ref, source_ref, target_ref, zs_ref, bs_ref,
):
    feats, total = points_ref.shape
    rhs = charges_ref.shape[0]
    width = source_ref.shape[2]
    base = base_ref[:, :1]
    blocks = total // BLOCK
    shift = BLOCK.bit_length() - 1
    row = lax.broadcasted_iota(jnp.int32, (feats, feats), 0)
    lane = lax.broadcasted_iota(jnp.int32, (feats, feats), 1)
    scale = jnp.sum(jnp.where(row == lane, scale_ref[...], 0.0), 1, keepdims=True)
    scale = scale * math.sqrt(math.log2(math.e))
    for k in range(blocks):
        span = slice(k * BLOCK, (k + 1) * BLOCK)
        hi, mid = halves(points_ref[:, span] * scale)
        zs_ref[k * feats : (k + 1) * feats, :BLOCK] = hi
        zs_ref[k * feats : (k + 1) * feats, BLOCK:] = mid
        bs_ref[k * rhs : (k + 1) * rhs, :] = charges_ref[:, span].astype(BF)

    def step(j, carry):
        start = pl.multiple_of(j * CHUNK, CHUNK)
        index = order_ref[:, pl.ds(start, CHUNK)] - base
        hot = one_hot(index & (BLOCK - 1), BLOCK)
        yz = dot(zs_ref[...], jnp.concatenate([hot, hot], 0))
        yb = dot(bs_ref[...], hot)
        high = jnp.broadcast_to(index >> shift, (feats, CHUNK))
        az = jnp.zeros((feats, CHUNK), F32)
        ab = jnp.zeros((rhs, CHUNK), F32)
        for k in range(blocks):
            mask = high == k
            az = jnp.where(mask, yz[k * feats : (k + 1) * feats], az)
            ab = jnp.where(mask, yb[k * rhs : (k + 1) * rhs], ab)
        pack_ref[:feats, pl.ds(start, CHUNK)] = az
        pack_ref[feats:, pl.ds(start, CHUNK)] = ab
        source, target = stacked_rows(az)
        leaf, at = j * CHUNK // width, pl.multiple_of(j * CHUNK % width, CHUNK)
        source_ref[leaf, :, pl.ds(at, CHUNK)] = source
        target_ref[:, pl.ds(start, CHUNK)] = target
        return carry

    lax.fori_loop(0, total // CHUNK, step, 0, unroll=True)


def sort_points(inv_scale, points, charges, order, base, leaves):
    feats, total = points.shape
    rhs = charges.shape[0]
    blocks = total // BLOCK
    stack = 4 * feats + 16
    return pl.pallas_call(
        sort_kernel,
        out_shape=(
            jax.ShapeDtypeStruct((feats + rhs, total), F32),
            jax.ShapeDtypeStruct((leaves, stack, total // leaves), BF),
            jax.ShapeDtypeStruct((stack, total), BF),
        ),
        in_specs=[VMEM] * 5,
        out_specs=(VMEM,) * 3,
        scratch_shapes=[
            pltpu.VMEM((blocks * feats, 2 * BLOCK), BF),
            pltpu.VMEM((blocks * rhs, BLOCK), BF),
        ],
        compiler_params=params(),
        cost_estimate=pl.CostEstimate(
            flops=6 * total * total * 16, bytes_accessed=4 * 10**6, transcendentals=0
        ),
        name="sort_points",
    )(inv_scale, points, charges, order, base)


def skeleton_kernel(
    sorted_ref, skel_ref, map_ref, interp_ref, list_ref, count_ref, far_ref,
    pack_ref, first_ref, rest_ref, node_ref, near_code_ref, far_code_ref, *, feats
):
    leaves, rank = skel_ref.shape
    rows, total = sorted_ref.shape
    width = total // leaves
    group_q = jnp.zeros((rows - feats, rank), F32)
    for leaf in range(leaves):
        span = slice(leaf * width, (leaf + 1) * width)
        out = slice(total + leaf * rank, total + (leaf + 1) * rank)
        columns = [
            sorted_ref[:feats, leaf * width + k : leaf * width + k + LANES]
            for k in range(0, width, LANES)
        ]
        pack_ref[:feats, out] = pick_lanes(columns, skel_ref[leaf : leaf + 1, :])
        charge = dot_t(sorted_ref[feats:, span].astype(BF), interp_ref[:, span]).astype(BF)
        pack_ref[feats:, out] = charge.astype(F32)
        group_q += dot(charge, map_ref[leaf * rank : (leaf + 1) * rank, :])
        pack_ref[:, span] = sorted_ref[:, span]
    columns = [pack_ref[:feats, total + k : total + k + LANES] for k in range(0, leaves * rank, LANES)]
    node_ref[:feats, :] = pick_lanes(
        columns, lax.broadcasted_iota(jnp.int32, (1, rank), 1) * leaves
    )
    node_ref[feats:, :] = group_q
    pack_ref[:, total + leaves * rank :] = node_ref[...]
    early = total - rest_ref.shape[1]
    first_ref[:, :early] = sorted_ref[:, :early]
    first_ref[:, early:] = pack_ref[:, total : total + leaves * rank]
    rest_ref[...] = sorted_ref[:, early:]
    used = lax.broadcasted_iota(jnp.int32, list_ref.shape, 0) < count_ref[...]
    near_code_ref[...] = jnp.where(used, code_of(list_ref[...], leaves), -1)
    far_code_ref[...] = code_of(far_ref[...], leaves)


def skeletons(points, skel_idx, group_map, interp, near_list, near_count, far_list, feats, early):
    rows, total = points.shape
    leaves, rank = skel_idx.shape
    skels = leaves * rank
    return pl.pallas_call(
        functools.partial(skeleton_kernel, feats=feats),
        out_shape=(
            jax.ShapeDtypeStruct((rows, total + skels + rank), F32),
            jax.ShapeDtypeStruct((rows, early + skels), F32),
            jax.ShapeDtypeStruct((rows, total - early), F32),
            jax.ShapeDtypeStruct((rows, rank), F32),
            jax.ShapeDtypeStruct(near_list.shape, jnp.int32),
            jax.ShapeDtypeStruct(far_list.shape, jnp.int32),
        ),
        in_specs=[VMEM] * 7,
        out_specs=(VMEM,) * 6,
        compiler_params=params(),
        name="skeletons",
    )(points, skel_idx, group_map, interp, near_list, near_count, far_list)


def code_of(leaf_id, leaves):
    device = lax.axis_index("leaf")
    rel = leaf_id - (device - 1) * leaves
    side = (rel >= leaves).astype(jnp.int32) + (rel >= 2 * leaves).astype(jnp.int32)
    chip = 2 * (1 - (device & 1))
    region = jnp.where(side == 1, 0, jnp.where(side == chip, 1, 2))
    return rel + (region - side) * leaves


def build_stacks(src_ref, stack_ref, feats):
    width = stack_ref.shape[2]
    for place in range(stack_ref.shape[0]):
        stack_ref[place] = stacked_rows(src_ref[:feats, place * width : (place + 1) * width])[0]


def add_tiles(code_ref, target_ref, out_ref, parts, feats):
    slots, leaves = code_ref.shape
    width = out_ref.shape[1] // leaves

    def add(leaf, place, src_ref, stack_ref):
        start = pl.multiple_of(leaf * width, width)
        at = pl.multiple_of(place * width, width)
        charge = src_ref[feats:, pl.ds(at, width)].astype(BF)
        tile = tile_of(stack_ref[place], target_ref[:, pl.ds(start, width)])
        out_ref[:, pl.ds(start, width)] += dot(charge, tile)

    def per_leaf(leaf, carry):
        def per_slot(slot, carry):
            code = code_ref[slot, leaf]
            for low, src_ref, stack_ref in parts:

                @pl.when((code >= low) & (code < low + stack_ref.shape[0]))
                def _():
                    add(leaf, code - low, src_ref, stack_ref)

            return carry

        return lax.fori_loop(0, slots, per_slot, carry)

    lax.fori_loop(0, leaves, per_leaf, 0)


def near_own_kernel(
    code_vmem, target_ref, own_ref, own_stack, chip_ref, out_ref, code_ref, chip_stack, sem, *, feats
):
    copy = pltpu.make_async_copy(code_vmem, code_ref, sem)
    copy.start()
    leaves = own_stack.shape[0]
    out_ref[...] = jnp.zeros_like(out_ref)
    build_stacks(chip_ref, chip_stack, feats)
    copy.wait()
    parts = [(0, own_ref, own_stack), (leaves, chip_ref, chip_stack)]
    add_tiles(code_ref, target_ref, out_ref, parts, feats)


def near_more_kernel(
    code_vmem, target_ref, acc_ref, src_ref, out_ref, code_ref, stack_ref, sem, *, feats, low
):
    copy = pltpu.make_async_copy(code_vmem, code_ref, sem)
    copy.start()
    out_ref[...] = acc_ref[...]
    build_stacks(src_ref, stack_ref, feats)
    copy.wait()
    add_tiles(code_ref, target_ref, out_ref, [(low, src_ref, stack_ref)], feats)


def near_part(kernel, codes, targets, operands, count, rhs, tiles, name):
    leaves = codes.shape[1]
    total = targets.shape[1]
    width = total // leaves
    return pl.pallas_call(
        kernel,
        out_shape=jax.ShapeDtypeStruct((rhs, total), F32),
        in_specs=[VMEM] * (2 + len(operands)),
        out_specs=VMEM,
        scratch_shapes=[
            pltpu.SMEM(codes.shape, jnp.int32),
            pltpu.VMEM((count, targets.shape[0], width), BF),
            pltpu.SemaphoreType.DMA,
        ],
        compiler_params=params(),
        cost_estimate=pl.CostEstimate(
            flops=tiles * width * width * 1024,
            bytes_accessed=tiles * 48 * width * 4,
            transcendentals=tiles * width * width,
        ),
        name=name,
    )(codes, targets, *operands)


def climb(nodes, base, levels, parent_map, feats, top=False):
    device = lax.axis_index("leaf")
    rank = nodes[0].shape[1]
    lane = lax.broadcasted_iota(jnp.int32, (1, rank), 1)
    inters = []
    for level in range(levels):
        own, other = nodes[0], nodes[1]
        source, _ = stacked_rows(other[:feats])
        _, target = stacked_rows(own[:feats])
        inters.append(dot(other[feats:].astype(BF), tile_of(source, target)))
        if top and level == levels - 1:
            break
        odd = (device >> (base + level)) & 1
        parents = []
        for k in range(0, len(nodes), 2):
            left = jnp.where(odd == 1, nodes[k + 1], nodes[k])
            right = jnp.where(odd == 1, nodes[k], nodes[k + 1])
            z = pick_lanes([left[:feats], right[:feats]], lane * 2)
            q = dot(left[feats:].astype(BF), parent_map[:rank, :])
            q += dot(right[feats:].astype(BF), parent_map[rank:, :])
            parents.append(jnp.concatenate([z, q], 0))
        nodes = parents
    return inters, nodes[0]


def climb_kernel(*refs, base, levels, feats):
    count = 2**levels
    rank = refs[count].shape[1]
    nodes = [ref[:, ref.shape[1] - rank :] for ref in refs[:count]]
    _, refs[count + 1][...] = climb(nodes, base, levels, refs[count][...], feats)


def climb_stage(nodes, base, levels, parent_map, feats):
    rows, rank = nodes[0].shape[0], parent_map.shape[1]
    return pl.pallas_call(
        functools.partial(climb_kernel, base=base, levels=levels, feats=feats),
        out_shape=jax.ShapeDtypeStruct((rows, rank), F32),
        in_specs=[VMEM] * (len(nodes) + 1),
        out_specs=VMEM,
        compiler_params=params(),
        name=f"climb_{base}",
    )(*nodes, parent_map)


def finish_kernel(
    near_vmem, far_vmem, near_ref, target_ref, own_ref, chip_ref, beyond_ref, interp_ref, order_ref,
    map_ref, parent_ref, *refs, feats, stages, low,
):
    refs = list(refs)
    rank = parent_ref.shape[1]
    groups = []
    for _, count in stages:
        taken = [refs.pop(0) for _ in range(2**count)]
        groups.append([ref[:, ref.shape[1] - rank :] for ref in taken])
    out_ref, code_ref, far_ref, sum_ref, stack_ref, skel_ref, charge_ref, acc_ref, sems = refs
    copies = [
        pltpu.make_async_copy(near_vmem, code_ref, sems.at[0]),
        pltpu.make_async_copy(far_vmem, far_ref, sems.at[1]),
    ]
    for copy in copies:
        copy.start()
    leaves, slots = far_ref.shape
    rank = interp_ref.shape[0]
    rhs, total = near_ref.shape
    width = total // leaves
    device = lax.axis_index("leaf")
    parent_map = parent_ref[...]
    inters = []
    for nodes, (base, count) in zip(groups, stages):
        inters += climb(nodes, base, count, parent_map, feats, top=True)[0]
    down = inters[-1]
    for level in range(len(inters) - 2, -1, -1):
        spread = dot_t(down.astype(BF), parent_map)
        odd = (device >> level) & 1
        down = inters[level] + jnp.where(odd == 1, spread[:, rank:], spread[:, :rank])
    leaf_out = dot_t(down.astype(BF), map_ref[...])

    targets = []
    for region, ref in enumerate((own_ref, chip_ref, beyond_ref)):
        first = ref.shape[1] - leaves * rank if region == 2 else total
        skels = slice(first, first + leaves * rank)
        source, target = stacked_rows(ref[:feats, skels])
        charge = ref[feats:, skels].astype(BF)
        for leaf in range(leaves):
            span = slice(leaf * rank, (leaf + 1) * rank)
            skel_ref[region * leaves + leaf] = source[:, span]
            charge_ref[region * leaves + leaf] = charge[:, span]
            if region == 0:
                targets.append(target[:, span])
    sum_ref[...] = near_ref[...]
    build_stacks(beyond_ref, stack_ref, feats)
    for copy in copies:
        copy.wait()
    fields = []
    for leaf in range(leaves):
        field = leaf_out[:, leaf * rank : (leaf + 1) * rank]
        where = [far_ref[leaf, slot] for slot in range(slots)]
        sources = jnp.concatenate([skel_ref[w] for w in where], 1)
        charges = jnp.concatenate([charge_ref[w] for w in where], 1)
        field += dot_t(charges, tile_of(targets[leaf], sources))
        fields.append(field.astype(BF))
    add_tiles(code_ref, target_ref, sum_ref, [(low, beyond_ref, stack_ref)], feats)
    pieces = []
    for leaf in range(leaves):
        span = slice(leaf * width, (leaf + 1) * width)
        pieces.append(sum_ref[:, span] + dot(fields[leaf], interp_ref[:, span]))

    blocks = total // BLOCK
    shift = BLOCK.bit_length() - 1
    for leaf in range(leaves):
        index = order_ref[:, leaf * width : (leaf + 1) * width] - device * total
        hot = one_hot(index & (BLOCK - 1), BLOCK)
        high = jnp.broadcast_to(index >> shift, (rhs, width))
        rows = []
        piece = pieces[leaf].astype(BF)
        high = high.astype(jnp.int16)
        for k in range(blocks):
            rows.append(jnp.where(high == k, piece, jnp.zeros((), BF)))
        part = dot_t(jnp.concatenate(rows, 0), hot)
        acc_ref[...] = part if leaf == 0 else acc_ref[...] + part
    for k in range(blocks):
        out_ref[:, k * BLOCK : (k + 1) * BLOCK] = acc_ref[k * rhs : (k + 1) * rhs, :]


def finish(codes, sums, targets, packs, interp, order, maps, nodes, stages, feats, low):
    rhs, total = sums.shape
    leaves = codes[1].shape[0]
    rank = interp.shape[0]
    stack, width = targets.shape[0], total // leaves
    fresh = (packs[2].shape[1] - leaves * rank) // width
    operands = [*codes, sums, targets, *packs, interp, order, *maps, *nodes]
    return pl.pallas_call(
        functools.partial(
            finish_kernel, feats=feats, stages=stages, low=low
        ),
        out_shape=jax.ShapeDtypeStruct((rhs, total), F32),
        in_specs=[VMEM] * len(operands),
        out_specs=VMEM,
        scratch_shapes=[
            pltpu.SMEM(codes[0].shape, jnp.int32),
            pltpu.SMEM(codes[1].shape, jnp.int32),
            pltpu.VMEM((rhs, total), F32),
            pltpu.VMEM((fresh, stack, width), BF),
            pltpu.VMEM((3 * leaves, stack, rank), BF),
            pltpu.VMEM((3 * leaves, rhs, rank), BF),
            pltpu.VMEM((total // BLOCK * rhs, BLOCK), F32),
            pltpu.SemaphoreType.DMA((2,)),
        ],
        compiler_params=params(),
        name="finish",
    )(*operands)


def body(
    points,
    charges,
    inv_scale,
    order,
    near_list,
    near_count,
    far_list,
    skel_idx,
    interp,
    group_map,
    parent_map,
):
    feats = points.shape[0]
    leaves = near_list.shape[0]
    devices = lax.axis_size("leaf")
    order = order.reshape(1, -1)
    base = first_point(points.shape[1])
    chip = [(i, i ^ 1) for i in range(devices)]
    fleets = lax.axis_size("fleet")
    beyond = []
    for first in range(0, fleets * devices, devices):
        for i in range(first + 1, first + devices - 1, 2):
            beyond += [(i, i + 1), (i + 1, i)]
        other = first ^ devices if fleets % 2 == 0 else first
        beyond += [(first, other), (first + devices - 1, other + devices - 1)]

    def send(value, mask):
        return lax.ppermute(value, "leaf", [(i, i ^ mask) for i in range(devices)])

    width = points.shape[1] // leaves
    early = leaves // 2
    placed, sources, targets = sort_points(
        inv_scale.reshape(1, -1), points, charges, order, base, leaves
    )
    pack, first, rest, node, near_codes, far_codes = skeletons(
        placed,
        skel_idx,
        group_map,
        interp,
        near_list.T,
        near_count.reshape(1, -1),
        far_list,
        feats,
        early * width,
    )
    levels = devices.bit_length() - 1
    stages = [(base, min(2, levels - base)) for base in range(0, levels, 2)]
    pack_chip = send(pack, 1)
    nodes = [node, pack_chip] + [send(node, mask) for mask in range(2, 2 ** stages[0][1])]
    first = lax.ppermute(first, ("fleet", "leaf"), beyond)
    rest = lax.ppermute(rest, ("fleet", "leaf"), beyond)
    every = list(nodes)
    for stage, (base, count) in zip(stages[:-1], stages[1:]):
        node = climb_stage(nodes, *stage, parent_map, feats)
        nodes = [node] + [send(node, mask << base) for mask in range(1, 2**count)]
        every += nodes
    rhs = charges.shape[0]
    low = 2 * leaves
    total = near_part(
        functools.partial(near_own_kernel, feats=feats),
        near_codes,
        targets,
        (pack, sources, pack_chip),
        leaves,
        rhs,
        2 * leaves,
        "near_own",
    )
    total = near_part(
        functools.partial(near_more_kernel, feats=feats, low=low + early),
        near_codes,
        targets,
        (total, rest),
        leaves - early,
        rhs,
        leaves // 2,
        "near_beyond",
    )
    return finish(
        (near_codes, far_codes),
        total,
        targets,
        (pack, pack_chip, first),
        interp,
        order,
        (group_map, parent_map),
        every,
        stages,
        feats,
        low,
    )


def solution(mesh):
    placed = (
        P(None, ("fleet", "leaf")),
        P(None, ("fleet", "leaf")),
        P("fleet"),
        P(("fleet", "leaf")),
        P(("fleet", "leaf"), None),
        P(("fleet", "leaf")),
        P(("fleet", "leaf"), None),
        P(("fleet", "leaf"), None),
        P(None, ("fleet", "leaf")),
        P(("fleet", "leaf"), None),
        P("fleet", None),
    )
    return jax.shard_map(
        body, mesh=mesh, in_specs=placed, out_specs=P(None, ("fleet", "leaf")), check_vma=False
    )
```
